32 devices in a mesh: head: 4 (over z), seq: 8 (over y, x, core).
Axes of the slice: x: 2, y: 2, z: 4, core: 2. Of those that a mesh axis runs over, the one named last changes fastest.
Arguments:
- tokens: bfloat16 [4096, 1536], P('seq'), may hold values from -8 to 8
- cotangent: bfloat16 [4096, 1536], P('seq'), may hold values from -6 to 6
- starts: int32 [4096], P('seq'), may hold values from 0 to 1, as said below
- gain_attn: bfloat16 [1536], P('seq'), may hold values from 0.5 to 1.5
- w_query: bfloat16 [1536, 1536], P('seq', 'head'), may hold values from -0.15625 to 0.15625
- w_key: bfloat16 [1536, 1536], P('seq', 'head'), may hold values from -0.15625 to 0.15625
- w_value: bfloat16 [1536, 1536], P('seq', 'head'), may hold values from -0.15625 to 0.15625
- w_dir: bfloat16 [1536, 1536], P('seq', 'head'), may hold values from -0.15625 to 0.15625
- w_beta: bfloat16 [1536, 12], P('seq', 'head'), may hold values from -3 to 3
- w_out: bfloat16 [1536, 1536], P('head', 'seq'), may hold values from -3.5 to 3.5
- gain_mlp: bfloat16 [1536], P('seq'), may hold values from 0.5 to 1.5
- w_gate: bfloat16 [1536, 4096], P('seq', 'head'), may hold values from -0.15625 to 0.15625
- w_up: bfloat16 [1536, 4096], P('seq', 'head'), may hold values from -0.15625 to 0.15625
- w_down: bfloat16 [4096, 1536], P('head', 'seq'), may hold values from -0.09375 to 0.09375
Outputs:
- result: bfloat16 [4096, 1536], P('seq')
- d_tokens: float32 [4096, 1536], P('seq')
- grad_gain_attn: float32 [1536], P('seq')
- grad_w_query: float32 [1536, 1536], P('seq', 'head')
- grad_w_key: float32 [1536, 1536], P('seq', 'head')
- grad_w_value: float32 [1536, 1536], P('seq', 'head')
- grad_w_dir: float32 [1536, 1536], P('seq', 'head')
- grad_w_beta: float32 [1536, 12], P('seq', 'head')
- grad_w_out: float32 [1536, 1536], P('head', 'seq')
- grad_gain_mlp: float32 [1536], P('seq')
- grad_w_gate: float32 [1536, 4096], P('seq', 'head')
- grad_w_up: float32 [1536, 4096], P('seq', 'head')
- grad_w_down: float32 [4096, 1536], P('head', 'seq')
The draws below stay inside these ranges and needn't reach their ends.
Inputs may be any that keep to these rules, and one draw needn't show every extreme that they name: `starts`: 1 marks the first token of a document, 0 any other token; the first token of every packed row of 4096 tokens is marked.
All inputs are finite; a program needn't handle non-finite values.
Results may differ from the reference program's by a relative error of at most 0.028.
The reference program's roundings to bfloat16 on the way count: a program that leaves them out, or rounds other values in their place, can miss the bound.
Values may be sent and summed in bfloat16 or wider, within the bound.
No kernel may reach another device: no remote copies, remote signals or barrier semaphores. Data moves between devices by JAX's collectives and lax.ppermute only.
A program may use at most 192 MiB of HBM per device.

```python
import jax
import jax.numpy as jnp
from jax import lax

D = 1536
HEADS = 12
HD = 128
FF = 4096
INNER = 1536
TOK_DEV = 512
SPAN = 8
ROW_LEN = 4096
ROW = 4096


def common_feature(key):
    return jnp.clip(jax.random.normal(key, (D,), jnp.float32), -4.0, 4.0)


def draw_tokens(key, part):
    shared = common_feature(key)
    key = jax.random.fold_in(key, 5)
    noise = jnp.clip(jax.random.normal(key, (ROW, D), jnp.float32), -6.0, 6.0)
    return (noise + 0.5 * shared[None, :]).astype(jnp.bfloat16)


def draw_w_beta(key, part):
    shared = common_feature(key)
    key = jax.random.fold_in(key, 7)
    reach_key, rest_key = jax.random.split(key)
    reach = jax.random.uniform(reach_key, (HEADS,), jnp.float32, -27.0, 27.0)
    rest = jnp.clip(jax.random.normal(rest_key, (D, HEADS), jnp.float32), -4.0, 4.0) * D ** (-0.5)
    return (reach[None, :] * shared[:, None] / D + rest).astype(jnp.bfloat16)


def draw_starts(key, part):
    key = jax.random.fold_in(key, 3)
    first_key, last_key, coin_key, pick_key, edge_key = jax.random.split(key, 5)
    row_total = ROW // ROW_LEN
    drawn_rate = max(ROW_LEN // 8, 4)
    first_start = jax.random.randint(first_key, (), 1, TOK_DEV)
    last_start = jax.random.randint(last_key, (), ROW_LEN - TOK_DEV, ROW_LEN)
    long_row = jax.random.randint(pick_key, (), 0, row_total)
    position = jnp.arange(ROW, dtype=jnp.int32)
    inside = position % ROW_LEN
    row_number = position // ROW_LEN
    coins = jax.random.randint(coin_key, (ROW,), 0, drawn_rate) == 0
    edge_coins = jax.random.randint(edge_key, (ROW,), 0, 3) == 0
    edges = (inside < first_start) | (inside > last_start)
    long_marks = (inside == first_start) | (inside == last_start) | edge_coins & edges
    chosen = jnp.where(row_number == long_row, long_marks, coins)
    marked = (inside == 0) | chosen
    return marked.astype(jnp.int32)


def block_levels(key, shape, pieces, least, largest):
    level = 1.0
    for axis_at, parts in pieces:
        heights = jax.random.uniform(jax.random.fold_in(jax.random.fold_in(key, 6), axis_at), (parts,), jnp.float32, least / len(pieces), largest / len(pieces))
        level = level * jnp.repeat(jnp.exp(heights), shape[axis_at] // parts).reshape((-1,) + (1,) * (len(shape) - 1 - axis_at))
    return level


def normal_values(stream_key, dims, scale, bound, cuts=(), kind=jnp.bfloat16):
    drawn = jax.random.normal(stream_key, dims, jnp.float32) * scale
    if len(cuts) > 0:
        drawn = block_levels(stream_key, dims, cuts, -0.22, 0.18) * drawn
    return jnp.clip(drawn, min=-bound, max=bound).astype(kind)


def setup_inputs(seed: int = 0) -> dict:
    keys = jax.random.split(jax.random.key(seed), 15)
    tokens = draw_tokens(jax.random.fold_in(keys[14], 71), 0)
    cotangent = normal_values(keys[1], (ROW, D), 1.0, 6.0, ((0, 8),))
    starts = draw_starts(jax.random.fold_in(keys[14], 71), 0)
    gain_attn = jnp.clip(1.0 + 0.1 * jax.random.normal(keys[3], (D,), jnp.float32), 0.5, 1.5).astype(jnp.bfloat16)
    w_query = normal_values(keys[4], (D, INNER), D ** -0.5, 0.15625, ((0, 8), (1, 4)))
    w_key = normal_values(keys[5], (D, INNER), D ** -0.5, 0.15625, ((0, 8), (1, 4)))
    w_value = normal_values(keys[6], (D, INNER), D ** -0.5, 0.15625, ((0, 8), (1, 4)))
    w_dir = normal_values(keys[7], (D, INNER), D ** -0.5, 0.15625, ((0, 8), (1, 4)))
    w_beta = draw_w_beta(jax.random.fold_in(keys[14], 71), 0)
    w_out = normal_values(keys[9], (INNER, D), (max(1, 8 * INNER // ROW_LEN)) ** -0.5, 3.5, ((0, 4), (1, 8)))
    gain_mlp = jnp.clip(1.0 + 0.1 * jax.random.normal(keys[10], (D,), jnp.float32), 0.5, 1.5).astype(jnp.bfloat16)
    w_gate = normal_values(keys[11], (D, FF), D ** -0.5, 0.15625, ((0, 8), (1, 4)))
    w_up = normal_values(keys[12], (D, FF), D ** -0.5, 0.15625, ((0, 8), (1, 4)))
    w_down = normal_values(keys[13], (FF, D), FF ** -0.5, 0.09375, ((0, 4), (1, 8)))
    return {"tokens": tokens, "cotangent": cotangent, "starts": starts, "gain_attn": gain_attn, "w_query": w_query, "w_key": w_key, "w_value": w_value, "w_dir": w_dir, "w_beta": w_beta, "w_out": w_out, "gain_mlp": gain_mlp, "w_gate": w_gate, "w_up": w_up, "w_down": w_down}


EPSILON = 1e-06
NEGATIVE = -1e+30

@jax.custom_vjp
def low(v):
    return lax.optimization_barrier(v.astype(jnp.bfloat16)).astype(jnp.float32)

@jax.custom_vjp
def low_back(v):
    return v

def low_keep(v):
    return (low(v), None)

def low_pass(kept, grad):
    return (grad,)

def back_keep(v):
    return (v, None)

def back_low(kept, grad):
    return (low(grad),)
low.defvjp(low_keep, low_pass)
low_back.defvjp(back_keep, back_low)

def exact_dot(left, right):
    return jnp.matmul(left, right, precision=lax.Precision.HIGHEST)

def norm_rows(value, gain):
    scale = lax.rsqrt(lax.optimization_barrier(jnp.mean(value * value, axis=-1, keepdims=True)) + EPSILON)
    return value * scale * gain

def householder_block(query, key_rows, dir_raw, beta_raw):
    unit_dir = dir_raw * lax.rsqrt(lax.optimization_barrier(jnp.sum(dir_raw * dir_raw, axis=-1, keepdims=True)) + EPSILON)
    beta_gate = 2.0 * jax.nn.sigmoid(beta_raw)
    length = query.shape[0]
    row_ids = lax.broadcasted_iota(jnp.int32, (length, length), 0)
    col_ids = lax.broadcasted_iota(jnp.int32, (length, length), 1)
    dir_gram = exact_dot(unit_dir, unit_dir.T)
    lower_mat = jnp.where(row_ids > col_ids, dir_gram, 0.0) + jnp.diag(1.0 / beta_gate)
    inner_solve = lax.linalg.triangular_solve(lower_mat, unit_dir, left_side=True, lower=True)
    dir_key = jnp.where(row_ids > col_ids, exact_dot(unit_dir, key_rows.T), 0.0)
    carried = lax.linalg.triangular_solve(lower_mat, dir_key, left_side=True, lower=True)
    query_dir = jnp.where(row_ids >= col_ids, exact_dot(query, unit_dir.T), 0.0)
    q_moved = query - exact_dot(query_dir, inner_solve)
    k_moved = key_rows - exact_dot(carried.T, unit_dir)
    inside = exact_dot(query, key_rows.T) - exact_dot(query_dir, carried)
    identity_mat = jnp.eye(query.shape[1], dtype=query.dtype)
    through = identity_mat - exact_dot(unit_dir.T, inner_solve)
    return (q_moved, k_moved, inside, through)

def row_attention(query, key_in, values, dir_in, beta_in, doc_row):
    blocks = SPAN
    width = TOK_DEV
    head_dim = query.shape[1]
    q_blocks = query.reshape(blocks, width, head_dim)
    k_blocks = key_in.reshape(blocks, width, head_dim)
    v_blocks = values.reshape(blocks, width, head_dim)
    d_blocks = dir_in.reshape(blocks, width, head_dim)
    q_moved, k_moved, inside, through = jax.vmap(householder_block)(q_blocks, k_blocks, d_blocks, beta_in.reshape(blocks, width))
    docs = doc_row.reshape(blocks, width)
    row_ids = lax.broadcasted_iota(jnp.int32, (width, width), 0)
    col_ids = lax.broadcasted_iota(jnp.int32, (width, width), 1)
    own_ok = (docs[:, :, None] == docs[:, None, :]) & (row_ids >= col_ids)[None]
    score_scale = head_dim ** (-0.5)
    own_scores = jnp.where(own_ok, inside * score_scale, NEGATIVE)

    def hop(carry, offset):
        send_keys, send_vals = carry
        recv_keys = jnp.concatenate([jnp.zeros_like(send_keys[:1]), send_keys[:-1]], axis=0)
        recv_vals = jnp.concatenate([jnp.zeros_like(send_vals[:1]), send_vals[:-1]], axis=0)
        onward = jnp.einsum('bnd,bed->bne', recv_keys, through, precision=lax.Precision.HIGHEST)
        return ((onward, recv_vals), (recv_keys, recv_vals))
    offsets = jnp.arange(1, blocks, dtype=jnp.int32)
    unused, stacks = lax.scan(hop, (k_moved, v_blocks), offsets)
    key_stack, val_stack = stacks
    anchor = jnp.arange(blocks, dtype=jnp.int32)[None, :] - offsets[:, None]
    key_docs = docs[jnp.maximum(anchor, 0)]
    cross_ok = (anchor >= 0)[:, :, None, None] & (docs[None, :, :, None] == key_docs[:, :, None, :])
    cross_scores = jnp.einsum('cid,hcjd->hcij', q_moved, key_stack, precision=lax.Precision.HIGHEST) * score_scale
    cross_scores = jnp.where(cross_ok, cross_scores, NEGATIVE)
    scores = jnp.concatenate([own_scores[None], cross_scores], axis=0)
    all_vals = jnp.concatenate([v_blocks[None], val_stack], axis=0)
    row_peak = lax.optimization_barrier(jnp.max(lax.optimization_barrier(jnp.max(scores, axis=3, keepdims=True)), axis=0, keepdims=True))
    exp_scores = jnp.exp(scores - row_peak)
    probs = low(exp_scores / lax.optimization_barrier(jnp.sum(lax.optimization_barrier(jnp.sum(exp_scores, axis=3, keepdims=True)), axis=0, keepdims=True)))
    mixed = jnp.einsum('hcij,hcjd->cid', probs, all_vals, precision=lax.Precision.HIGHEST)
    return mixed.reshape(blocks * width, head_dim)

def split_heads(array_in):
    return array_in.reshape(ROW, HEADS, HD).transpose(1, 0, 2)

def layer(stream, gain_attn, w_query, w_key, w_value, w_dir, w_beta, w_out, gain_mlp, w_gate, w_up, w_down, doc_row):
    normed = low(norm_rows(stream, gain_attn))
    query = low_back(exact_dot(normed, w_query))
    key_in = low_back(exact_dot(normed, w_key))
    values = low_back(low(exact_dot(normed, w_value)))
    dir_in = low_back(exact_dot(normed, w_dir))
    beta_in = low_back(exact_dot(normed, w_beta))
    row_total = ROW // ROW_LEN
    doc_rows = doc_row.reshape(row_total, ROW_LEN)

    def one_row(bundle):
        return row_attention(bundle[0], bundle[1], bundle[2], bundle[3], bundle[4], bundle[5])

    def one_head(bundle):
        shaped = tuple((part.reshape((row_total, ROW_LEN) + part.shape[1:]) for part in bundle))
        mixed_rows = lax.map(jax.checkpoint(one_row), shaped + (doc_rows,))
        return mixed_rows.reshape(ROW, HD)
    mixed = lax.map(one_head, (split_heads(query), split_heads(key_in), split_heads(values), split_heads(dir_in), beta_in.T))
    attention = low_back(low(mixed.transpose(1, 0, 2).reshape(ROW, INNER)))
    branch = low_back(exact_dot(attention, w_out))
    middle = stream + branch
    normed_two = low(norm_rows(middle, gain_mlp))
    gate_in = low_back(exact_dot(normed_two, w_gate))
    up_in = low_back(exact_dot(normed_two, w_up))
    hidden = low(jax.nn.silu(gate_in) * up_in)
    return middle + exact_dot(hidden, w_down)

def reference(tokens, cotangent, starts, gain_attn, w_query, w_key, w_value, w_dir, w_beta, w_out, gain_mlp, w_gate, w_up, w_down):
    doc_row = jnp.cumsum(starts.astype(jnp.int32)).astype(jnp.int32)

    def forward(stream, gain_a, w_q, w_k, w_v, w_d, w_b, w_o, gain_m, w_g, w_u, w_dn):
        return layer(stream, gain_a, w_q, w_k, w_v, w_d, w_b, w_o, gain_m, w_g, w_u, w_dn, doc_row)
    output, pull = jax.vjp(forward, tokens.astype(jnp.float32), gain_attn.astype(jnp.float32), w_query.astype(jnp.float32), w_key.astype(jnp.float32), w_value.astype(jnp.float32), w_dir.astype(jnp.float32), w_beta.astype(jnp.float32), w_out.astype(jnp.float32), gain_mlp.astype(jnp.float32), w_gate.astype(jnp.float32), w_up.astype(jnp.float32), w_down.astype(jnp.float32))
    grads = pull(cotangent.astype(jnp.float32))
    return (output.astype(jnp.bfloat16), grads[0], grads[1], grads[2], grads[3], grads[4], grads[5], grads[6], grads[7], grads[8], grads[9], grads[10], grads[11])
```

```python
import functools

import jax
import jax.numpy as jnp
from jax import lax
from jax.experimental import pallas as pl
from jax.experimental.pallas import tpu as pltpu
from jax.sharding import PartitionSpec as P

SPAN = 8
EPSILON = 1e-06
NEGATIVE = -1e30
LOW = jnp.bfloat16
WIDE = jnp.float32
VMEM_BYTES = 48 * 2**20


def mm(left, right, ta=False, tb=False):
    dims = (((0 if ta else 1,), (1 if tb else 0,)), ((), ()))
    return lax.dot_general(
        left.astype(LOW), right.astype(LOW), dims, preferred_element_type=WIDE
    )


def halves(value):
    high = value.astype(LOW)
    return high, (value - high.astype(WIDE)).astype(LOW)


def mm3(left, right, ta=False, tb=False):
    left_hi, left_lo = left if isinstance(left, tuple) else halves(left)
    right_hi, right_lo = right if isinstance(right, tuple) else halves(right)
    return mm(left_hi, right_hi, ta, tb) + (mm(left_hi, right_lo, ta, tb) + mm(left_lo, right_hi, ta, tb))


def iota(shape, axis):
    return lax.broadcasted_iota(jnp.int32, shape, axis)


def lower_inverse(strict, beta):
    length = strict.shape[0]
    size = 128
    row, col = iota((size, size), 0), iota((size, size), 1)
    subs, blocks = [], []
    for at in range(0, length, size):
        sub = strict[at : at + size, at : at + size]
        scale = beta[at : at + size]
        diag = jnp.where(row == col, scale, 0.0)
        across = jnp.sum(diag, axis=0, keepdims=True)
        pair = ((row >> 1) == (col >> 1)) & (row > col)
        subs.append(sub)
        blocks.append(diag - jnp.where(pair, sub * scale * across, 0.0))
    bit = 1
    while (1 << bit) < size:
        mask = ((row >> (bit + 1)) == (col >> (bit + 1))) & ((row >> bit) != (col >> bit)) & (row > col)
        right = [mm3(jnp.where(mask, sub, 0.0), block) for sub, block in zip(subs, blocks)]
        blocks = [block - mm3(block, part) for block, part in zip(blocks, right)]
        bit += 1
    while len(blocks) > 1:
        size = blocks[0].shape[0]
        joined = []
        for pair_at in range(len(blocks) // 2):
            first, second = blocks[2 * pair_at], blocks[2 * pair_at + 1]
            at = 2 * pair_at * size
            corner = -mm3(second, mm3(strict[at + size : at + 2 * size, at : at + size], first))
            joined.append(
                jnp.concatenate(
                    [
                        jnp.concatenate([first, jnp.zeros_like(first)], axis=1),
                        jnp.concatenate([corner, second], axis=1),
                    ],
                    axis=0,
                )
            )
        blocks = joined
    return blocks[0]


def pick_beta(beta_ref, head):
    tile = beta_ref[...]
    raw = jnp.sum(jnp.where(iota(tile.shape, 1) == head, tile, 0.0), axis=1, keepdims=True)
    return 2.0 * jax.nn.sigmoid(raw)


def block_forward(
    q_ref, k_ref, v_ref, d_ref, beta_ref, doc_col_ref, doc_row_ref,
    pack_ref, qm_ref, score_ref, inv_ref, carried_ref, qdir_ref, solve_ref, peak_ref, total_ref, acc_ref,
):
    query, key, dirs = q_ref[...], k_ref[...], d_ref[...]
    length, dim = query.shape
    beta = pick_beta(beta_ref, pl.program_id(0))
    unit = dirs * lax.rsqrt(jnp.sum(dirs * dirs, axis=-1, keepdims=True) + EPSILON)
    row, col = iota((length, length), 0), iota((length, length), 1)
    unit_two = halves(unit)
    strict = jnp.where(row > col, mm3(unit_two, unit_two, tb=True), 0.0)
    inverse = lower_inverse(strict, beta)
    inverse_two = halves(inverse)
    solve = mm3(inverse_two, unit_two)
    solve_two = halves(solve)
    dir_key = jnp.where(row > col, mm3(unit_two, key, tb=True), 0.0)
    carried = mm3(inverse_two, dir_key)
    carried_two = halves(carried)
    qdir = jnp.where(row >= col, mm3(query, unit_two, tb=True), 0.0)
    qdir_two = halves(qdir)
    qm_ref[...] = query - mm3(qdir_two, solve_two)
    value = v_ref[...].astype(LOW)
    pack_ref[0:length, :] = (key - mm3(carried_two, unit_two, ta=True)).astype(LOW)
    pack_ref[length : 2 * length, :] = value
    eye = jnp.where(iota((dim, dim), 0) == iota((dim, dim), 1), 1.0, 0.0)
    pack_ref[2 * length :, :] = (eye - mm3(unit_two, solve_two, ta=True)).astype(LOW)
    inside = mm(query, key, tb=True) - mm(qdir_two[0], carried_two[0])
    inv_ref[...] = inverse.astype(LOW)
    carried_ref[...] = carried.astype(LOW)
    qdir_ref[...] = qdir.astype(LOW)
    solve_ref[...] = solve.astype(LOW)
    allowed = (doc_col_ref[...] == doc_row_ref[...]) & (row >= col)
    score = jnp.where(allowed, inside * dim**-0.5, NEGATIVE)
    score_ref[...] = score
    peak = jnp.max(score, axis=1, keepdims=True)
    weight = jnp.exp(score - peak)
    peak_ref[...] = jnp.broadcast_to(peak, (length, dim))
    total_ref[...] = jnp.broadcast_to(jnp.sum(weight, axis=1, keepdims=True), (length, dim))
    acc_ref[...] = mm(weight, value)


def cross_forward(
    place_ref, qm_ref, pack_ref, peak_ref, total_ref, acc_ref, doc_col_ref, doc_row_ref,
    att_ref, att_low_ref, log_ref, moved_ref, stat_ref,
):
    length, dim = qm_ref.shape
    stride = 2 * length + dim
    place = place_ref[0]
    doc_col = doc_col_ref[...]

    moved_ref[...] = qm_ref[...]
    att_ref[...] = acc_ref[...]
    stat_ref[0] = peak_ref[:, 0:1]
    stat_ref[1] = total_ref[:, 0:1]

    def hop(step, carry):
        at = place - step
        base = pl.multiple_of(at * stride, 128)
        key = pack_ref[pl.ds(base, length), :]
        value = pack_ref[pl.ds(pl.multiple_of(base + length, 128), length), :]
        through = pack_ref[pl.ds(pl.multiple_of(base + 2 * length, 128), dim), :]
        allowed = doc_col == doc_row_ref[at]
        moved = moved_ref[...]
        peak = stat_ref[0]
        score = jnp.where(allowed, mm(moved, key, tb=True) * dim**-0.5, NEGATIVE)
        new_peak = jnp.maximum(peak, jnp.max(score, axis=1, keepdims=True))
        rescale = jnp.exp(peak - new_peak)
        weight = jnp.exp(score - new_peak)
        stat_ref[0] = new_peak
        stat_ref[1] = stat_ref[1] * rescale + jnp.sum(weight, axis=1, keepdims=True)
        att_ref[...] = att_ref[...] * rescale + mm(weight, value)
        moved_ref[...] = mm(moved, through)
        return carry

    lax.fori_loop(1, place + 1, hop, 0)
    total = stat_ref[1]
    attention = att_ref[...] / total
    att_ref[...] = attention
    att_low_ref[...] = attention.astype(LOW)
    log_ref[...] = jnp.broadcast_to(stat_ref[0] + jnp.log(total), (length, dim))


def cross_backward(
    place_ref, qm_ref, pack_ref, score_ref, att_ref, log_ref, datt_ref, doc_col_ref, doc_row_ref,
    dpack_ref, dqm_ref, dinside_ref, dval_ref, chain_ref, dchain_ref,
):
    length, dim = qm_ref.shape
    stride = 2 * length + dim
    place = place_ref[0]
    doc_col = doc_col_ref[...]
    scale = dim**-0.5
    datt = datt_ref[...]
    log_total = log_ref[:, 0:1]
    delta = jnp.sum(datt.astype(WIDE) * att_ref[...], axis=1, keepdims=True)
    own = pl.multiple_of(place * stride, 128)
    value = pack_ref[pl.ds(pl.multiple_of(own + length, 128), length), :]
    probs = jnp.exp(score_ref[...] - log_total)
    dprob = mm(datt, value, tb=True)
    dinside_ref[...] = (probs * (dprob - delta) * scale).astype(LOW)
    dval_ref[...] = mm(probs, datt, ta=True)
    chain_ref[1] = qm_ref[...]

    def blank(at, carry):
        base = pl.multiple_of(at * stride, 128)
        dpack_ref[pl.ds(base, stride), :] = jnp.zeros((stride, dim), LOW)
        return carry

    lax.fori_loop(place, SPAN, blank, 0)

    def hop(step, carry):
        at = place - step
        base = pl.multiple_of(at * stride, 128)
        moved = chain_ref[step]
        key = pack_ref[pl.ds(base, length), :]
        value = pack_ref[pl.ds(pl.multiple_of(base + length, 128), length), :]
        through = pack_ref[pl.ds(pl.multiple_of(base + 2 * length, 128), dim), :]
        chain_ref[step + 1] = mm(moved, through)
        allowed = doc_col == doc_row_ref[at]
        score = jnp.where(allowed, mm(moved, key, tb=True) * scale, NEGATIVE)
        probs = jnp.exp(score - log_total)
        dprob = mm(datt, value, tb=True)
        dscore = probs * (dprob - delta) * scale
        dchain_ref[step] = mm(dscore, key)
        dpack_ref[pl.ds(base, length), :] = mm(dscore, moved, ta=True).astype(LOW)
        dpack_ref[pl.ds(pl.multiple_of(base + length, 128), length), :] = mm(probs, datt, ta=True).astype(LOW)
        return carry

    lax.fori_loop(1, place + 1, hop, 0)

    def back(count, carry):
        step = place - count
        base = pl.multiple_of((place - step) * stride + 2 * length, 128)
        through = pack_ref[pl.ds(base, dim), :]
        grad = dqm_ref[...]
        dpack_ref[pl.ds(base, dim), :] = mm(chain_ref[step], grad, ta=True).astype(LOW)
        dqm_ref[...] = dchain_ref[step] + mm(grad, through, tb=True)
        return carry

    dqm_ref[...] = jnp.zeros((length, dim), WIDE)
    lax.fori_loop(0, place, back, 0)


def block_backward(
    q_ref, k_ref, d_ref, beta_ref, inv_ref, carried_ref, qdir_ref, solve_ref,
    dqm_ref, dinside_ref, dval_ref, dpack_ref,
    dq_ref, dk_ref, dv_ref, dd_ref, dbeta_ref,
):
    head = pl.program_id(0)
    query, key, dirs = q_ref[...], k_ref[...], d_ref[...]
    length, dim = query.shape
    beta = pick_beta(beta_ref, head)
    norm = lax.rsqrt(jnp.sum(dirs * dirs, axis=-1, keepdims=True) + EPSILON)
    unit = dirs * norm
    low_unit, low_key, low_query = unit.astype(LOW), key.astype(LOW), query.astype(LOW)
    row, col = iota((length, length), 0), iota((length, length), 1)
    inverse, carried, qdir, solve = inv_ref[...], carried_ref[...], qdir_ref[...], solve_ref[...]
    dqm, dinside = dqm_ref[...].astype(LOW), dinside_ref[...]
    dkm = dpack_ref[0:length, :]
    dthrough = dpack_ref[2 * length :, :]
    dv_ref[...] = (dval_ref[...] + dpack_ref[length : 2 * length, :].astype(WIDE)).astype(LOW)
    dqdir = -jnp.where(row >= col, mm(dqm, solve, tb=True) + mm(dinside, carried, tb=True), 0.0).astype(LOW)
    dq_ref[...] = (dqm_ref[...] + mm(dinside, low_key) + mm(dqdir, low_unit)).astype(LOW)
    dsolve = -(mm(qdir, dqm, ta=True) + mm(low_unit, dthrough))
    dcarried = -(mm(low_unit, dkm, tb=True) + mm(qdir, dinside, ta=True))
    ysolve = mm(inverse, dsolve, ta=True)
    ycarried = mm(inverse, dcarried, ta=True)
    ddir_key = jnp.where(row > col, ycarried, 0.0).astype(LOW)
    dlower = -(mm(ysolve, solve, tb=True) + mm(ycarried, carried, tb=True))
    ddiag = jnp.sum(jnp.where(row == col, dlower, 0.0), axis=1, keepdims=True)
    dgram = jnp.where(row > col, dlower, 0.0).astype(LOW)
    dk_ref[...] = (dkm.astype(WIDE) + mm(dinside, low_query, ta=True) + mm(ddir_key, low_unit, ta=True)).astype(LOW)
    dunit = (
        ysolve
        - mm(solve, dthrough, tb=True)
        - mm(carried, dkm)
        + mm(dqdir, low_query, ta=True)
        + mm(ddir_key, low_key)
        + mm(dgram, low_unit)
        + mm(dgram, low_unit, ta=True)
    )
    along = jnp.sum(dunit * dirs, axis=1, keepdims=True)
    dd_ref[...] = (norm * dunit - dirs * (norm * norm * norm * along)).astype(LOW)
    dbeta = -ddiag / jnp.maximum(beta, 1e-30) * (1.0 - 0.5 * beta)
    lane = iota(dbeta_ref.shape, 1)

    @pl.when(head == 0)
    def start():
        dbeta_ref[...] = jnp.zeros_like(dbeta_ref)

    dbeta_ref[...] = jnp.where(lane == head, dbeta.astype(LOW), dbeta_ref[...])


def column(rows, cols, offset=0):
    return pl.BlockSpec((rows, cols), lambda head, *unused, offset=offset: (0, head + offset))


def stacked(rows, cols):
    return pl.BlockSpec((rows, cols), lambda head, *unused: (head, 0))


def fixed(shape):
    return pl.BlockSpec(shape, lambda head, *unused: (0,) * len(shape))


def params():
    return pltpu.CompilerParams(vmem_limit_bytes=VMEM_BYTES)


def shape_of(rows, cols, dtype):
    return jax.ShapeDtypeStruct((rows, cols), dtype)


def dot(left, right, ta=False, tb=False):
    dims = (((0 if ta else 1,), (1 if tb else 0,)), ((), ()))
    return lax.dot_general(left, right, dims, preferred_element_type=WIDE)


def norm_back(grad, value, scale, gain):
    weighted = grad * gain
    return scale * weighted - value * scale * scale * scale * jnp.mean(weighted * value, axis=-1, keepdims=True)


def run_block_forward(proj, my_docs_col, my_docs, heads, inner):
    row_count = proj.shape[0]
    dim = inner // heads
    stride = 2 * row_count + dim
    wide_block = column(row_count, dim)
    square = stacked(row_count, row_count)
    beta_spec = pl.BlockSpec((row_count, 128), lambda head, *unused: (0, 4 * inner // 128))
    square_low = shape_of(heads * row_count, row_count, LOW)
    tall_wide = shape_of(row_count, inner, WIDE)
    return pl.pallas_call(
        block_forward,
        grid=(heads,),
        in_specs=[
            column(row_count, dim),
            column(row_count, dim, heads),
            column(row_count, dim, 2 * heads),
            column(row_count, dim, 3 * heads),
            beta_spec,
            fixed((row_count, 1)),
            fixed((1, row_count)),
        ],
        out_specs=[column(stride, dim), wide_block, square, square, square, square, wide_block, wide_block, wide_block, wide_block],
        out_shape=[
            shape_of(stride, inner, LOW),
            tall_wide,
            shape_of(heads * row_count, row_count, WIDE),
            square_low,
            square_low,
            square_low,
            shape_of(row_count, inner, LOW),
            tall_wide,
            tall_wide,
            tall_wide,
        ],
        compiler_params=params(),
        name="block_forward",
    )(proj, proj, proj, proj, proj, my_docs_col, my_docs)


def run_cross_forward(place, q_moved, packs, peak, total, acc, my_docs_col, docs, heads):
    row_count, inner = q_moved.shape
    dim = inner // heads
    wide_block = column(row_count, dim)
    tall_wide = shape_of(row_count, inner, WIDE)
    return pl.pallas_call(
        cross_forward,
        grid_spec=pltpu.PrefetchScalarGridSpec(
            num_scalar_prefetch=1,
            grid=(heads,),
            in_specs=[
                wide_block,
                column(packs.shape[0], dim),
                wide_block,
                wide_block,
                wide_block,
                fixed((row_count, 1)),
                fixed((SPAN, 1, row_count)),
            ],
            out_specs=[wide_block, wide_block, wide_block],
            scratch_shapes=[pltpu.VMEM((row_count, dim), WIDE), pltpu.VMEM((2, row_count, 1), WIDE)],
        ),
        out_shape=[tall_wide, shape_of(row_count, inner, LOW), tall_wide],
        compiler_params=params(),
        name="cross_forward",
    )(place, q_moved, packs, peak, total, acc, my_docs_col, docs)


def run_cross_backward(place, q_moved, packs, own_scores, attention, log_total, d_attention, my_docs_col, docs, heads):
    row_count, inner = q_moved.shape
    dim = inner // heads
    wide_block = column(row_count, dim)
    packs_spec = column(packs.shape[0], dim)
    square = stacked(row_count, row_count)
    tall_wide = shape_of(row_count, inner, WIDE)
    return pl.pallas_call(
        cross_backward,
        grid_spec=pltpu.PrefetchScalarGridSpec(
            num_scalar_prefetch=1,
            grid=(heads,),
            in_specs=[
                wide_block,
                packs_spec,
                square,
                wide_block,
                wide_block,
                wide_block,
                fixed((row_count, 1)),
                fixed((SPAN, 1, row_count)),
            ],
            out_specs=[packs_spec, wide_block, square, wide_block],
            scratch_shapes=[
                pltpu.VMEM((SPAN + 1, row_count, dim), WIDE),
                pltpu.VMEM((SPAN, row_count, dim), WIDE),
            ],
        ),
        out_shape=[shape_of(packs.shape[0], inner, LOW), tall_wide, shape_of(heads * row_count, row_count, LOW), tall_wide],
        compiler_params=params(),
        name="cross_backward",
    )(place, q_moved, packs, own_scores, attention, log_total, d_attention, my_docs_col, docs)


def run_block_backward(proj, inverse, carried, qdir, solve, dq_moved, d_inside, d_val_own, d_pack, heads):
    row_count, inner = dq_moved.shape
    dim = inner // heads
    wide_block = column(row_count, dim)
    square = stacked(row_count, row_count)
    tall_low = shape_of(row_count, inner, LOW)
    return pl.pallas_call(
        block_backward,
        grid=(heads,),
        in_specs=[
            column(row_count, dim),
            column(row_count, dim, heads),
            column(row_count, dim, 3 * heads),
            pl.BlockSpec((row_count, 128), lambda head, *unused: (0, 4 * inner // 128)),
            square,
            square,
            square,
            wide_block,
            wide_block,
            square,
            wide_block,
            column(d_pack.shape[0], dim),
        ],
        out_specs=[wide_block, wide_block, wide_block, wide_block, fixed((row_count, 128))],
        out_shape=[tall_low, tall_low, tall_low, tall_low, shape_of(row_count, 128, LOW)],
        compiler_params=params(),
        name="block_backward",
    )(proj, proj, proj, proj, inverse, carried, qdir, solve, dq_moved, d_inside, d_val_own, d_pack)


def per_device(
    tokens, cotangent, starts, gain_attn, w_query, w_key, w_value, w_dir, w_beta, w_out, gain_mlp, w_gate, w_up, w_down
):
    row_count, width = tokens.shape
    shard = w_query.shape[0]
    inner = w_query.shape[1]
    hidden_units = w_gate.shape[1]
    heads = w_beta.shape[1]
    dim = inner // heads
    count = lax.axis_size("seq")
    seq_place = lax.axis_index("seq")
    row_place = seq_place % SPAN
    groups = [list(range(at, at + SPAN)) for at in range(0, count, SPAN)]

    start_cols = -(-row_count // shard)
    marks = jnp.pad(starts.astype(LOW), (0, start_cols * shard - row_count)).reshape(start_cols, shard).T
    extra = jnp.concatenate([w_beta, gain_attn[:, None], gain_mlp[:, None], marks], axis=1)
    extra = jnp.pad(extra, ((0, 0), (0, 128 - extra.shape[1])))
    packed_in = jnp.concatenate([w_query, w_key, w_value, w_dir, extra], axis=1)
    w_in = lax.all_gather(packed_in, "seq", axis=0, tiled=True)
    tail = w_in[:, 4 * inner :]
    packed_rest = jnp.concatenate([w_out.T, w_gate, w_up, w_down.T], axis=1)
    packed_rest, tail = lax.optimization_barrier((packed_rest, tail))
    w_rest = lax.all_gather(packed_rest, "seq", axis=0, tiled=True)

    gain_one = tail[:, heads].astype(WIDE)
    gain_two = tail[:, heads + 1].astype(WIDE)
    start_all = tail[:, heads + 2 : heads + 2 + start_cols].reshape(count, shard, start_cols)
    start_all = start_all.transpose(0, 2, 1).reshape(count, start_cols * shard)[:, :row_count]
    row_marks = lax.dynamic_slice_in_dim(start_all, seq_place // SPAN * SPAN, SPAN, axis=0)
    docs = jnp.cumsum(row_marks.astype(jnp.int32).reshape(-1)).reshape(SPAN, 1, row_count)
    my_docs = lax.dynamic_slice_in_dim(docs, row_place, 1, axis=0).reshape(1, row_count)
    my_docs_col = my_docs.reshape(row_count, 1)
    place = row_place.astype(jnp.int32).reshape(1)

    stream = tokens.astype(WIDE)
    scale_one = lax.rsqrt(jnp.mean(stream * stream, axis=-1, keepdims=True) + EPSILON)
    normed = (stream * scale_one * gain_one).astype(LOW)
    proj = dot(normed, w_in)

    pack, q_moved, own_scores, inverse, carried, qdir, solve, peak, total, acc = run_block_forward(
        proj, my_docs_col, my_docs, heads, inner
    )
    packs = lax.all_gather(pack, "seq", axis=0, tiled=True, axis_index_groups=groups)
    attention, attention_low, log_total = run_cross_forward(
        place, q_moved, packs, peak, total, acc, my_docs_col, docs, heads
    )

    w_out_t = w_rest[:, :inner]
    w_gate_all = w_rest[:, inner : inner + hidden_units]
    w_up_all = w_rest[:, inner + hidden_units : inner + 2 * hidden_units]
    w_down_t = w_rest[:, inner + 2 * hidden_units :]
    branch_part = dot(attention_low, w_out_t, tb=True).astype(LOW)
    branch = lax.psum(branch_part, "head").astype(WIDE)
    middle = stream + branch
    scale_two = lax.rsqrt(jnp.mean(middle * middle, axis=-1, keepdims=True) + EPSILON)
    normed_two = (middle * scale_two * gain_two).astype(LOW)
    gate_in = dot(normed_two, w_gate_all)
    up_in = dot(normed_two, w_up_all)
    d_hidden = dot(cotangent, w_down_t)
    gate_sig = jax.nn.sigmoid(gate_in)
    hidden = (gate_in * gate_sig * up_in).astype(LOW)
    d_gate = (d_hidden * up_in * gate_sig * (1.0 + gate_in * (1.0 - gate_sig))).astype(LOW)
    d_up = (d_hidden * gate_in * gate_sig).astype(LOW)
    back_two = (dot(d_gate, w_gate_all, tb=True) + dot(d_up, w_up_all, tb=True)).astype(LOW)
    d_normed_two = lax.psum(back_two, "head").astype(WIDE)
    mlp_part = dot(hidden, w_down_t, tb=True).astype(LOW)
    mlp_part, d_normed_two = lax.optimization_barrier((mlp_part, d_normed_two))

    grad_mlp = jnp.concatenate(
        [
            dot(normed_two, d_gate, ta=True).astype(LOW),
            dot(normed_two, d_up, ta=True).astype(LOW),
            dot(cotangent, hidden, ta=True).astype(LOW),
        ],
        axis=1,
    )
    reduced_mlp = lax.psum_scatter(grad_mlp, "seq", scatter_dimension=0, tiled=True)

    grad_gain_two = jnp.sum(d_normed_two * middle * scale_two, axis=0)
    d_middle = cotangent.astype(WIDE) + norm_back(d_normed_two, middle, scale_two, gain_two)
    d_branch = d_middle.astype(LOW)
    d_attention = dot(d_branch, w_out_t).astype(LOW)
    grad_out_t = dot(d_branch, attention_low, ta=True).astype(LOW)

    d_packs, dq_moved, d_inside, d_val_own = run_cross_backward(
        place, q_moved, packs, own_scores, attention, log_total, d_attention, my_docs_col, docs, heads
    )
    d_pack = lax.psum_scatter(d_packs, "seq", scatter_dimension=0, tiled=True, axis_index_groups=groups)

    d_query, d_key, d_value, d_dir, d_beta = run_block_backward(
        proj, inverse, carried, qdir, solve, dq_moved, d_inside, d_val_own, d_pack, heads
    )
    d_proj = jnp.concatenate([d_query, d_key, d_value, d_dir, d_beta], axis=1)
    back_one = dot(d_proj, w_in, tb=True)
    d_normed = lax.psum(back_one.astype(LOW), "head").astype(WIDE)
    d_tokens = d_middle + norm_back(d_normed, stream, scale_one, gain_one)
    gain_sum = jnp.sum(d_normed * stream * scale_one, axis=0)
    gains = jnp.stack([gain_sum, grad_gain_two], axis=1).astype(LOW)

    grad_in = jnp.concatenate([dot(normed, d_proj, ta=True).astype(LOW), grad_out_t], axis=1)
    reduced_in = lax.psum_scatter(grad_in, "seq", scatter_dimension=0, tiled=True).astype(WIDE)
    gains = lax.psum_scatter(gains, "seq", scatter_dimension=0, tiled=True).astype(WIDE)

    mlp_out = lax.psum(mlp_part, "head").astype(WIDE)
    result = (middle + mlp_out).astype(LOW)
    reduced_mlp = reduced_mlp.astype(WIDE)
    end = 4 * inner + 128
    return (
        result,
        d_tokens,
        gains[:, 0],
        reduced_in[:, :inner],
        reduced_in[:, inner : 2 * inner],
        reduced_in[:, 2 * inner : 3 * inner],
        reduced_in[:, 3 * inner : 4 * inner],
        reduced_in[:, 4 * inner : 4 * inner + heads],
        reduced_in[:, end:].T,
        gains[:, 1],
        reduced_mlp[:, :hidden_units],
        reduced_mlp[:, hidden_units : 2 * hidden_units],
        reduced_mlp[:, 2 * hidden_units :].T,
    )


def solution(mesh):
    placed = (
        P("seq", None),
        P("seq", None),
        P("seq"),
        P("seq"),
        P("seq", "head"),
        P("seq", "head"),
        P("seq", "head"),
        P("seq", "head"),
        P("seq", "head"),
        P("head", "seq"),
        P("seq"),
        P("seq", "head"),
        P("seq", "head"),
        P("head", "seq"),
    )
    return jax.shard_map(
        per_device,
        mesh=mesh,
        in_specs=placed,
        out_specs=(
            P("seq", None),
            P("seq", None),
            P("seq"),
            P("seq", "head"),
            P("seq", "head"),
            P("seq", "head"),
            P("seq", "head"),
            P("seq", "head"),
            P("head", "seq"),
            P("seq"),
            P("seq", "head"),
            P("seq", "head"),
            P("head", "seq"),
        ),
        check_vma=False,
    )
```

```python
import functools

import jax
import jax.numpy as jnp
from jax import lax
from jax.experimental import pallas as pl
from jax.experimental.pallas import tpu as pltpu
from jax.sharding import PartitionSpec as P

SPAN = 8
EPSILON = 1e-06
NEGATIVE = -1e30
LOW = jnp.bfloat16
WIDE = jnp.float32
VMEM_BYTES = 60 * 2**20


def mm(left, right, ta=False, tb=False):
    dims = (((0 if ta else 1,), (1 if tb else 0,)), ((), ()))
    return lax.dot_general(
        left.astype(LOW), right.astype(LOW), dims, preferred_element_type=WIDE
    )


def halves(value):
    high = value.astype(LOW)
    return high, (value - high.astype(WIDE)).astype(LOW)


def mm3(left, right, ta=False, tb=False):
    left_hi, left_lo = left if isinstance(left, tuple) else halves(left)
    right_hi, right_lo = right if isinstance(right, tuple) else halves(right)
    return mm(left_hi, right_hi, ta, tb) + (mm(left_hi, right_lo, ta, tb) + mm(left_lo, right_hi, ta, tb))


def iota(shape, axis):
    return lax.broadcasted_iota(jnp.int32, shape, axis)


def lower_inverse(strict, beta):
    length = strict.shape[0]
    size = 128
    row, col = iota((size, size), 0), iota((size, size), 1)
    subs, blocks = [], []
    for at in range(0, length, size):
        sub = strict[at : at + size, at : at + size]
        scale = beta[at : at + size]
        diag = jnp.where(row == col, scale, 0.0)
        across = jnp.sum(diag, axis=0, keepdims=True)
        pair = ((row >> 1) == (col >> 1)) & (row > col)
        subs.append(sub)
        blocks.append(diag - jnp.where(pair, sub * scale * across, 0.0))
    bit = 1
    while (1 << bit) < size:
        mask = ((row >> (bit + 1)) == (col >> (bit + 1))) & ((row >> bit) != (col >> bit)) & (row > col)
        right = [mm3(jnp.where(mask, sub, 0.0), block) for sub, block in zip(subs, blocks)]
        blocks = [block - mm3(block, part) for block, part in zip(blocks, right)]
        bit += 1
    while len(blocks) > 1:
        size = blocks[0].shape[0]
        joined = []
        for pair_at in range(len(blocks) // 2):
            first, second = blocks[2 * pair_at], blocks[2 * pair_at + 1]
            at = 2 * pair_at * size
            corner = -mm3(second, mm3(strict[at + size : at + 2 * size, at : at + size], first))
            joined.append(
                jnp.concatenate(
                    [
                        jnp.concatenate([first, jnp.zeros_like(first)], axis=1),
                        jnp.concatenate([corner, second], axis=1),
                    ],
                    axis=0,
                )
            )
        blocks = joined
    return blocks[0]


def xor_move(value, axis, mask):
    return lax.ppermute(value, axis, [(at, at ^ mask) for at in range(lax.axis_size(axis))])


def after(value, *others):
    return lax.optimization_barrier((value, *others))[0]


def doubled_again(held, mask):
    return jnp.concatenate([held, xor_move(held, "seq", mask)], axis=0)


def doubled(block, masks):
    held = block[None]
    for mask in masks:
        held = doubled_again(held, mask)
    return held


def block_forward(
    head, place_ref, normed_ref, w_ref, beta_ref, doc_col_ref, doc_row_ref,
    proj_ref, pack_ref, qm_ref, score_ref, inv_ref, carried_ref, qdir_ref, solve_ref, stat_ref, acc_ref,
):
    proj_ref[...] = mm(normed_ref[...], w_ref[...])
    length, dim = qm_ref.shape
    query, key = proj_ref[:, 0:dim], proj_ref[:, dim : 2 * dim]
    value, dirs = proj_ref[:, 2 * dim : 3 * dim].astype(LOW), proj_ref[:, 3 * dim :]
    beta = 2.0 * jax.nn.sigmoid(beta_ref[:, head : head + 1])
    unit = dirs * lax.rsqrt(jnp.sum(dirs * dirs, axis=-1, keepdims=True) + EPSILON)
    row, col = iota((length, length), 0), iota((length, length), 1)
    unit_two = halves(unit)
    strict = jnp.where(row > col, mm3(unit_two, unit_two, tb=True), 0.0)
    inverse = lower_inverse(strict, beta)
    inverse_two = halves(inverse)
    solve = mm3(inverse_two, unit_two)
    solve_two = halves(solve)
    dir_key = jnp.where(row > col, mm3(unit_two, key, tb=True), 0.0)
    carried = mm3(inverse_two, dir_key)
    carried_two = halves(carried)
    qdir = jnp.where(row >= col, mm3(query, unit_two, tb=True), 0.0)
    qdir_two = halves(qdir)
    qm_ref[...] = query - mm3(qdir_two, solve_two)
    pack_ref[0:length, :] = (key - mm3(carried_two, unit_two, ta=True)).astype(LOW)
    pack_ref[length : 2 * length, :] = value
    eye = jnp.where(iota((dim, dim), 0) == iota((dim, dim), 1), 1.0, 0.0)
    pack_ref[2 * length :, :] = (eye - mm3(unit_two, solve_two, ta=True)).astype(LOW)
    inside = mm(query, key, tb=True) - mm(qdir_two[0], carried_two[0])
    inv_ref[...] = inverse.astype(LOW)
    carried_ref[...] = carried_two[0]
    qdir_ref[...] = qdir_two[0]
    solve_ref[...] = solve_two[0]
    allowed = (doc_col_ref[:, 0:1] == doc_row_ref[pl.ds(place_ref[0], 1), :]) & (row >= col)
    score = jnp.where(allowed, inside * dim**-0.5, NEGATIVE)
    score_ref[...] = score
    peak = jnp.max(score, axis=1, keepdims=True)
    weight = jnp.exp(score - peak)
    lane = iota((length, 128), 1)
    stat_ref[...] = jnp.where(lane == 0, peak, jnp.sum(weight, axis=1, keepdims=True))
    acc_ref[...] = mm(weight, value)


def slot_of(mask, swapped):
    core, first, second = mask & 1, (mask >> 1) & 1, mask >> 2
    return 4 * core + (2 * first + second if swapped else first + 2 * second)


def cross_forward(
    swapped, place_ref, qm_ref, stat_in_ref, acc_ref, doc_col_ref, doc_row_ref, pack_ref,
    att_ref, att_x_ref, log_ref, moved_ref, stat_ref,
):
    length, dim = qm_ref.shape
    place = place_ref[0]
    doc_col = doc_col_ref[:, 0:1]
    moved_ref[...] = qm_ref[...]
    att_ref[...] = acc_ref[...]
    stat_ref[0] = stat_in_ref[:, 0:1]
    stat_ref[1] = stat_in_ref[:, 1:2]

    def hop(step, carry):
        at = place - step
        slot = slot_of(place ^ at, swapped)
        key = pack_ref[slot, 0:length, :]
        value = pack_ref[slot, length : 2 * length, :]
        through = pack_ref[slot, 2 * length :, :]
        allowed = doc_col == doc_row_ref[pl.ds(at, 1), :]
        moved = moved_ref[...]
        peak = stat_ref[0]
        score = jnp.where(allowed, mm(moved, key, tb=True) * dim**-0.5, NEGATIVE)
        new_peak = jnp.maximum(peak, jnp.max(score, axis=1, keepdims=True))
        rescale = jnp.exp(peak - new_peak)
        weight = jnp.exp(score - new_peak)
        stat_ref[0] = new_peak
        stat_ref[1] = stat_ref[1] * rescale + jnp.sum(weight, axis=1, keepdims=True)
        att_ref[...] = att_ref[...] * rescale + mm(weight, value)
        moved_ref[...] = mm(moved, through)
        return carry

    lax.fori_loop(1, place + 1, hop, 0)
    total = stat_ref[1]
    attention = att_ref[...] / total
    att_ref[...] = attention
    scatter_rows(att_x_ref, slice(None), attention.astype(LOW), place_ref[1])
    log_ref[...] = jnp.broadcast_to(stat_ref[0] + jnp.log(total), (length, dim))


def scatter_rows(ref, columns, value, mask, chunk=128):
    for at in range(value.shape[0] // chunk):
        start = pl.multiple_of((mask ^ at) * chunk, chunk)
        ref[pl.ds(start, chunk), columns] = value[at * chunk : (at + 1) * chunk]


def cross_backward(swapped, place_ref, qm_ref, score_ref, att_ref, log_ref, doc_col_ref, doc_row_ref, pack_ref, *rest):
    *datts, even_ref, odd_ref, dqm_ref, dinside_ref, dval_ref, chain_ref, dchain_ref, datt_ref = rest
    length, dim = qm_ref.shape
    place = place_ref[0]
    chunk = datts[0].shape[0]
    for at, part in enumerate(datts):
        start = pl.multiple_of((place_ref[1] ^ at) * chunk, chunk)
        datt_ref[pl.ds(start, chunk), :] = part[...]
    doc_col = doc_col_ref[:, 0:1]
    scale = dim**-0.5
    datt = datt_ref[...]
    log_total = log_ref[:, 0:1]
    delta = jnp.sum(datt.astype(WIDE) * att_ref[...], axis=1, keepdims=True)
    value = pack_ref[0, length : 2 * length, :]
    probs = jnp.exp(score_ref[...] - log_total)
    dprob = mm(datt, value, tb=True)
    dinside_ref[...] = (probs * (dprob - delta) * scale).astype(LOW)
    dval_ref[...] = mm(probs, datt, ta=True)
    chain_ref[1] = qm_ref[...]

    def put(slot, rows, part):
        @pl.when(slot < 4)
        def to_even():
            even_ref[slot, rows, :] = part.astype(LOW)

        @pl.when(slot >= 4)
        def to_odd():
            odd_ref[slot - 4, rows, :] = part.astype(LOW)

    def blank(at, carry):
        put(slot_of(place ^ at, swapped), slice(None), jnp.zeros(even_ref.shape[1:], LOW))
        return carry

    lax.fori_loop(place, SPAN, blank, 0)

    def hop(step, carry):
        at = place - step
        slot = slot_of(place ^ at, swapped)
        moved = chain_ref[step]
        key = pack_ref[slot, 0:length, :]
        value = pack_ref[slot, length : 2 * length, :]
        through = pack_ref[slot, 2 * length :, :]
        chain_ref[step + 1] = mm(moved, through)
        allowed = doc_col == doc_row_ref[pl.ds(at, 1), :]
        score = jnp.where(allowed, mm(moved, key, tb=True) * scale, NEGATIVE)
        probs = jnp.exp(score - log_total)
        dprob = mm(datt, value, tb=True)
        dscore = probs * (dprob - delta) * scale
        dchain_ref[step] = mm(dscore, key)
        put(slot, slice(0, length), mm(dscore, moved, ta=True))
        put(slot, slice(length, 2 * length), mm(probs, datt, ta=True))
        return carry

    lax.fori_loop(1, place + 1, hop, 0)

    def back(count, carry):
        step = place - count
        slot = slot_of(place ^ (place - step), swapped)
        through = pack_ref[slot, 2 * length :, :]
        grad = dqm_ref[...]
        put(slot, slice(2 * length, 2 * length + dim), mm(chain_ref[step], grad, ta=True))
        dqm_ref[...] = dchain_ref[step] + mm(grad, through, tb=True)
        return carry

    dqm_ref[...] = jnp.zeros((length, dim), WIDE)
    lax.fori_loop(0, place, back, 0)


def block_backward(
    head, place_ref, proj_ref, beta_ref, inv_ref, carried_ref, qdir_ref, solve_ref, dqm_ref, dinside_ref, dval_ref, *rest
):
    *dpacks, dproj_ref, dbeta_ref = rest
    length, dim = dqm_ref.shape
    query, key, dirs = proj_ref[:, 0:dim], proj_ref[:, dim : 2 * dim], proj_ref[:, 3 * dim :]
    beta = 2.0 * jax.nn.sigmoid(beta_ref[:, head : head + 1])
    norm = lax.rsqrt(jnp.sum(dirs * dirs, axis=-1, keepdims=True) + EPSILON)
    unit = dirs * norm
    low_unit, low_key, low_query = unit.astype(LOW), key.astype(LOW), query.astype(LOW)
    row, col = iota((length, length), 0), iota((length, length), 1)
    inverse, carried, qdir, solve = inv_ref[...], carried_ref[...], qdir_ref[...], solve_ref[...]
    dqm, dinside = dqm_ref[...].astype(LOW), dinside_ref[...]

    def summed(rows):
        return sum(part[rows, :].astype(WIDE) for part in dpacks)

    dkm = summed(slice(0, length))
    dthrough = summed(slice(2 * length, 2 * length + dim)).astype(LOW)
    dvalue = dval_ref[...] + summed(slice(length, 2 * length))
    dkm_low = dkm.astype(LOW)
    dqdir = -jnp.where(row >= col, mm(dqm, solve, tb=True) + mm(dinside, carried, tb=True), 0.0).astype(LOW)
    dquery = dqm_ref[...] + mm(dinside, low_key) + mm(dqdir, low_unit)
    dsolve = -(mm(qdir, dqm, ta=True) + mm(low_unit, dthrough))
    dcarried = -(mm(low_unit, dkm_low, tb=True) + mm(qdir, dinside, ta=True))
    ysolve = mm(inverse, dsolve, ta=True)
    ycarried = mm(inverse, dcarried, ta=True)
    ddir_key = jnp.where(row > col, ycarried, 0.0).astype(LOW)
    dlower = -(mm(ysolve, solve, tb=True) + mm(ycarried, carried, tb=True))
    ddiag = jnp.sum(jnp.where(row == col, dlower, 0.0), axis=1, keepdims=True)
    dgram = jnp.where(row > col, dlower, 0.0).astype(LOW)
    dkey = dkm + mm(dinside, low_query, ta=True) + mm(ddir_key, low_unit, ta=True)
    dunit = (
        ysolve
        - mm(solve, dthrough, tb=True)
        - mm(carried, dkm_low)
        + mm(dqdir, low_query, ta=True)
        + mm(ddir_key, low_key)
        + mm(dgram, low_unit)
        + mm(dgram, low_unit, ta=True)
    )
    along = jnp.sum(dunit * dirs, axis=1, keepdims=True)
    ddirs = norm * dunit - dirs * (norm * norm * norm * along)
    dbeta = -ddiag / jnp.maximum(beta, 1e-30) * (1.0 - 0.5 * beta)
    lane = iota((length, 128), 1)
    mask = place_ref[1]
    for at, part in enumerate((dquery, dkey, dvalue, ddirs)):
        scatter_rows(dproj_ref, slice(at * dim, (at + 1) * dim), part.astype(LOW), mask)
    scatter_rows(dbeta_ref, slice(None), jnp.where(lane == head, dbeta, 0.0).astype(LOW), mask)


def prepare(heads, place_ref, tokens_ref, cot_ref, w_ref, mark_ref, *rest):
    normed_ref, normed_t_ref, tokens_x_ref, cot_x_ref, gains_ref, beta_ref, docs_ref, doc_col_ref, marks_ref = rest
    for slot in range(SPAN):
        mask = 2 * (slot & 1) + 4 * ((slot >> 1) & 1) + (slot >> 2)
        marks_ref[place_ref[0] ^ mask] = mark_ref[slot]
    span = SPAN
    small = w_ref[...]
    across = small.astype(WIDE).T
    gains_ref[...] = across[0:8]
    gain = across[heads : heads + 1]
    stream = tokens_ref[...].astype(WIDE)
    scale = lax.rsqrt(jnp.mean(stream * stream, axis=-1, keepdims=True) + EPSILON)
    normed_wide = stream * scale * gain
    normed = normed_wide.astype(LOW)
    normed_ref[...] = normed
    beta_ref[...] = mm(normed, small)
    mask = place_ref[1]
    scatter_rows(tokens_x_ref, slice(None), tokens_ref[...], mask)
    scatter_rows(cot_x_ref, slice(None), cot_ref[...], mask)
    for at in range(normed.shape[0] // 128):
        start = pl.multiple_of((mask ^ at) * 128, 128)
        normed_t_ref[:, pl.ds(start, 128)] = normed_wide[at * 128 : (at + 1) * 128].T.astype(LOW)
    marks = jnp.sum(marks_ref[...].astype(WIDE), axis=1)
    length = marks.shape[1]
    upper = jnp.where(iota((length, length), 0) <= iota((length, length), 1), 1.0, 0.0)
    docs = mm(marks, upper)
    row = iota(docs.shape, 0)
    before = jnp.zeros_like(docs)
    for at in range(span - 1):
        before = before + jnp.where(row > at, docs[at : at + 1, length - 1 : length], 0.0)
    docs = docs + before
    docs_ref[...] = docs
    own = jnp.sum(jnp.where(row == place_ref[0], docs, 0.0), axis=0, keepdims=True)
    eye = iota((length, length), 0) == iota((length, length), 1)
    column = jnp.sum(jnp.where(eye, own, 0.0), axis=1, keepdims=True)
    doc_col_ref[...] = jnp.broadcast_to(column, doc_col_ref.shape)


def branch_forward(heads, dim, tokens_x_ref, gains_ref, w_out_ref, *rest):
    *pieces, middle_ref, normed_ref, att_ref = rest
    for at, part in enumerate(pieces):
        att_ref[:, at * dim : (at + 1) * dim] = part[...]
    middle = tokens_x_ref[...].astype(WIDE) + mm(att_ref[...], w_out_ref[...], tb=True)
    middle_ref[...] = middle
    scale = lax.rsqrt(jnp.mean(middle * middle, axis=-1, keepdims=True) + EPSILON)
    normed_ref[...] = (middle * scale * gains_ref[heads + 1 : heads + 2]).astype(LOW)


def mlp_forward(cot_ref, gate_ref, up_ref, down_ref, *rest):
    ways = (len(rest) - 3) // 2
    pieces, outs = rest[:ways], rest[ways + 1 : -2]
    all_ref, normed_ref, acc_ref = rest[ways], rest[-2], rest[-1]
    step = pl.program_id(0)
    chunk = pieces[0].shape[0]

    @pl.when(step == 0)
    def start():
        for at, part in enumerate(pieces):
            normed_ref[at * chunk : (at + 1) * chunk, :] = part[...]
        acc_ref[...] = jnp.zeros_like(acc_ref)

    normed = normed_ref[...]
    gate, up, d_hidden = mm(normed, gate_ref[...]), mm(normed, up_ref[...]), mm(cot_ref[...], down_ref[...])
    sig = jax.nn.sigmoid(gate)
    silu = gate * sig
    d_gate = (d_hidden * up * sig * (1.0 + gate * (1.0 - sig))).astype(LOW)
    d_up = (d_hidden * silu).astype(LOW)
    all_ref[0] = d_gate
    all_ref[1] = d_up
    all_ref[2] = (silu * up).astype(LOW)
    acc_ref[...] += mm(d_gate, gate_ref[...], tb=True) + mm(d_up, up_ref[...], tb=True)

    @pl.when(step == pl.num_programs(0) - 1)
    def finish():
        for at, part in enumerate(outs):
            part[...] = acc_ref[at * chunk : (at + 1) * chunk, :].astype(LOW)


def mlp_grads(cot_ref, all_ref, down_ref, middle_ref, *rest):
    ways = (len(rest) - 3) // 2
    pieces, grad_ref, outs, left_ref, acc_ref = rest[:ways], rest[ways], rest[ways + 1 : -2], rest[-2], rest[-1]
    step, third = pl.program_id(0), pl.num_programs(0) // 3
    chunk = pieces[0].shape[0]

    @pl.when(step == 0)
    def start():
        for at, part in enumerate(pieces):
            left_ref[:, at * chunk : (at + 1) * chunk] = part[...].astype(WIDE).T.astype(LOW)
        acc_ref[...] = jnp.zeros_like(acc_ref)
        acc_ref[0:chunk, :] = middle_ref[...]

    @pl.when(step == 2 * third)
    def turn():
        for at in range(ways):
            part = cot_ref[at * chunk : (at + 1) * chunk, :]
            left_ref[:, at * chunk : (at + 1) * chunk] = part.astype(WIDE).T.astype(LOW)

    right = all_ref[0]
    grad_ref[...] = mm(left_ref[...], right).astype(LOW)

    @pl.when(step >= 2 * third)
    def down():
        acc_ref[...] += mm(right, down_ref[...], tb=True)

    @pl.when(step == 3 * third - 1)
    def finish():
        for at, part in enumerate(outs):
            part[...] = acc_ref[at * chunk : (at + 1) * chunk, :].astype(LOW)


def branch_backward(heads, inner, middle_ref, gains_ref, cot_ref, w_out_ref, *rest):
    ways = (len(rest) - 3) // 2
    backs, d_middle_ref, d_branch_ref, gain_ref, d_atts = rest[:ways], rest[ways], rest[ways + 1], rest[ways + 2], rest[ways + 3 :]
    grad = total([part[...] for part in backs])
    middle = middle_ref[...]
    scale = lax.rsqrt(jnp.mean(middle * middle, axis=-1, keepdims=True) + EPSILON)
    gain_ref[...] = jnp.broadcast_to(jnp.sum(grad * middle * scale, axis=0, keepdims=True), gain_ref.shape)
    d_middle = cot_ref[...].astype(WIDE) + norm_back(grad, middle, scale, gains_ref[heads + 1 : heads + 2])
    d_middle_ref[...] = d_middle
    d_branch = d_middle.astype(LOW)
    d_branch_ref[...] = d_branch
    for at, part in enumerate(d_atts):
        part[...] = mm(d_branch, w_out_ref[:, at * inner : (at + 1) * inner]).astype(LOW)


def project_back(heads, tokens_x_ref, w_ref, part_ref, d_proj_ref, *rest):
    d_betas, (gain_ref, d_beta_ref, *outs) = rest[:heads], rest[heads:]
    cols = d_proj_ref.shape[1]
    d_beta = total([part[...] for part in d_betas]).astype(LOW)
    d_beta_ref[...] = d_beta
    back = part_ref[...] + mm(d_beta, w_ref[:, heads * cols :], tb=True)
    back = back + mm(d_proj_ref[...], w_ref[:, (heads - 1) * cols : heads * cols], tb=True)
    stream = tokens_x_ref[...].astype(WIDE)
    scale = lax.rsqrt(jnp.mean(stream * stream, axis=-1, keepdims=True) + EPSILON)
    gain_ref[...] = jnp.broadcast_to(jnp.sum(back * stream * scale, axis=0, keepdims=True), gain_ref.shape)
    chunk = outs[0].shape[0]
    for at, part in enumerate(outs):
        part[...] = back[at * chunk : (at + 1) * chunk].astype(LOW)


def token_grad(heads, tokens_x_ref, gains_ref, d_middle_ref, *rest):
    *backs, out_ref = rest
    grad = total([part[...] for part in backs])
    stream = tokens_x_ref[...].astype(WIDE)
    scale = lax.rsqrt(jnp.mean(stream * stream, axis=-1, keepdims=True) + EPSILON)
    out_ref[...] = (d_middle_ref[...] + norm_back(grad, stream, scale, gains_ref[heads : heads + 1])).astype(LOW)


def token_join(place_ref, *rest):
    *pieces, out_ref = rest
    chunk = pieces[0].shape[0]
    for at, part in enumerate(pieces):
        start = pl.multiple_of((place_ref[1] ^ at) * chunk, chunk)
        out_ref[pl.ds(start, chunk), :] = part[...].astype(out_ref.dtype)


def weight_grads(left_ref, d_proj_ref, *rest):
    rest[-1][...] = mm(left_ref[...], d_proj_ref[...]).astype(LOW)


def out_grads(heads, places_ref, branch_ref, *rest):
    atts, out_ref, turned_ref = rest[:heads], rest[-2], rest[-1]
    step = pl.program_id(0)

    @pl.when(step == 0)
    def turn():
        for at in range(branch_ref.shape[0] // 128):
            start = pl.multiple_of((places_ref[1] ^ at) * 128, 128)
            turned_ref[:, pl.ds(start, 128)] = branch_ref[at * 128 : (at + 1) * 128].astype(WIDE).T.astype(LOW)

    for head in range(heads):

        @pl.when(step == head)
        def one(head=head):
            out_ref[...] = mm(turned_ref[...], atts[head][...]).astype(LOW)


def small_grads(heads, left_ref, d_beta_ref, gain_one_ref, gain_two_ref, *rest):
    out_ref, rows_ref = rest[-2:]
    rows_ref[...] = jnp.zeros_like(rows_ref)
    rows_ref[heads : heads + 1, :] = gain_one_ref[0:1, :]
    rows_ref[heads + 1 : heads + 2, :] = gain_two_ref[0:1, :]
    out_ref[...] = (mm(left_ref[...], d_beta_ref[...]) + rows_ref[...].T).astype(LOW)


def project_more(d_proj_ref, w_ref, *rest):
    part = mm(d_proj_ref[...], w_ref[...], tb=True)
    if len(rest) > 1:
        part = rest[0][...] + part
    rest[-1][...] = part


def grad_join(heads, dim, in_ref, *outs):
    width = 4 * dim
    for head in range(heads):
        for kind, out in enumerate(outs[:4]):
            at = head * width + kind * dim
            out[:, head * dim : (head + 1) * dim] = in_ref[:, at : at + dim].astype(WIDE)
    outs[4][...] = in_ref[:, heads * width : heads * width + 128].astype(WIDE)
    outs[5][...] = in_ref[:, heads * width + 128 :].astype(WIDE)


def fixed(shape):
    return pl.BlockSpec(shape, lambda *unused: (0,) * len(shape))


def column_at(shape, at):
    return pl.BlockSpec(shape, lambda *unused: (0, at))


ANYWHERE = pl.BlockSpec(memory_space=pl.ANY)
SCALARS = pl.BlockSpec(memory_space=pltpu.SMEM)


def run(kernel, name, ins, specs, outs, scratch=(), flops=10**9):
    return pl.pallas_call(
        kernel,
        grid=(1,),
        in_specs=specs,
        out_specs=[fixed(shape) for shape, unused in outs],
        out_shape=[jax.ShapeDtypeStruct(shape, dtype) for shape, dtype in outs],
        scratch_shapes=list(scratch),
        compiler_params=pltpu.CompilerParams(vmem_limit_bytes=VMEM_BYTES),
        cost_estimate=pl.CostEstimate(flops=flops, bytes_accessed=4 * 2**20, transcendentals=2**18),
        name=name,
    )(*ins)


def whole(*arrays):
    return [fixed(array.shape) for array in arrays]


def run_block_forward(places, normed, w_in, at, beta_raw, doc_col, doc_row, dim, head):
    length, width = normed.shape
    square, tall = (length, length), (length, dim)
    return run(
        functools.partial(block_forward, head),
        "block_forward",
        (places, normed, w_in, beta_raw, doc_col, doc_row),
        [SCALARS, *whole(normed), column_at((width, 4 * dim), at), *whole(beta_raw, doc_col, doc_row)],
        [
            ((length, 4 * dim), WIDE),
            ((2 * length + dim, dim), LOW),
            (tall, WIDE),
            (square, WIDE),
            (square, LOW),
            (square, LOW),
            (square, LOW),
            (tall, LOW),
            ((length, 128), WIDE),
            (tall, WIDE),
        ],
        flops=10**10,
    )


def run_cross_forward(places, q_moved, stats, acc, doc_col, docs, packs, swapped):
    length, dim = q_moved.shape
    ins = (q_moved, stats, acc, doc_col, docs, packs)
    return run(
        functools.partial(cross_forward, swapped),
        "cross_forward",
        (places, *ins),
        [SCALARS, *whole(*ins)],
        [((length, dim), WIDE), ((length, dim), LOW), ((length, dim), WIDE)],
        [pltpu.VMEM((length, dim), WIDE), pltpu.VMEM((2, length, 1), WIDE)],
        flops=10**10,
    )


def run_cross_backward(places, q_moved, scores, attention, log_total, doc_col, docs, packs, d_atts, head, swapped):
    length, dim = q_moved.shape
    half = ((SPAN // 2,) + packs.shape[1:], LOW)
    ins = (q_moved, scores, attention, log_total, doc_col, docs, packs)
    return run(
        functools.partial(cross_backward, swapped),
        "cross_backward",
        (places, *ins, *d_atts),
        [SCALARS, *whole(*ins)] + [column_at((part.shape[0], dim), head) for part in d_atts],
        [half, half, ((length, dim), WIDE), ((length, length), LOW), ((length, dim), WIDE)],
        [
            pltpu.VMEM((SPAN + 1, length, dim), WIDE),
            pltpu.VMEM((SPAN, length, dim), WIDE),
            pltpu.VMEM((length, dim), LOW),
        ],
        flops=10**10,
    )


def run_block_backward(places, proj, beta_raw, kept, d_packs, head, dim):
    length = proj.shape[0]
    ins = (proj, beta_raw, *kept, *d_packs)
    return run(
        functools.partial(block_backward, head),
        "block_backward",
        (places, *ins),
        [SCALARS, *whole(*ins)],
        [(proj.shape, LOW), ((length, 128), LOW)],
        flops=5 * 10**9,
    )


def norm_back(grad, value, scale, gain):
    weighted = grad * gain
    return scale * weighted - value * scale * scale * scale * jnp.mean(weighted * value, axis=-1, keepdims=True)


def total(parts):
    out = parts[0].astype(WIDE)
    for part in parts[1:]:
        out = out + part.astype(WIDE)
    return out


def per_device(
    tokens, cotangent, starts, gain_attn, w_query, w_key, w_value, w_dir, w_beta, w_out, gain_mlp, w_gate, w_up, w_down
):
    row_count, width = tokens.shape
    shard, inner = w_query.shape
    hidden_units = w_gate.shape[1]
    heads = w_beta.shape[1]
    dim = inner // heads
    count = lax.axis_size("seq")
    ways = lax.axis_size("head")
    chunk = row_count // ways
    seq_place, head_place = lax.axis_index("seq"), lax.axis_index("head")
    places = jnp.stack([seq_place % SPAN, head_place, seq_place]).astype(jnp.int32)

    def to_heads(parts):
        return [xor_move(part, "head", at) if at else part for at, part in enumerate(parts)]

    def over_heads(part):
        return to_heads([part] * ways)

    parts = []
    for head in range(heads):
        cut = slice(head * dim, (head + 1) * dim)
        parts += [w_query[:, cut], w_key[:, cut], w_value[:, cut], w_dir[:, cut]]
    parts += [w_beta, gain_attn[:, None], gain_mlp[:, None], jnp.zeros((shard, 128 - heads - 2), LOW)]
    w_in = lax.all_gather(jnp.concatenate(parts, axis=1), "seq", axis=0, tiled=True)
    marks = doubled(jnp.pad(starts.astype(LOW)[None], ((0, 15), (0, 0))), (2, 4, 1))
    out_parts = jnp.concatenate(over_heads(w_out.T), axis=1)
    w_in, marks, out_parts = lax.optimization_barrier((w_in, marks, out_parts))
    w_out_x = lax.all_gather(out_parts, "seq", axis=0, tiled=True)

    tall, wide_tall, part_low = (row_count, width), (width, row_count), ((chunk, width), LOW)
    small_at = heads * 4 * dim // 128
    normed, normed_x_t, tokens_x, cot_x, gains, beta_raw, docs, doc_col = run(
        functools.partial(prepare, heads),
        "prepare",
        (places, tokens, cotangent, w_in, marks),
        [SCALARS, *whole(tokens, cotangent), column_at((width, 128), small_at), *whole(marks)],
        [
            (tall, LOW),
            (wide_tall, LOW),
            (tall, LOW),
            (tall, LOW),
            ((8, width), WIDE),
            ((row_count, 128), WIDE),
            ((SPAN, row_count), WIDE),
            ((row_count, 128), WIDE),
        ],
        [pltpu.VMEM((SPAN, 16, row_count), LOW)],
    )

    orders = [(4, 2) if head % 2 else (2, 4) for head in range(heads)]
    first, mixed, ready, full = [], [], {}, {}

    def step(kind, head):
        return (head, kind, xor_move(ready[head], "seq", orders[head][kind] if kind < 2 else 1))

    def meet(outs, moves):
        outs, arrived = lax.optimization_barrier((outs, [move[2] for move in moves]))
        for (head, unused, unused_too), part in zip(moves, arrived):
            ready[head] = jnp.concatenate([ready[head], part], axis=0)
        return outs

    flying = []
    for head in range(heads):
        held = normed if head == 0 else after(normed, first[-1][2])
        outs = run_block_forward(places, held, w_in, head, beta_raw, doc_col, docs, dim, head)
        first.append(meet(outs, flying))
        ready[head] = first[head][1][None]
        flying = [step(at, head - at) for at in range(max(0, head - 2), head + 1)]
    rest_in = jnp.concatenate([w_gate, w_up, w_down.T], axis=1)
    stage = {move[0]: move[1] for move in flying}
    for head in range(heads):
        kept = first[head]
        while stage.get(head, 2) < 2 or any(move[0] == head for move in flying):
            now = [move for move in flying if move[0] == head]
            flying = [move for move in flying if move[0] != head]
            meet((), now)
            if stage[head] < 2:
                stage[head] += 1
                flying.append(step(stage[head], head))
        if head == 0:
            held = kept[2]
        else:
            held = after(kept[2], mixed[-1][0])
        outs = run_cross_forward(places, held, kept[8], kept[9], doc_col, docs, ready[head], head % 2 == 1)
        mixed.append(meet(outs, flying))
        flying = []
        for later in range(head + 1, heads):
            if stage[later] < 2:
                stage[later] += 1
                flying.append(step(stage[later], later))
        if head == 0:
            w_rest = lax.all_gather(after(rest_in, mixed[0][0], w_out_x), "seq", axis=0, tiled=True)
    packs = [ready[head] for head in range(heads)]

    att_x = jnp.concatenate([part[1] for part in mixed], axis=1)
    att_parts = to_heads([att_x[at * chunk : (at + 1) * chunk] for at in range(ways)])
    own_rows = fixed((chunk, width))
    middle, normed_two = run(
        functools.partial(branch_forward, heads, inner),
        "branch_forward",
        (tokens_x, gains, w_out_x, *att_parts),
        [own_rows, *whole(gains, w_out_x, *att_parts)],
        [((chunk, width), WIDE), part_low],
        [pltpu.VMEM((chunk, ways * inner), LOW)],
    )
    two_parts = over_heads(normed_two)

    blocks = 4
    cols = hidden_units // blocks
    all_three, *backs = pl.pallas_call(
        mlp_forward,
        grid=(blocks,),
        in_specs=[
            fixed(tall),
            pl.BlockSpec((width, cols), lambda step: (0, step)),
            pl.BlockSpec((width, cols), lambda step: (0, blocks + step)),
            pl.BlockSpec((width, cols), lambda step: (0, 2 * blocks + step)),
            *whole(*two_parts),
        ],
        out_specs=[pl.BlockSpec((3, row_count, cols), lambda step: (0, 0, step))] + [fixed((chunk, width))] * ways,
        out_shape=[jax.ShapeDtypeStruct((3, row_count, hidden_units), LOW)]
        + [jax.ShapeDtypeStruct((chunk, width), LOW)] * ways,
        scratch_shapes=[pltpu.VMEM(tall, LOW), pltpu.VMEM(tall, WIDE)],
        compiler_params=pltpu.CompilerParams(vmem_limit_bytes=VMEM_BYTES),
        cost_estimate=pl.CostEstimate(flops=10**10, bytes_accessed=2**24, transcendentals=2**19),
        name="mlp_forward",
    )(cot_x, w_rest, w_rest, w_rest, *two_parts)
    backs = to_heads(backs)
    grad_mlp, *mlp_parts = pl.pallas_call(
        mlp_grads,
        grid=(3 * blocks,),
        in_specs=[
            fixed(tall),
            pl.BlockSpec((1, row_count, cols), lambda step: (step // blocks, 0, step % blocks)),
            pl.BlockSpec((width, cols), lambda step: (0, jnp.maximum(step, 2 * blocks))),
            fixed((chunk, width)),
            *whole(*two_parts),
        ],
        out_specs=[pl.BlockSpec((width, cols), lambda step: (0, step))] + [fixed((chunk, width))] * ways,
        out_shape=[jax.ShapeDtypeStruct((width, 3 * hidden_units), LOW)]
        + [jax.ShapeDtypeStruct((chunk, width), LOW)] * ways,
        scratch_shapes=[pltpu.VMEM(wide_tall, LOW), pltpu.VMEM(tall, WIDE)],
        compiler_params=pltpu.CompilerParams(vmem_limit_bytes=VMEM_BYTES),
        cost_estimate=pl.CostEstimate(flops=10**10, bytes_accessed=2**24, transcendentals=0),
        name="mlp_grads",
    )(cot_x, all_three, w_rest, middle, *two_parts)
    grad_mlp, mlp_parts, backs = lax.optimization_barrier((grad_mlp, mlp_parts, backs))
    reduced_mlp = lax.psum_scatter(grad_mlp, "seq", scatter_dimension=0, tiled=True)

    d_middle, d_branch, gain_two_sum, *d_atts = run(
        functools.partial(branch_backward, heads, inner),
        "branch_backward",
        (middle, gains, cot_x, w_out_x, *backs),
        [*whole(middle, gains), own_rows, *whole(w_out_x, *backs)],
        [((chunk, width), WIDE), part_low, ((8, width), WIDE)] + [((chunk, inner), LOW)] * ways,
    )
    d_atts = to_heads(d_atts)

    def add(left, right):
        return (left.astype(WIDE) + right.astype(WIDE)).astype(LOW)

    second, sums, mlp_terms = [], {}, [mlp_parts[0]]
    core, across = {}, {}
    for head in range(heads):
        kept = first[head]
        held = kept[2] if head == 0 else after(kept[2], second[-1][0])
        flying = [move for move in (core.get(head - 1), across.get(head - 2)) if move is not None]
        if head + 1 < ways:
            flying.append(xor_move(mlp_parts[head + 1], "head", head + 1))
        outs = run_cross_backward(
            places, held, kept[3], mixed[head][0], mixed[head][2], doc_col, docs, packs[head], d_atts, head, head % 2 == 1
        )
        (even, odd, *rest), flying = lax.optimization_barrier((outs, flying))
        second.append(rest)
        if head + 1 < ways:
            mlp_terms.append(flying.pop())
        if head >= 2:
            half = add(sums[head - 2][:2], flying.pop())
            sums[head - 2] = [half[0], half[1]]
        if head >= 1:
            sums[head - 1] = add(sums[head - 1], flying.pop())
            across[head - 1] = xor_move(sums[head - 1][2:], "seq", orders[head - 1][1])
        sums[head] = even
        core[head] = xor_move(odd, "seq", 1)
    mlp_terms += [xor_move(mlp_parts[at], "head", at) for at in range(heads + 1, ways)]
    result_own = total(mlp_terms).astype(LOW)
    d_branch_all = lax.all_gather(after(d_branch, reduced_mlp), "head", axis=0, tiled=True)

    cols = 4 * dim
    grad_in = None

    def grads_into(kernel, ins, specs, at, grid, name, scratch=()):
        given = () if grad_in is None else (grad_in,)
        return pl.pallas_call(
            kernel,
            grid=(grid,),
            in_specs=specs + [ANYWHERE] * len(given),
            out_specs=at,
            out_shape=jax.ShapeDtypeStruct((width, (heads + 1) * cols), LOW),
            input_output_aliases={len(ins): 0} if given else {},
            scratch_shapes=list(scratch),
            compiler_params=pltpu.CompilerParams(vmem_limit_bytes=VMEM_BYTES),
            cost_estimate=pl.CostEstimate(flops=10**9, bytes_accessed=2**22, transcendentals=0),
            name=name,
        )(*ins, *given)

    d_projs, d_betas, result_parts = [], [], [result_own]
    back_part = None
    for head in range(heads):
        if isinstance(sums[head], list):
            near_sum, far_sum = sums[head]
        else:
            half = add(sums[head][:2], across[head])
            near_sum, far_sum = half[0], half[1]
        sent = [near_sum, xor_move(far_sum, "seq", orders[head][0])]
        if head >= 1:
            grad_in = grads_into(
                weight_grads,
                (normed_x_t, d_projs[-1]),
                whole(normed_x_t, d_projs[-1]),
                column_at((width, cols), head - 1),
                1,
                "weight_grads",
            )
            ins = (d_projs[-1], w_in) + (() if back_part is None else (back_part,))
            (back_part,) = run(
                project_more,
                "project_more",
                ins,
                [*whole(d_projs[-1]), column_at((width, cols), head - 1), *whole(*ins[2:])],
                [(tall, WIDE)],
            )
            grad_in, back_part, sent = lax.optimization_barrier((grad_in, back_part, sent))
        flying = []
        if head + 1 < ways:
            flying.append(xor_move(result_own, "head", head + 1))
        if head + 1 in across:
            flying.append(across[head + 1])
        late = heads - 1 if head == 0 and heads - 1 not in across else None
        if late:
            flying.append(core[late])
        proj, inverse, carried, qdir, solve = (first[head][at] for at in (0, 4, 5, 6, 7))
        outs = run_block_backward(
            places, proj, beta_raw, (inverse, carried, qdir, solve, *second[head]), sent, head, dim
        )
        (d_proj, d_beta), flying = lax.optimization_barrier((outs, flying))
        if late:
            sums[late] = add(sums[late], flying.pop())
            across[late] = xor_move(sums[late][2:], "seq", orders[late][1])
        if head + 1 in across and head + 1 != late:
            across[head + 1] = flying.pop()
        if head + 1 < ways:
            result_parts.append(flying.pop())
        d_projs.append(d_proj)
        d_betas.append(d_beta)
    result_parts += [xor_move(result_own, "head", at) for at in range(heads + 1, ways)]
    atts = [part[1] for part in mixed]
    grad_in = grads_into(
        functools.partial(out_grads, heads),
        (places, d_branch_all, *atts),
        [SCALARS, *whole(d_branch_all, *atts)],
        pl.BlockSpec((width, 128), lambda step: (0, heads * cols // 128 + 1 + step)),
        heads,
        "out_grads",
        [pltpu.VMEM(wide_tall, LOW)],
    )
    back_ins = (tokens_x, w_in, back_part, d_projs[-1], *d_betas)
    gain_one_sum, d_beta, *backs = run(
        functools.partial(project_back, heads),
        "project_back",
        back_ins,
        whole(*back_ins),
        [((8, width), WIDE), ((row_count, 128), LOW)] + [part_low] * ways,
    )
    backs = to_heads(backs)
    (d_tokens_own,) = run(
        functools.partial(token_grad, heads),
        "token_grad",
        (tokens_x, gains, d_middle, *backs),
        [own_rows, *whole(gains, d_middle, *backs)],
        [part_low],
    )
    token_parts = over_heads(d_tokens_own)
    (result,) = run(
        token_join, "result_join", (places, *result_parts), [SCALARS, *whole(*result_parts)], [(tall, LOW)]
    )
    (d_tokens,) = run(
        token_join, "token_join", (places, *token_parts), [SCALARS, *whole(*token_parts)], [(tall, WIDE)]
    )

    grad_in = grads_into(
        weight_grads,
        (normed_x_t, d_projs[-1]),
        whole(normed_x_t, d_projs[-1]),
        column_at((width, cols), heads - 1),
        1,
        "weight_grads",
    )
    ins = (normed_x_t, d_beta, gain_one_sum, gain_two_sum)
    grad_in = grads_into(
        functools.partial(small_grads, heads),
        ins,
        whole(*ins),
        column_at((width, 128), heads * cols // 128),
        1,
        "small_grads",
        [pltpu.VMEM((128, width), WIDE)],
    )
    reduced_in = lax.psum_scatter(grad_in, "seq", scatter_dimension=0, tiled=True)
    *grads, small_sum, grad_out_t = run(
        functools.partial(grad_join, heads, dim),
        "grad_join",
        (reduced_in,),
        whole(reduced_in),
        [((shard, inner), WIDE)] * 4 + [((shard, 128), WIDE), ((shard, inner), WIDE)],
    )
    gain_sums = total(over_heads(small_sum))
    reduced_mlp = reduced_mlp.astype(WIDE)
    return (
        result,
        d_tokens,
        gain_sums[:, heads],
        *grads,
        small_sum[:, :heads],
        grad_out_t.T,
        gain_sums[:, heads + 1],
        reduced_mlp[:, :hidden_units],
        reduced_mlp[:, hidden_units : 2 * hidden_units],
        reduced_mlp[:, 2 * hidden_units :].T,
    )


def solution(mesh):
    placed = (
        P("seq", None),
        P("seq", None),
        P("seq"),
        P("seq"),
        P("seq", "head"),
        P("seq", "head"),
        P("seq", "head"),
        P("seq", "head"),
        P("seq", "head"),
        P("head", "seq"),
        P("seq"),
        P("seq", "head"),
        P("seq", "head"),
        P("head", "seq"),
    )
    return jax.shard_map(
        per_device,
        mesh=mesh,
        in_specs=placed,
        out_specs=(
            P("seq", None),
            P("seq", None),
            P("seq"),
            P("seq", "head"),
            P("seq", "head"),
            P("seq", "head"),
            P("seq", "head"),
            P("seq", "head"),
            P("head", "seq"),
            P("seq"),
            P("seq", "head"),
            P("seq", "head"),
            P("head", "seq"),
        ),
        check_vma=False,
    )
```

```python
import functools

import jax
import jax.numpy as jnp
from jax import lax
from jax.experimental import pallas as pl
from jax.experimental.pallas import tpu as pltpu
from jax.sharding import PartitionSpec as P

SPAN = 8
EPSILON = 1e-06
NEGATIVE = -1e30
LOG2E = 1.4426950408889634
LOW = jnp.bfloat16
WIDE = jnp.float32
VMEM_BYTES = 60 * 2**20


def mm(left, right, ta=False, tb=False):
    dims = (((0 if ta else 1,), (1 if tb else 0,)), ((), ()))
    return lax.dot_general(
        left.astype(LOW), right.astype(LOW), dims, preferred_element_type=WIDE
    )


def halves(value):
    high = value.astype(LOW)
    return high, (value - high.astype(WIDE)).astype(LOW)


def mm3(left, right, ta=False, tb=False):
    left_hi, left_lo = left if isinstance(left, tuple) else halves(left)
    right_hi, right_lo = right if isinstance(right, tuple) else halves(right)
    return mm(left_hi, right_hi, ta, tb) + (mm(left_hi, right_lo, ta, tb) + mm(left_lo, right_hi, ta, tb))


def iota(shape, axis):
    return lax.broadcasted_iota(jnp.int32, shape, axis)


def lower_inverse(strict, beta):
    length = strict.shape[0]
    size = 128
    row, col = iota((size, size), 0), iota((size, size), 1)
    subs, blocks = [], []
    for at in range(0, length, size):
        sub = strict[at : at + size, at : at + size]
        scale = beta[at : at + size]
        diag = jnp.where(row == col, scale, 0.0)
        across = jnp.sum(diag, axis=0, keepdims=True)
        pair = ((row >> 1) == (col >> 1)) & (row > col)
        subs.append(sub)
        blocks.append(diag - jnp.where(pair, sub * scale * across, 0.0))
    bit = 1
    while (1 << bit) < size:
        mask = ((row >> (bit + 1)) == (col >> (bit + 1))) & ((row >> bit) != (col >> bit)) & (row > col)
        right = [mm3(jnp.where(mask, sub, 0.0), block) for sub, block in zip(subs, blocks)]
        blocks = [block - mm3(block, part) for block, part in zip(blocks, right)]
        bit += 1
    while len(blocks) > 1:
        size = blocks[0].shape[0]
        joined = []
        for pair_at in range(len(blocks) // 2):
            first, second = blocks[2 * pair_at], blocks[2 * pair_at + 1]
            at = 2 * pair_at * size
            corner = -mm3(second, mm3(strict[at + size : at + 2 * size, at : at + size], first))
            joined.append(
                jnp.concatenate(
                    [
                        jnp.concatenate([first, jnp.zeros_like(first)], axis=1),
                        jnp.concatenate([corner, second], axis=1),
                    ],
                    axis=0,
                )
            )
        blocks = joined
    return blocks[0]


def xor_move(value, axis, mask):
    return lax.ppermute(value, axis, [(at, at ^ mask) for at in range(lax.axis_size(axis))])


def after(value, *others):
    return lax.optimization_barrier((value, *others))[0]


def doubled_again(held, mask):
    return jnp.concatenate([held, xor_move(held, "seq", mask)], axis=0)


def doubled(block, masks):
    held = block[None]
    for mask in masks:
        held = doubled_again(held, mask)
    return held


def block_forward(
    head, place_ref, normed_ref, w_ref, beta_ref, doc_col_ref, doc_row_ref,
    proj_ref, pack_ref, qm_ref, score_ref, inv_ref, carried_ref, qdir_ref, solve_ref, stat_ref, acc_ref,
):
    proj_ref[...] = mm(normed_ref[...], w_ref[...])
    length, dim = qm_ref.shape
    query, key = proj_ref[:, 0:dim], proj_ref[:, dim : 2 * dim]
    value, dirs = proj_ref[:, 2 * dim : 3 * dim].astype(LOW), proj_ref[:, 3 * dim :]
    beta = 2.0 * jax.nn.sigmoid(beta_ref[:, head : head + 1])
    unit = dirs * lax.rsqrt(jnp.sum(dirs * dirs, axis=-1, keepdims=True) + EPSILON)
    row, col = iota((length, length), 0), iota((length, length), 1)
    unit_two = halves(unit)
    strict = jnp.where(row > col, mm3(unit_two, unit_two, tb=True), 0.0)
    inverse = lower_inverse(strict, beta)
    inverse_two = halves(inverse)
    solve = mm3(inverse_two, unit_two)
    solve_two = halves(solve)
    dir_key = jnp.where(row > col, mm3(unit_two, key, tb=True), 0.0)
    carried = mm3(inverse_two, dir_key)
    carried_two = halves(carried)
    qdir = jnp.where(row >= col, mm3(query, unit_two, tb=True), 0.0)
    qdir_two = halves(qdir)
    qm_ref[...] = query - mm3(qdir_two, solve_two)
    pack_ref[0:length, :] = (key - mm3(carried_two, unit_two, ta=True)).astype(LOW)
    pack_ref[length : 2 * length, :] = value
    eye = jnp.where(iota((dim, dim), 0) == iota((dim, dim), 1), 1.0, 0.0)
    pack_ref[2 * length :, :] = (eye - mm3(unit_two, solve_two, ta=True)).astype(LOW)
    inside = mm(query, key, tb=True) - mm(qdir_two[0], carried_two[0])
    inv_ref[...] = inverse.astype(LOW)
    carried_ref[...] = carried_two[0]
    qdir_ref[...] = qdir_two[0]
    solve_ref[...] = solve_two[0]
    allowed = (doc_col_ref[:, 0:1] == doc_row_ref[pl.ds(place_ref[0], 1), :]) & (row >= col)
    score = jnp.where(allowed, inside * (LOG2E * dim**-0.5), NEGATIVE)
    score_ref[...] = score
    peak = jnp.max(score, axis=1, keepdims=True)
    weight = jnp.exp2(score - peak)
    lane = iota((length, 128), 1)
    stat_ref[...] = jnp.where(lane == 0, peak, jnp.sum(weight, axis=1, keepdims=True))
    acc_ref[...] = mm(weight, value)


def bring(halves_in, pack_ref, sems):
    size = halves_in[0].shape[0]
    copies = [
        pltpu.make_async_copy(part, pack_ref.at[pl.ds(at * size, size)], sems.at[at]) for at, part in enumerate(halves_in)
    ]
    for copy in copies:
        copy.start()
    for copy in copies:
        copy.wait()


def slot_of(mask, swapped):
    core, first, second = mask & 1, (mask >> 1) & 1, mask >> 2
    return 4 * core + (2 * first + second if swapped else first + 2 * second)


def cross_forward(
    swapped, place_ref, qm_ref, stat_in_ref, acc_ref, doc_col_ref, doc_row_ref, far_ref, core_ref,
    att_ref, att_x_ref, log_ref, pack_ref, moved_ref, score_ref, peak_ref, sems,
):
    bring((far_ref, core_ref), pack_ref, sems)
    length, dim = qm_ref.shape
    place = place_ref[0]
    moved_ref[...] = qm_ref[...]
    att_ref[...] = acc_ref[...]
    own_peak = stat_in_ref[:, 0:1]
    peak_ref[...] = jnp.broadcast_to(own_peak, (length, 128))

    def look(step, carry):
        at = place - step
        slot = slot_of(place ^ at, swapped)
        moved = moved_ref[...]
        score = mm(moved * (LOG2E * dim**-0.5), pack_ref[slot, 0:length, :], tb=True)
        moved_ref[...] = mm(moved, pack_ref[slot, 2 * length :, :])
        allowed = doc_col_ref[:, 0:1] == doc_row_ref[pl.ds(at, 1), :]
        score = jnp.where(allowed, score, NEGATIVE)
        score_ref[at] = score
        high = peak_ref[...]
        for lane in range(0, length, 128):
            high = jnp.maximum(high, score[:, lane : lane + 128])
        peak_ref[...] = high
        return carry

    def two_looks(pair, carry):
        look(2 * pair + 1, carry)
        return look(2 * pair + 2, carry)

    lax.fori_loop(0, place // 2, two_looks, 0)
    lax.fori_loop(place // 2 * 2 + 1, place + 1, look, 0)
    peak = jnp.max(peak_ref[...], axis=1, keepdims=True)
    rescale = jnp.exp2(own_peak - peak)
    att_ref[...] = att_ref[...] * rescale
    lanes = iota((length, 128), 1)
    moved_ref[...] = jnp.where(lanes == 0, stat_in_ref[:, 1:2] * rescale, 0.0)

    def use(at, carry):
        slot = slot_of(place ^ at, swapped)
        weight = jnp.exp2(score_ref[at] - peak)
        sums = moved_ref[...]
        for lane in range(0, length, 128):
            sums = sums + weight[:, lane : lane + 128]
        moved_ref[...] = sums
        att_ref[...] += mm(weight, pack_ref[slot, length : 2 * length, :])
        return carry

    def two_uses(pair, carry):
        use(2 * pair, carry)
        return use(2 * pair + 1, carry)

    lax.fori_loop(0, place // 2, two_uses, 0)
    lax.fori_loop(place // 2 * 2, place, use, 0)
    total = jnp.sum(moved_ref[...], axis=1, keepdims=True)
    attention = att_ref[...] / total
    att_ref[...] = attention
    scatter_rows(att_x_ref, slice(None), attention.astype(LOW), place_ref[1])
    log_ref[...] = jnp.broadcast_to(peak + jnp.log2(total), (length, 128))


def same_document(doc_row_ref, at, place):
    first = doc_row_ref[pl.ds(at, 1), :][:, 0:1]
    last = doc_row_ref[pl.ds(place, 1), :][:, doc_row_ref.shape[1] - 1 :]
    return jnp.sum(last - first) == 0.0


def scatter_rows(ref, columns, value, mask, chunk=128):
    for at in range(value.shape[0] // chunk):
        start = pl.multiple_of((mask ^ at) * chunk, chunk)
        ref[pl.ds(start, chunk), columns] = value[at * chunk : (at + 1) * chunk]


def cross_backward(swapped, place_ref, qm_ref, score_ref, att_ref, log_ref, doc_col_ref, doc_row_ref, far_ref, core_ref, *rest):
    *datts, even_ref, odd_ref, dqm_ref, dinside_ref, dval_ref = rest[:-7]
    pack_ref, sums_ref, chain_ref, dchain_ref, datt_ref, turned_ref, sems = rest[-7:]
    bring((far_ref, core_ref), pack_ref, sems)
    length, dim = qm_ref.shape
    place = place_ref[0]
    chunk = datts[0].shape[0]
    for at, part in enumerate(datts):
        start = pl.multiple_of((place_ref[1] ^ at) * chunk, chunk)
        datt_ref[pl.ds(start, chunk), :] = part[...]
    scale = dim**-0.5
    datt = datt_ref[...]
    log_total = log_ref[:, 0:1]
    delta = jnp.sum(datt.astype(WIDE) * att_ref[...], axis=1, keepdims=True)
    value = pack_ref[0, length : 2 * length, :]
    probs = jnp.exp2(score_ref[...] - log_total)
    dprob = mm(datt, value, tb=True)
    dinside_ref[...] = (probs * (dprob - delta) * scale).astype(LOW)
    dval_ref[...] = mm(probs, datt, ta=True)
    chain_ref[1] = qm_ref[...]

    def put(slot, rows, part):
        sums_ref[slot, rows, :] = part.astype(LOW)

    def blank(at, carry):
        put(slot_of(place ^ at, swapped), slice(None), jnp.zeros(sums_ref.shape[1:], LOW))
        return carry

    lax.fori_loop(place, SPAN, blank, 0)

    def hop(step, carry):
        at = place - step
        slot = slot_of(place ^ at, swapped)
        moved = chain_ref[step]
        key = pack_ref[slot, 0:length, :]
        value = pack_ref[slot, length : 2 * length, :]
        through = pack_ref[slot, 2 * length :, :]
        chain_ref[step + 1] = mm(moved, through)
        allowed = doc_col_ref[:, 0:1] == doc_row_ref[pl.ds(at, 1), :]
        probs = jnp.exp2(jnp.where(allowed, mm(moved * (LOG2E * scale), key, tb=True), NEGATIVE) - log_total)
        dscore = (probs * (mm(datt, value, tb=True) - delta)).astype(LOW)
        dchain_ref[step] = mm(dscore, key) * scale
        put(slot, slice(0, length), mm(dscore, moved * scale, ta=True))
        put(slot, slice(length, 2 * length), mm(probs, datt, ta=True))
        return carry

    def two_hops(pair, carry):
        hop(2 * pair + 1, carry)
        return hop(2 * pair + 2, carry)

    lax.fori_loop(0, place // 2, two_hops, 0)
    lax.fori_loop(place // 2 * 2 + 1, place + 1, hop, 0)

    def back(count, carry):
        step = place - count
        slot = slot_of(place ^ (place - step), swapped)
        through = pack_ref[slot, 2 * length :, :]
        grad = dqm_ref[...]
        put(slot, slice(2 * length, 2 * length + dim), mm(chain_ref[step], grad, ta=True))
        dqm_ref[...] = dchain_ref[step] + mm(grad, through, tb=True)
        return carry

    dqm_ref[...] = jnp.zeros((length, dim), WIDE)
    lax.fori_loop(0, place, back, 0)
    even_ref[...] = sums_ref[: SPAN // 2]
    odd_ref[...] = sums_ref[SPAN // 2 :]


def block_backward(
    head, place_ref, proj_ref, beta_ref, inv_ref, carried_ref, qdir_ref, solve_ref, dqm_ref, dinside_ref, dval_ref, *rest
):
    *dpacks, dproj_ref, dbeta_ref = rest
    length, dim = dqm_ref.shape
    query, key, dirs = proj_ref[:, 0:dim], proj_ref[:, dim : 2 * dim], proj_ref[:, 3 * dim :]
    beta = 2.0 * jax.nn.sigmoid(beta_ref[:, head : head + 1])
    norm = lax.rsqrt(jnp.sum(dirs * dirs, axis=-1, keepdims=True) + EPSILON)
    unit = dirs * norm
    low_unit, low_key, low_query = unit.astype(LOW), key.astype(LOW), query.astype(LOW)
    row, col = iota((length, length), 0), iota((length, length), 1)
    inverse, carried, qdir, solve = inv_ref[...], carried_ref[...], qdir_ref[...], solve_ref[...]
    dqm, dinside = dqm_ref[...].astype(LOW), dinside_ref[...]

    def summed(rows):
        return sum(part[rows, :].astype(WIDE) for part in dpacks)

    dkm = summed(slice(0, length))
    dthrough = summed(slice(2 * length, 2 * length + dim)).astype(LOW)
    dvalue = dval_ref[...] + summed(slice(length, 2 * length))
    dkm_low = dkm.astype(LOW)
    dqdir = -jnp.where(row >= col, mm(dqm, solve, tb=True) + mm(dinside, carried, tb=True), 0.0).astype(LOW)
    dquery = dqm_ref[...] + mm(dinside, low_key) + mm(dqdir, low_unit)
    dsolve = -(mm(qdir, dqm, ta=True) + mm(low_unit, dthrough))
    dcarried = -(mm(low_unit, dkm_low, tb=True) + mm(qdir, dinside, ta=True))
    ysolve = mm(inverse, dsolve, ta=True)
    ycarried = mm(inverse, dcarried, ta=True)
    ddir_key = jnp.where(row > col, ycarried, 0.0).astype(LOW)
    dlower = -(mm(ysolve, solve, tb=True) + mm(ycarried, carried, tb=True))
    ddiag = jnp.sum(jnp.where(row == col, dlower, 0.0), axis=1, keepdims=True)
    dgram = jnp.where(row > col, dlower, 0.0).astype(LOW)
    dkey = dkm + mm(dinside, low_query, ta=True) + mm(ddir_key, low_unit, ta=True)
    dunit = (
        ysolve
        - mm(solve, dthrough, tb=True)
        - mm(carried, dkm_low)
        + mm(dqdir, low_query, ta=True)
        + mm(ddir_key, low_key)
        + mm(dgram, low_unit)
        + mm(dgram, low_unit, ta=True)
    )
    along = jnp.sum(dunit * dirs, axis=1, keepdims=True)
    ddirs = norm * dunit - dirs * (norm * norm * norm * along)
    dbeta = -ddiag / jnp.maximum(beta, 1e-30) * (1.0 - 0.5 * beta)
    lane = iota((length, 128), 1)
    mask = place_ref[1]
    for at, part in enumerate((dquery, dkey, dvalue, ddirs)):
        scatter_rows(dproj_ref, slice(at * dim, (at + 1) * dim), part.astype(LOW), mask)
    scatter_rows(dbeta_ref, slice(None), jnp.where(lane == head, dbeta, 0.0).astype(LOW), mask)


def pack_heads(heads, *refs):
    *parts, out_ref = refs
    dim = parts[0].shape[1] // heads
    for head in range(heads):
        for at, part in enumerate(parts):
            start = (head * len(parts) + at) * dim
            out_ref[:, start : start + dim] = part[:, head * dim : (head + 1) * dim]


def prepare(heads, shard, masks, place_ref, tokens_ref, cot_ref, parts_ref, *rest):
    normed_ref, normed_t_ref, tokens_x_ref, cot_x_ref, small_ref, gains_ref, beta_ref, docs_ref, doc_col_ref = rest[:9]
    marks_ref, sems, mark_sems = rest[9:]
    span = marks_ref.shape[0]
    copies = []
    for slot in range(parts_ref.shape[0]):
        mask = sum(part for at, part in enumerate(masks) if slot >> at & 1)
        at = pl.multiple_of((place_ref[2] ^ mask) * shard, 16)
        copies.append(
            pltpu.make_async_copy(parts_ref.at[slot, pl.ds(0, shard), :], small_ref.at[pl.ds(at, shard), :], sems.at[slot])
        )
        if mask < span:
            copies.append(
                pltpu.make_async_copy(
                    parts_ref.at[slot, pl.ds(shard, 16), :], marks_ref.at[place_ref[0] ^ mask], mark_sems.at[mask]
                )
            )
    for copy in copies:
        copy.start()
    for copy in copies:
        copy.wait()
    small = small_ref[...]
    across = small.astype(WIDE).T
    gains_ref[...] = across[0:8]
    gain = across[heads : heads + 1]
    stream = tokens_ref[...].astype(WIDE)
    scale = lax.rsqrt(jnp.mean(stream * stream, axis=-1, keepdims=True) + EPSILON)
    normed_wide = stream * scale * gain
    normed = normed_wide.astype(LOW)
    normed_ref[...] = normed
    beta_ref[...] = mm(normed, small)
    mask = place_ref[1]
    scatter_rows(tokens_x_ref, slice(None), tokens_ref[...], mask)
    scatter_rows(cot_x_ref, slice(None), cot_ref[...], mask)
    for at in range(normed.shape[0] // 128):
        start = pl.multiple_of((mask ^ at) * 128, 128)
        normed_t_ref[:, pl.ds(start, 128)] = normed_wide[at * 128 : (at + 1) * 128].T.astype(LOW)
    all_marks = marks_ref[...].astype(WIDE)
    line = iota(all_marks.shape, 1)
    length = tokens_ref.shape[0]
    marks = jnp.concatenate(
        [jnp.sum(jnp.where(line == at, all_marks, 0.0), axis=1) for at in range(length // 128)], axis=1
    )
    upper = jnp.where(iota((length, length), 0) <= iota((length, length), 1), 1.0, 0.0)
    docs = mm(marks, upper)
    row = iota(docs.shape, 0)
    before = jnp.zeros_like(docs)
    for at in range(span - 1):
        before = before + jnp.where(row > at, docs[at : at + 1, length - 1 : length], 0.0)
    docs = docs + before
    docs_ref[...] = docs
    own = jnp.sum(jnp.where(row == place_ref[0], docs, 0.0), axis=0, keepdims=True)
    eye = iota((length, length), 0) == iota((length, length), 1)
    column = jnp.sum(jnp.where(eye, own, 0.0), axis=1, keepdims=True)
    doc_col_ref[...] = jnp.broadcast_to(column, doc_col_ref.shape)


def branch_forward(heads, dim, tokens_x_ref, gains_ref, w_out_ref, *rest):
    *pieces, middle_ref, normed_ref, att_ref = rest
    for at, part in enumerate(pieces):
        att_ref[:, at * dim : (at + 1) * dim] = part[...]
    middle = tokens_x_ref[...].astype(WIDE) + mm(att_ref[...], w_out_ref[...], tb=True)
    middle_ref[...] = middle
    scale = lax.rsqrt(jnp.mean(middle * middle, axis=-1, keepdims=True) + EPSILON)
    normed_ref[...] = (middle * scale * gains_ref[heads + 1 : heads + 2]).astype(LOW)


def mlp_forward(cot_ref, gate_ref, up_ref, down_ref, *rest):
    ways = (len(rest) - 3) // 2
    pieces, outs = rest[:ways], rest[ways + 1 : -2]
    all_ref, normed_ref, acc_ref = rest[ways], rest[-2], rest[-1]
    step = pl.program_id(0)
    chunk = pieces[0].shape[0]

    @pl.when(step == 0)
    def start():
        for at, part in enumerate(pieces):
            normed_ref[at * chunk : (at + 1) * chunk, :] = part[...]
        acc_ref[...] = jnp.zeros_like(acc_ref)

    normed = normed_ref[...]
    gate, up, d_hidden = mm(normed, gate_ref[...]), mm(normed, up_ref[...]), mm(cot_ref[...], down_ref[...])
    sig = jax.nn.sigmoid(gate)
    silu = gate * sig
    d_gate = (d_hidden * up * sig * (1.0 + gate * (1.0 - sig))).astype(LOW)
    d_up = (d_hidden * silu).astype(LOW)
    all_ref[0] = d_gate
    all_ref[1] = d_up
    all_ref[2] = (silu * up).astype(LOW)
    acc_ref[...] += mm(d_gate, gate_ref[...], tb=True) + mm(d_up, up_ref[...], tb=True)

    @pl.when(step == pl.num_programs(0) - 1)
    def finish():
        for at, part in enumerate(outs):
            part[...] = acc_ref[at * chunk : (at + 1) * chunk, :].astype(LOW)


def mlp_grads(cot_ref, all_ref, down_ref, middle_ref, *rest):
    ways = (len(rest) - 3) // 2
    pieces, grad_ref, outs, left_ref, acc_ref = rest[:ways], rest[ways], rest[ways + 1 : -2], rest[-2], rest[-1]
    step, third = pl.program_id(0), pl.num_programs(0) // 3
    chunk = pieces[0].shape[0]

    @pl.when(step == 0)
    def start():
        for at, part in enumerate(pieces):
            left_ref[:, at * chunk : (at + 1) * chunk] = part[...].astype(WIDE).T.astype(LOW)
        acc_ref[...] = jnp.zeros_like(acc_ref)
        acc_ref[0:chunk, :] = middle_ref[...]

    @pl.when(step == 2 * third)
    def turn():
        for at in range(ways):
            part = cot_ref[at * chunk : (at + 1) * chunk, :]
            left_ref[:, at * chunk : (at + 1) * chunk] = part.astype(WIDE).T.astype(LOW)

    right = all_ref[0]
    grad_ref[...] = mm(left_ref[...], right).astype(LOW)

    @pl.when(step >= 2 * third)
    def down():
        acc_ref[...] += mm(right, down_ref[...], tb=True)

    @pl.when(step == 3 * third - 1)
    def finish():
        for at, part in enumerate(outs):
            part[...] = acc_ref[at * chunk : (at + 1) * chunk, :].astype(LOW)


def branch_backward(heads, inner, middle_ref, gains_ref, cot_ref, w_out_ref, *rest):
    ways = (len(rest) - 4) // 2
    backs, d_middle_ref, gain_ref, upper_ref, lower_ref, d_atts = rest[:ways], *rest[ways : ways + 4], rest[ways + 4 :]
    grad = total([part[...] for part in backs])
    middle = middle_ref[...]
    scale = lax.rsqrt(jnp.mean(middle * middle, axis=-1, keepdims=True) + EPSILON)
    gain_ref[...] = jnp.broadcast_to(jnp.sum(grad * middle * scale, axis=0, keepdims=True), gain_ref.shape)
    d_middle = cot_ref[...].astype(WIDE) + norm_back(grad, middle, scale, gains_ref[heads + 1 : heads + 2])
    d_middle_ref[...] = d_middle
    d_branch = d_middle.astype(LOW)
    half = upper_ref.shape[0]
    upper_ref[...] = d_branch[:half]
    lower_ref[...] = d_branch[half:]
    for at, part in enumerate(d_atts):
        part[...] = mm(d_branch, w_out_ref[:, at * inner : (at + 1) * inner]).astype(LOW)


def project_back(heads, tokens_x_ref, small_ref, w_ref, gain_two_ref, part_ref, d_proj_ref, *rest):
    d_betas, (gain_ref, d_beta_ref, *outs) = rest[:heads], rest[heads:]
    d_beta = total([part[...] for part in d_betas]).astype(LOW)
    d_beta_ref[...] = d_beta
    back = part_ref[...] + mm(d_beta, small_ref[...], tb=True) + mm(d_proj_ref[...], w_ref[...], tb=True)
    stream = tokens_x_ref[...].astype(WIDE)
    scale = lax.rsqrt(jnp.mean(stream * stream, axis=-1, keepdims=True) + EPSILON)
    gain = jnp.sum(back * stream * scale, axis=0, keepdims=True)
    gain_ref[...] = jnp.where(iota(gain_ref.shape, 0) == 0, gain, gain_two_ref[...])
    chunk = outs[0].shape[0]
    for at, part in enumerate(outs):
        part[...] = back[at * chunk : (at + 1) * chunk].astype(LOW)


def token_grad(heads, tokens_x_ref, gains_ref, d_middle_ref, *rest):
    *backs, out_ref = rest
    grad = total([part[...] for part in backs])
    stream = tokens_x_ref[...].astype(WIDE)
    scale = lax.rsqrt(jnp.mean(stream * stream, axis=-1, keepdims=True) + EPSILON)
    out_ref[...] = (d_middle_ref[...] + norm_back(grad, stream, scale, gains_ref[heads : heads + 1])).astype(LOW)


def token_join(place_ref, *rest):
    *pieces, out_ref = rest
    chunk = pieces[0].shape[0]
    for at, part in enumerate(pieces):
        start = pl.multiple_of((place_ref[1] ^ at) * chunk, chunk)
        out_ref[pl.ds(start, chunk), :] = part[...].astype(out_ref.dtype)


def weight_grads(left_ref, d_proj_ref, *rest):
    rest[-1][...] = mm(left_ref[...], d_proj_ref[...]).astype(LOW)


def out_grads(heads, ways, *rest):
    branches, atts, out_ref, turned_ref = rest[:ways], rest[ways : ways + heads], rest[-2], rest[-1]
    step = pl.program_id(0)
    chunk = 2 * branches[0].shape[0]

    @pl.when(step == 0)
    def turn():
        for at in range(ways // 2):
            part = jnp.concatenate([branches[2 * at][...], branches[2 * at + 1][...]], axis=0)
            turned_ref[:, at * chunk : (at + 1) * chunk] = part.astype(WIDE).T.astype(LOW)

    for head in range(heads):

        @pl.when(step == head)
        def one(head=head):
            out_ref[...] = mm(turned_ref[...], atts[head][...]).astype(LOW)


def small_grads(heads, ways, left_ref, d_beta_ref, *rest):
    gains, out_ref, rows_ref = rest[:ways], rest[-2], rest[-1]
    gain = total([part[...] for part in gains])
    rows_ref[...] = jnp.zeros_like(rows_ref)
    rows_ref[heads : heads + 1, :] = gain[0:1]
    rows_ref[heads + 1 : heads + 2, :] = gain[1:2]
    out_ref[...] = (mm(left_ref[...], d_beta_ref[...]) + rows_ref[...].T).astype(LOW)


def project_more(d_proj_ref, w_ref, *rest):
    part = mm(d_proj_ref[...], w_ref[...], tb=True)
    if len(rest) > 1:
        part = rest[0][...] + part
    rest[-1][...] = part


def grad_join(heads, dim, in_ref, *outs):
    width = 4 * dim
    for head in range(heads):
        for kind, out in enumerate(outs[:4]):
            at = head * width + kind * dim
            out[:, head * dim : (head + 1) * dim] = in_ref[:, at : at + dim].astype(WIDE)
    outs[4][...] = in_ref[:, heads * width : heads * width + 128].astype(WIDE)
    outs[5][...] = in_ref[:, heads * width + 128 :].astype(WIDE)


def fixed(shape):
    return pl.BlockSpec(shape, lambda *unused: (0,) * len(shape))


def column_at(shape, at):
    return pl.BlockSpec(shape, lambda *unused: (0, at))


ANYWHERE = pl.BlockSpec(memory_space=pl.ANY)
SCALARS = pl.BlockSpec(memory_space=pltpu.SMEM)


def run(kernel, name, ins, specs, outs, scratch=(), flops=10**9):
    return pl.pallas_call(
        kernel,
        grid=(1,),
        in_specs=specs,
        out_specs=[fixed(shape) for shape, unused in outs],
        out_shape=[jax.ShapeDtypeStruct(shape, dtype) for shape, dtype in outs],
        scratch_shapes=list(scratch),
        compiler_params=pltpu.CompilerParams(vmem_limit_bytes=VMEM_BYTES),
        cost_estimate=pl.CostEstimate(flops=flops, bytes_accessed=4 * 2**20, transcendentals=2**18),
        name=name,
    )(*ins)


def whole(*arrays):
    return [fixed(array.shape) for array in arrays]


def run_block_forward(places, normed, w_in, at, beta_raw, doc_col, doc_row, dim, head):
    length, width = normed.shape
    square, tall = (length, length), (length, dim)
    return run(
        functools.partial(block_forward, head),
        "block_forward",
        (places, normed, w_in, beta_raw, doc_col, doc_row),
        [SCALARS, *whole(normed), column_at((width, 4 * dim), at), *whole(beta_raw, doc_col, doc_row)],
        [
            ((length, 4 * dim), WIDE),
            ((2 * length + dim, dim), LOW),
            (tall, WIDE),
            (square, WIDE),
            (square, LOW),
            (square, LOW),
            (square, LOW),
            (tall, LOW),
            ((length, 128), WIDE),
            (tall, WIDE),
        ],
        flops=10**10,
    )


def run_cross_forward(places, q_moved, stats, acc, doc_col, docs, packs, swapped):
    length, dim = q_moved.shape
    ins = (q_moved, stats, acc, doc_col, docs)
    return run(
        functools.partial(cross_forward, swapped),
        "cross_forward",
        (places, *ins, *packs),
        [SCALARS, *whole(*ins), ANYWHERE, ANYWHERE],
        [((length, dim), WIDE), ((length, dim), LOW), ((length, dim), WIDE)],
        [
            pltpu.VMEM((SPAN,) + packs[0].shape[1:], LOW),
            pltpu.VMEM((length, dim), WIDE),
            pltpu.VMEM((SPAN - 1, length, length), WIDE),
            pltpu.VMEM((length, 128), WIDE),
            pltpu.SemaphoreType.DMA((2,)),
        ],
        flops=10**10,
    )


def run_cross_backward(places, q_moved, scores, attention, log_total, doc_col, docs, packs, d_atts, head, swapped):
    length, dim = q_moved.shape
    ins = (q_moved, scores, attention, log_total, doc_col, docs)
    both = (SPAN,) + packs[0].shape[1:]
    return run(
        functools.partial(cross_backward, swapped),
        "cross_backward",
        (places, *ins, *packs, *d_atts),
        [SCALARS, *whole(*ins), ANYWHERE, ANYWHERE] + [column_at((part.shape[0], dim), head) for part in d_atts],
        [(packs[0].shape, LOW)] * 2 + [((length, dim), WIDE), ((length, length), LOW), ((length, dim), WIDE)],
        [
            pltpu.VMEM(both, LOW),
            pltpu.VMEM(both, LOW),
            pltpu.VMEM((SPAN + 1, length, dim), WIDE),
            pltpu.VMEM((SPAN, length, dim), WIDE),
            pltpu.VMEM((length, dim), LOW),
            pltpu.VMEM((length, length), WIDE),
            pltpu.SemaphoreType.DMA((2,)),
        ],
        flops=10**10,
    )


def run_block_backward(places, proj, beta_raw, kept, d_packs, head, dim):
    length = proj.shape[0]
    ins = (proj, beta_raw, *kept, *d_packs)
    return run(
        functools.partial(block_backward, head),
        "block_backward",
        (places, *ins),
        [SCALARS, *whole(*ins)],
        [(proj.shape, LOW), ((length, 128), LOW)],
        flops=5 * 10**9,
    )


def norm_back(grad, value, scale, gain):
    weighted = grad * gain
    return scale * weighted - value * scale * scale * scale * jnp.mean(weighted * value, axis=-1, keepdims=True)


def total(parts):
    out = parts[0].astype(WIDE)
    for part in parts[1:]:
        out = out + part.astype(WIDE)
    return out


def per_device(
    tokens, cotangent, starts, gain_attn, w_query, w_key, w_value, w_dir, w_beta, w_out, gain_mlp, w_gate, w_up, w_down
):
    row_count, width = tokens.shape
    shard, inner = w_query.shape
    hidden_units = w_gate.shape[1]
    heads = w_beta.shape[1]
    dim = inner // heads
    count = lax.axis_size("seq")
    ways = lax.axis_size("head")
    chunk = row_count // ways
    seq_place, head_place = lax.axis_index("seq"), lax.axis_index("head")
    places = jnp.stack([seq_place % SPAN, head_place, seq_place]).astype(jnp.int32)

    def to_heads(parts):
        return [xor_move(part, "head", at) if at else part for at, part in enumerate(parts)]

    def over_heads(part):
        return to_heads([part] * ways)

    small = jnp.concatenate([w_beta, gain_attn[:, None], gain_mlp[:, None]], axis=1)
    small = jnp.pad(small, ((0, 0), (0, 128 - heads - 2)))
    marks = jnp.pad(starts.astype(LOW).reshape(row_count // 128, 128), ((0, 16 - row_count // 128), (0, 0)))
    masks = tuple(2 << at for at in range((count // 2).bit_length() - 1)) + (1,)
    small = doubled(jnp.concatenate([small, marks], axis=0), masks)
    four = (w_query, w_key, w_value, w_dir)
    (packed,) = run(functools.partial(pack_heads, heads), "pack_heads", four, whole(*four), [((shard, 4 * inner), LOW)])
    w_in = lax.all_gather(packed, "seq", axis=0, tiled=True)
    out_parts = jnp.concatenate(over_heads(w_out.T), axis=1)

    tall, wide_tall, part_low = (row_count, width), (width, row_count), ((chunk, width), LOW)
    normed, normed_x_t, tokens_x, cot_x, small_all, gains, beta_raw, docs, doc_col = run(
        functools.partial(prepare, heads, shard, masks),
        "prepare",
        (places, tokens, cotangent, small),
        [SCALARS, *whole(tokens, cotangent), ANYWHERE],
        [
            (tall, LOW),
            (wide_tall, LOW),
            (tall, LOW),
            (tall, LOW),
            ((width, 128), LOW),
            ((8, width), WIDE),
            ((row_count, 128), WIDE),
            ((SPAN, row_count), WIDE),
            ((row_count, 128), WIDE),
        ],
        [
            pltpu.VMEM((SPAN, 16, 128), LOW),
            pltpu.SemaphoreType.DMA((count,)),
            pltpu.SemaphoreType.DMA((SPAN,)),
        ],
    )
    normed, out_parts = lax.optimization_barrier((normed, out_parts))
    w_out_x = lax.all_gather(after(out_parts, w_in), "seq", axis=0, tiled=True)

    orders = [(4, 2) if head % 2 else (2, 4) for head in range(heads)]
    first, mixed, ready, full = [], [], {}, {}

    def step(kind, head):
        return (head, kind, xor_move(ready[head], "seq", orders[head][kind] if kind < 2 else 1))

    def meet(outs, moves):
        outs, arrived = lax.optimization_barrier((outs, [move[2] for move in moves]))
        for (head, kind, unused), part in zip(moves, arrived):
            ready[head] = (ready[head], part) if kind == 2 else jnp.concatenate([ready[head], part], axis=0)
        return outs

    flying = []
    for head in range(heads):
        held = normed if head == 0 else after(normed, first[-1][2])
        outs = run_block_forward(places, held, w_in, head, beta_raw, doc_col, docs, dim, head)
        first.append(meet(outs, flying))
        ready[head] = first[head][1][None]
        flying = [step(at, head - at) for at in range(max(0, head - 2), head + 1)]
    rest_in = jnp.concatenate([w_gate, w_up, w_down.T], axis=1)
    stage = {move[0]: move[1] for move in flying}
    for head in range(heads):
        kept = first[head]
        while stage.get(head, 2) < 2 or any(move[0] == head for move in flying):
            now = [move for move in flying if move[0] == head]
            flying = [move for move in flying if move[0] != head]
            meet((), now)
            if stage[head] < 2:
                stage[head] += 1
                flying.append(step(stage[head], head))
        if head == 0:
            held = kept[2]
        else:
            held = after(kept[2], mixed[-1][0])
        outs = run_cross_forward(places, held, kept[8], kept[9], doc_col, docs, ready[head], head % 2 == 1)
        mixed.append(meet(outs, flying))
        flying = []
        for later in range(head + 1, heads):
            if stage[later] < 2:
                stage[later] += 1
                flying.append(step(stage[later], later))
        if head == 0:
            w_rest = lax.all_gather(after(rest_in, mixed[0][0], w_out_x), "seq", axis=0, tiled=True)
    packs = [ready[head] for head in range(heads)]

    att_x = jnp.concatenate([part[1] for part in mixed], axis=1)
    att_parts = to_heads([att_x[at * chunk : (at + 1) * chunk] for at in range(ways)])
    own_rows = fixed((chunk, width))
    middle, normed_two = run(
        functools.partial(branch_forward, heads, inner),
        "branch_forward",
        (tokens_x, gains, w_out_x, *att_parts),
        [own_rows, *whole(gains, w_out_x, *att_parts)],
        [((chunk, width), WIDE), part_low],
        [pltpu.VMEM((chunk, ways * inner), LOW)],
    )
    two_parts = over_heads(normed_two)

    blocks = 2
    cols = hidden_units // blocks
    all_three, *backs = pl.pallas_call(
        mlp_forward,
        grid=(blocks,),
        in_specs=[
            fixed(tall),
            pl.BlockSpec((width, cols), lambda step: (0, step)),
            pl.BlockSpec((width, cols), lambda step: (0, blocks + step)),
            pl.BlockSpec((width, cols), lambda step: (0, 2 * blocks + step)),
            *whole(*two_parts),
        ],
        out_specs=[pl.BlockSpec((3, row_count, cols), lambda step: (0, 0, step))] + [fixed((chunk, width))] * ways,
        out_shape=[jax.ShapeDtypeStruct((3, row_count, hidden_units), LOW)]
        + [jax.ShapeDtypeStruct((chunk, width), LOW)] * ways,
        scratch_shapes=[pltpu.VMEM(tall, LOW), pltpu.VMEM(tall, WIDE)],
        compiler_params=pltpu.CompilerParams(vmem_limit_bytes=VMEM_BYTES),
        cost_estimate=pl.CostEstimate(flops=10**10, bytes_accessed=2**24, transcendentals=2**19),
        name="mlp_forward",
    )(cot_x, w_rest, w_rest, w_rest, *two_parts)
    backs = to_heads(backs)
    grad_mlp, *mlp_parts = pl.pallas_call(
        mlp_grads,
        grid=(3 * blocks,),
        in_specs=[
            fixed(tall),
            pl.BlockSpec((1, row_count, cols), lambda step: (step // blocks, 0, step % blocks)),
            pl.BlockSpec((width, cols), lambda step: (0, jnp.maximum(step, 2 * blocks))),
            fixed((chunk, width)),
            *whole(*two_parts),
        ],
        out_specs=[pl.BlockSpec((width, cols), lambda step: (0, step))] + [fixed((chunk, width))] * ways,
        out_shape=[jax.ShapeDtypeStruct((width, 3 * hidden_units), LOW)]
        + [jax.ShapeDtypeStruct((chunk, width), LOW)] * ways,
        scratch_shapes=[pltpu.VMEM(wide_tall, LOW), pltpu.VMEM(tall, WIDE)],
        compiler_params=pltpu.CompilerParams(vmem_limit_bytes=VMEM_BYTES),
        cost_estimate=pl.CostEstimate(flops=10**10, bytes_accessed=2**24, transcendentals=0),
        name="mlp_grads",
    )(cot_x, all_three, w_rest, middle, *two_parts)
    grad_mlp, mlp_parts, backs = lax.optimization_barrier((grad_mlp, mlp_parts, backs))
    reduced_mlp = lax.psum_scatter(grad_mlp, "seq", scatter_dimension=0, tiled=True)

    d_middle, gain_two_sum, upper, lower, *d_atts = run(
        functools.partial(branch_backward, heads, inner),
        "branch_backward",
        (middle, gains, cot_x, w_out_x, *backs),
        [*whole(middle, gains), own_rows, *whole(w_out_x, *backs)],
        [((chunk, width), WIDE), ((8, width), WIDE)] + [((chunk // 2, width), LOW)] * 2 + [((chunk, inner), LOW)] * ways,
    )
    d_atts = to_heads(d_atts)

    def add(left, right):
        return (left.astype(WIDE) + right.astype(WIDE)).astype(LOW)

    second, low_sums, high_sums, last_sums, branch_parts = [], {}, {}, {}, [upper, lower]
    core, across = {}, {}
    halves_two = [after(part, *d_atts[1:]) for part in (upper, lower)]
    branch_moves = [(part, at) for at in range(1, ways) for part in halves_two]
    shares = [2] + [1] * (2 * heads - 3)

    def branch_next():
        some = shares.pop(0) if shares else len(branch_moves)
        out = [xor_move(part, "head", at) for part, at in branch_moves[:some]]
        del branch_moves[:some]
        return out

    for head in range(heads):
        kept = first[head]
        held = kept[2] if head == 0 else after(kept[2], second[-1][0])
        flying = (core.get(head - 1), across.get(head - 2), branch_next())
        outs = run_cross_backward(
            places, held, kept[3], mixed[head][0], mixed[head][2], doc_col, docs, packs[head], d_atts, head, head % 2 == 1
        )
        outs, (core_in, across_in, branch_in) = lax.optimization_barrier((outs, flying))
        even, odd, *rest = outs
        second.append(rest)
        branch_parts += branch_in
        if head >= 2:
            last_sums[head - 2] = [add(low_sums[head - 2][at], across_in[at]) for at in range(2)]
        if head >= 1:
            high_sums[head - 1] = add(low_sums[head - 1][2:], core_in[2:])
            across[head - 1] = xor_move(high_sums[head - 1], "seq", orders[head - 1][1])
            low_sums[head - 1] = add(low_sums[head - 1][:2], core_in[:2])
        low_sums[head] = even
        core[head] = xor_move(odd, "seq", 1)
    mlp_rows = jnp.stack(mlp_parts)
    mlp_rows = jnp.concatenate([lax.dynamic_index_in_dim(mlp_rows, head_place ^ at, 0, False) for at in range(ways)])
    result = lax.psum(after(mlp_rows, reduced_mlp, second[-1][0]), "head")

    cols = 4 * dim
    grad_in = None

    def grads_into(kernel, ins, specs, at, grid, name, scratch=()):
        given = () if grad_in is None else (grad_in,)
        return pl.pallas_call(
            kernel,
            grid=(grid,),
            in_specs=specs + [ANYWHERE] * len(given),
            out_specs=at,
            out_shape=jax.ShapeDtypeStruct((width, (heads + 1) * cols), LOW),
            input_output_aliases={len(ins): 0} if given else {},
            scratch_shapes=list(scratch),
            compiler_params=pltpu.CompilerParams(vmem_limit_bytes=VMEM_BYTES),
            cost_estimate=pl.CostEstimate(flops=10**9, bytes_accessed=2**22, transcendentals=0),
            name=name,
        )(*ins, *given)

    d_projs, d_betas = [], []
    back_part = None
    for head in range(heads):
        if head not in last_sums:
            last_sums[head] = [add(low_sums[head][at], across[head][at]) for at in range(2)]
        near_sum, far_sum = last_sums[head]
        sent = [near_sum, xor_move(far_sum, "seq", orders[head][0])]
        if head >= 1:
            grad_in = grads_into(
                weight_grads,
                (normed_x_t, d_projs[-1]),
                whole(normed_x_t, d_projs[-1]),
                column_at((width, cols), head - 1),
                1,
                "weight_grads",
            )
            ins = (d_projs[-1], w_in) + (() if back_part is None else (back_part,))
            (back_part,) = run(
                project_more,
                "project_more",
                ins,
                [*whole(d_projs[-1]), column_at((width, cols), head - 1), *whole(*ins[2:])],
                [(tall, WIDE)],
            )
            if head == heads - 1:
                atts = [part[1] for part in mixed]
                grad_in = grads_into(
                    functools.partial(out_grads, heads, len(branch_parts)),
                    (*branch_parts, *atts),
                    whole(*branch_parts, *atts),
                    pl.BlockSpec((width, 128), lambda step: (0, heads * cols // 128 + 1 + step)),
                    heads,
                    "out_grads",
                    [pltpu.VMEM(wide_tall, LOW)],
                )
            grad_in, back_part, sent = lax.optimization_barrier((grad_in, back_part, sent))
        late = heads - 1 if head == 0 and heads - 1 not in across else None
        flying = (across.get(head + 1), core[late] if late else None, branch_next() if head + 1 < heads else [])
        proj, inverse, carried, qdir, solve = (first[head][at] for at in (0, 4, 5, 6, 7))
        if head == 0:
            proj, reduced_mlp = lax.optimization_barrier((proj, reduced_mlp))
        outs = run_block_backward(
            places, proj, beta_raw, (inverse, carried, qdir, solve, *second[head]), sent, head, dim
        )
        (d_proj, d_beta), (across_in, core_in, branch_in) = lax.optimization_barrier((outs, flying))
        branch_parts += branch_in
        if across_in is not None:
            across[head + 1] = across_in
        if late:
            across[late] = xor_move(add(low_sums[late][2:], core_in[2:]), "seq", orders[late][1])
            low_sums[late] = add(low_sums[late][:2], core_in[:2])
        d_projs.append(d_proj)
        d_betas.append(d_beta)
    back_ins = (tokens_x, small_all, w_in, gain_two_sum, back_part, d_projs[-1], *d_betas)
    gain_sums, d_beta, *backs = run(
        functools.partial(project_back, heads),
        "project_back",
        back_ins,
        [
            *whole(tokens_x, small_all),
            column_at((width, cols), heads - 1),
            *whole(*back_ins[3:]),
        ],
        [((8, width), WIDE), ((row_count, 128), LOW)] + [part_low] * ways,
    )
    backs = to_heads(backs)
    (d_tokens_own,) = run(
        functools.partial(token_grad, heads),
        "token_grad",
        (tokens_x, gains, d_middle, *backs),
        [own_rows, *whole(gains, d_middle, *backs)],
        [part_low],
    )
    token_parts = over_heads(d_tokens_own)
    grad_in = grads_into(
        weight_grads,
        (normed_x_t, d_projs[-1]),
        whole(normed_x_t, d_projs[-1]),
        column_at((width, cols), heads - 1),
        1,
        "weight_grads",
    )
    gain_parts = over_heads(gain_sums)
    ins = (normed_x_t, d_beta, *gain_parts)
    grad_in = grads_into(
        functools.partial(small_grads, heads, ways),
        ins,
        whole(*ins),
        column_at((width, 128), heads * cols // 128),
        1,
        "small_grads",
        [pltpu.VMEM((128, width), WIDE)],
    )
    grad_in, result = lax.optimization_barrier((grad_in, result))
    reduced_in = lax.psum_scatter(grad_in, "seq", scatter_dimension=0, tiled=True)
    *grads, small_sum, grad_out_t = run(
        functools.partial(grad_join, heads, dim),
        "grad_join",
        (reduced_in,),
        whole(reduced_in),
        [((shard, inner), WIDE)] * 4 + [((shard, 128), WIDE), ((shard, inner), WIDE)],
    )
    (d_tokens,) = run(
        token_join, "token_join", (places, *token_parts), [SCALARS, *whole(*token_parts)], [(tall, WIDE)]
    )
    reduced_mlp = reduced_mlp.astype(WIDE)
    return (
        result,
        d_tokens,
        small_sum[:, heads],
        *grads,
        small_sum[:, :heads],
        grad_out_t.T,
        small_sum[:, heads + 1],
        reduced_mlp[:, :hidden_units],
        reduced_mlp[:, hidden_units : 2 * hidden_units],
        reduced_mlp[:, 2 * hidden_units :].T,
    )


def solution(mesh):
    placed = (
        P("seq", None),
        P("seq", None),
        P("seq"),
        P("seq"),
        P("seq", "head"),
        P("seq", "head"),
        P("seq", "head"),
        P("seq", "head"),
        P("seq", "head"),
        P("head", "seq"),
        P("seq"),
        P("seq", "head"),
        P("seq", "head"),
        P("head", "seq"),
    )
    return jax.shard_map(
        per_device,
        mesh=mesh,
        in_specs=placed,
        out_specs=(
            P("seq", None),
            P("seq", None),
            P("seq"),
            P("seq", "head"),
            P("seq", "head"),
            P("seq", "head"),
            P("seq", "head"),
            P("seq", "head"),
            P("head", "seq"),
            P("seq"),
            P("seq", "head"),
            P("seq", "head"),
            P("head", "seq"),
        ),
        check_vma=False,
    )
```

```python
import functools

import jax
import jax.numpy as jnp
from jax import lax
from jax.experimental import pallas as pl
from jax.experimental.pallas import tpu as pltpu
from jax.sharding import PartitionSpec as P

SPAN = 8
EPSILON = 1e-06
NEGATIVE = -1e30
LOG2E = 1.4426950408889634
LOW = jnp.bfloat16
WIDE = jnp.float32
VMEM_BYTES = 60 * 2**20


def mm(left, right, ta=False, tb=False):
    dims = (((0 if ta else 1,), (1 if tb else 0,)), ((), ()))
    return lax.dot_general(
        left.astype(LOW), right.astype(LOW), dims, preferred_element_type=WIDE
    )


def halves(value):
    high = value.astype(LOW)
    return high, (value - high.astype(WIDE)).astype(LOW)


def mm3(left, right, ta=False, tb=False):
    left_hi, left_lo = left if isinstance(left, tuple) else halves(left)
    right_hi, right_lo = right if isinstance(right, tuple) else halves(right)
    return mm(left_hi, right_hi, ta, tb) + (mm(left_hi, right_lo, ta, tb) + mm(left_lo, right_hi, ta, tb))


def iota(shape, axis):
    return lax.broadcasted_iota(jnp.int32, shape, axis)


def lower_inverse(strict, beta):
    length = strict.shape[0]
    size = 128
    row, col = iota((size, size), 0), iota((size, size), 1)
    subs, blocks = [], []
    for at in range(0, length, size):
        sub = strict[at : at + size, at : at + size]
        scale = beta[at : at + size]
        diag = jnp.where(row == col, scale, 0.0)
        across = jnp.sum(diag, axis=0, keepdims=True)
        pair = ((row >> 1) == (col >> 1)) & (row > col)
        subs.append(sub)
        blocks.append(diag - jnp.where(pair, sub * scale * across, 0.0))
    bit = 1
    while (1 << bit) < size:
        mask = ((row >> (bit + 1)) == (col >> (bit + 1))) & ((row >> bit) != (col >> bit)) & (row > col)
        right = [mm3(jnp.where(mask, sub, 0.0), block) for sub, block in zip(subs, blocks)]
        blocks = [block - mm3(block, part) for block, part in zip(blocks, right)]
        bit += 1
    while len(blocks) > 1:
        size = blocks[0].shape[0]
        joined = []
        for pair_at in range(len(blocks) // 2):
            first, second = blocks[2 * pair_at], blocks[2 * pair_at + 1]
            at = 2 * pair_at * size
            corner = -mm3(second, mm3(strict[at + size : at + 2 * size, at : at + size], first))
            joined.append(
                jnp.concatenate(
                    [
                        jnp.concatenate([first, jnp.zeros_like(first)], axis=1),
                        jnp.concatenate([corner, second], axis=1),
                    ],
                    axis=0,
                )
            )
        blocks = joined
    return blocks[0]


def xor_move(value, axis, mask):
    return lax.ppermute(value, axis, [(at, at ^ mask) for at in range(lax.axis_size(axis))])


def after(value, *others):
    return lax.optimization_barrier((value, *others))[0]


def doubled_again(held, mask):
    return jnp.concatenate([held, xor_move(held, "seq", mask)], axis=0)


def doubled(block, masks):
    held = block[None]
    for mask in masks:
        held = doubled_again(held, mask)
    return held


def block_forward(
    head, place_ref, normed_ref, w_ref, beta_ref, doc_col_ref, doc_row_ref,
    proj_ref, pack_ref, qm_ref, score_ref, inv_ref, carried_ref, qdir_ref, solve_ref, stat_ref, acc_ref,
):
    proj_ref[...] = mm(normed_ref[...], w_ref[...])
    length, dim = qm_ref.shape
    query, key = proj_ref[:, 0:dim], proj_ref[:, dim : 2 * dim]
    value, dirs = proj_ref[:, 2 * dim : 3 * dim].astype(LOW), proj_ref[:, 3 * dim :]
    beta = 2.0 * jax.nn.sigmoid(beta_ref[:, head : head + 1])
    unit = dirs * lax.rsqrt(jnp.sum(dirs * dirs, axis=-1, keepdims=True) + EPSILON)
    row, col = iota((length, length), 0), iota((length, length), 1)
    unit_two = halves(unit)
    strict = jnp.where(row > col, mm3(unit_two, unit_two, tb=True), 0.0)
    inverse = lower_inverse(strict, beta)
    inverse_two = halves(inverse)
    solve = mm3(inverse_two, unit_two)
    solve_two = halves(solve)
    dir_key = jnp.where(row > col, mm3(unit_two, key, tb=True), 0.0)
    carried = mm3(inverse_two, dir_key)
    carried_two = halves(carried)
    qdir = jnp.where(row >= col, mm3(query, unit_two, tb=True), 0.0)
    qdir_two = halves(qdir)
    qm_ref[...] = query - mm3(qdir_two, solve_two)
    pack_ref[0:length, :] = (key - mm3(carried_two, unit_two, ta=True)).astype(LOW)
    pack_ref[length : 2 * length, :] = value
    eye = jnp.where(iota((dim, dim), 0) == iota((dim, dim), 1), 1.0, 0.0)
    pack_ref[2 * length :, :] = (eye - mm3(unit_two, solve_two, ta=True)).astype(LOW)
    inside = mm(query, key, tb=True) - mm(qdir_two[0], carried_two[0])
    inv_ref[...] = inverse.astype(LOW)
    carried_ref[...] = carried_two[0]
    qdir_ref[...] = qdir_two[0]
    solve_ref[...] = solve_two[0]
    allowed = (doc_col_ref[:, 0:1] == doc_row_ref[pl.ds(place_ref[0], 1), :]) & (row >= col)
    score = jnp.where(allowed, inside * (LOG2E * dim**-0.5), NEGATIVE)
    score_ref[...] = score
    peak = jnp.max(score, axis=1, keepdims=True)
    weight = jnp.exp2(score - peak)
    lane = iota((length, 128), 1)
    stat_ref[...] = jnp.where(lane == 0, peak, jnp.sum(weight, axis=1, keepdims=True))
    acc_ref[...] = mm(weight, value)


def bring(halves_in, pack_ref, sems):
    size = halves_in[0].shape[0]
    copies = [
        pltpu.make_async_copy(part, pack_ref.at[pl.ds(at * size, size)], sems.at[at]) for at, part in enumerate(halves_in)
    ]
    for copy in copies:
        copy.start()
    for copy in copies:
        copy.wait()


def slot_of(mask, swapped):
    core, first, second = mask & 1, (mask >> 1) & 1, mask >> 2
    return 4 * core + (2 * first + second if swapped else first + 2 * second)


def cross_forward(
    swapped, place_ref, qm_ref, stat_in_ref, acc_ref, doc_col_ref, doc_row_ref, far_ref, core_ref,
    att_ref, att_x_ref, log_ref, pack_ref, moved_ref, score_ref, peak_ref, sems,
):
    bring((far_ref, core_ref), pack_ref, sems)
    length, dim = qm_ref.shape
    place = place_ref[0]
    moved_ref[...] = qm_ref[...]
    att_ref[...] = acc_ref[...]
    own_peak = stat_in_ref[:, 0:1]
    peak_ref[...] = jnp.broadcast_to(own_peak, (length, 128))

    def look(step, carry):
        at = place - step
        slot = slot_of(place ^ at, swapped)
        moved = moved_ref[...]
        score = mm(moved * (LOG2E * dim**-0.5), pack_ref[slot, 0:length, :], tb=True)
        moved_ref[...] = mm(moved, pack_ref[slot, 2 * length :, :])
        allowed = doc_col_ref[:, 0:1] == doc_row_ref[pl.ds(at, 1), :]
        score = jnp.where(allowed, score, NEGATIVE)
        score_ref[at] = score
        high = peak_ref[...]
        for lane in range(0, length, 128):
            high = jnp.maximum(high, score[:, lane : lane + 128])
        peak_ref[...] = high
        return carry

    def two_looks(pair, carry):
        look(2 * pair + 1, carry)
        return look(2 * pair + 2, carry)

    lax.fori_loop(0, place // 2, two_looks, 0)
    lax.fori_loop(place // 2 * 2 + 1, place + 1, look, 0)
    peak = jnp.max(peak_ref[...], axis=1, keepdims=True)
    rescale = jnp.exp2(own_peak - peak)
    att_ref[...] = att_ref[...] * rescale
    lanes = iota((length, 128), 1)
    moved_ref[...] = jnp.where(lanes == 0, stat_in_ref[:, 1:2] * rescale, 0.0)

    def use(at, carry):
        slot = slot_of(place ^ at, swapped)
        weight = jnp.exp2(score_ref[at] - peak)
        sums = moved_ref[...]
        for lane in range(0, length, 128):
            sums = sums + weight[:, lane : lane + 128]
        moved_ref[...] = sums
        att_ref[...] += mm(weight, pack_ref[slot, length : 2 * length, :])
        return carry

    def two_uses(pair, carry):
        use(2 * pair, carry)
        return use(2 * pair + 1, carry)

    lax.fori_loop(0, place // 2, two_uses, 0)
    lax.fori_loop(place // 2 * 2, place, use, 0)
    total = jnp.sum(moved_ref[...], axis=1, keepdims=True)
    attention = att_ref[...] / total
    att_ref[...] = attention
    scatter_rows(att_x_ref, slice(None), attention.astype(LOW), place_ref[1])
    log_ref[...] = jnp.broadcast_to(peak + jnp.log2(total), (length, 128))


def same_document(doc_row_ref, at, place):
    first = doc_row_ref[pl.ds(at, 1), :][:, 0:1]
    last = doc_row_ref[pl.ds(place, 1), :][:, doc_row_ref.shape[1] - 1 :]
    return jnp.sum(last - first) == 0.0


def scatter_rows(ref, columns, value, mask, chunk=128):
    for at in range(value.shape[0] // chunk):
        start = pl.multiple_of((mask ^ at) * chunk, chunk)
        ref[pl.ds(start, chunk), columns] = value[at * chunk : (at + 1) * chunk]


def cross_backward(swapped, place_ref, qm_ref, score_ref, att_ref, log_ref, doc_col_ref, doc_row_ref, far_ref, core_ref, *rest):
    *datts, even_ref, odd_ref, dqm_ref, dinside_ref, dval_ref = rest[:-7]
    pack_ref, sums_ref, chain_ref, dchain_ref, datt_ref, turned_ref, sems = rest[-7:]
    bring((far_ref, core_ref), pack_ref, sems)
    length, dim = qm_ref.shape
    place = place_ref[0]
    chunk = datts[0].shape[0]
    for at, part in enumerate(datts):
        start = pl.multiple_of((place_ref[1] ^ at) * chunk, chunk)
        datt_ref[pl.ds(start, chunk), :] = part[...]
    scale = dim**-0.5
    datt = datt_ref[...]
    log_total = log_ref[:, 0:1]
    delta = jnp.sum(datt.astype(WIDE) * att_ref[...], axis=1, keepdims=True)
    value = pack_ref[0, length : 2 * length, :]
    probs = jnp.exp2(score_ref[...] - log_total)
    dprob = mm(datt, value, tb=True)
    dinside_ref[...] = (probs * (dprob - delta) * scale).astype(LOW)
    dval_ref[...] = mm(probs, datt, ta=True)
    chain_ref[1] = qm_ref[...]

    def put(slot, rows, part):
        sums_ref[slot, rows, :] = part.astype(LOW)

    def blank(at, carry):
        put(slot_of(place ^ at, swapped), slice(None), jnp.zeros(sums_ref.shape[1:], LOW))
        return carry

    lax.fori_loop(place, SPAN, blank, 0)

    def hop(step, carry):
        at = place - step
        slot = slot_of(place ^ at, swapped)
        moved = chain_ref[step]
        key = pack_ref[slot, 0:length, :]
        value = pack_ref[slot, length : 2 * length, :]
        through = pack_ref[slot, 2 * length :, :]
        chain_ref[step + 1] = mm(moved, through)
        allowed = doc_col_ref[:, 0:1] == doc_row_ref[pl.ds(at, 1), :]
        probs = jnp.exp2(jnp.where(allowed, mm(moved * (LOG2E * scale), key, tb=True), NEGATIVE) - log_total)
        dscore = (probs * (mm(datt, value, tb=True) - delta)).astype(LOW)
        dchain_ref[step] = mm(dscore, key) * scale
        put(slot, slice(0, length), mm(dscore, moved * scale, ta=True))
        put(slot, slice(length, 2 * length), mm(probs, datt, ta=True))
        return carry

    def two_hops(pair, carry):
        hop(2 * pair + 1, carry)
        return hop(2 * pair + 2, carry)

    lax.fori_loop(0, place // 2, two_hops, 0)
    lax.fori_loop(place // 2 * 2 + 1, place + 1, hop, 0)

    def back(count, carry):
        step = place - count
        slot = slot_of(place ^ (place - step), swapped)
        through = pack_ref[slot, 2 * length :, :]
        grad = dqm_ref[...]
        put(slot, slice(2 * length, 2 * length + dim), mm(chain_ref[step], grad, ta=True))
        dqm_ref[...] = dchain_ref[step] + mm(grad, through, tb=True)
        return carry

    dqm_ref[...] = jnp.zeros((length, dim), WIDE)
    lax.fori_loop(0, place, back, 0)
    even_ref[...] = sums_ref[: SPAN // 2]
    odd_ref[...] = sums_ref[SPAN // 2 :]


def block_backward(
    head, place_ref, proj_ref, beta_ref, inv_ref, carried_ref, qdir_ref, solve_ref, dqm_ref, dinside_ref, dval_ref, *rest
):
    *dpacks, dproj_ref, dbeta_ref = rest
    length, dim = dqm_ref.shape
    query, key, dirs = proj_ref[:, 0:dim], proj_ref[:, dim : 2 * dim], proj_ref[:, 3 * dim :]
    beta = 2.0 * jax.nn.sigmoid(beta_ref[:, head : head + 1])
    norm = lax.rsqrt(jnp.sum(dirs * dirs, axis=-1, keepdims=True) + EPSILON)
    unit = dirs * norm
    low_unit, low_key, low_query = unit.astype(LOW), key.astype(LOW), query.astype(LOW)
    row, col = iota((length, length), 0), iota((length, length), 1)
    inverse, carried, qdir, solve = inv_ref[...], carried_ref[...], qdir_ref[...], solve_ref[...]
    dqm, dinside = dqm_ref[...].astype(LOW), dinside_ref[...]

    def summed(rows):
        return sum(part[rows, :].astype(WIDE) for part in dpacks)

    dkm = summed(slice(0, length))
    dthrough = summed(slice(2 * length, 2 * length + dim)).astype(LOW)
    dvalue = dval_ref[...] + summed(slice(length, 2 * length))
    dkm_low = dkm.astype(LOW)
    dqdir = -jnp.where(row >= col, mm(dqm, solve, tb=True) + mm(dinside, carried, tb=True), 0.0).astype(LOW)
    dquery = dqm_ref[...] + mm(dinside, low_key) + mm(dqdir, low_unit)
    dsolve = -(mm(qdir, dqm, ta=True) + mm(low_unit, dthrough))
    dcarried = -(mm(low_unit, dkm_low, tb=True) + mm(qdir, dinside, ta=True))
    ysolve = mm(inverse, dsolve, ta=True)
    ycarried = mm(inverse, dcarried, ta=True)
    ddir_key = jnp.where(row > col, ycarried, 0.0).astype(LOW)
    dlower = -(mm(ysolve, solve, tb=True) + mm(ycarried, carried, tb=True))
    ddiag = jnp.sum(jnp.where(row == col, dlower, 0.0), axis=1, keepdims=True)
    dgram = jnp.where(row > col, dlower, 0.0).astype(LOW)
    dkey = dkm + mm(dinside, low_query, ta=True) + mm(ddir_key, low_unit, ta=True)
    dunit = (
        ysolve
        - mm(solve, dthrough, tb=True)
        - mm(carried, dkm_low)
        + mm(dqdir, low_query, ta=True)
        + mm(ddir_key, low_key)
        + mm(dgram, low_unit)
        + mm(dgram, low_unit, ta=True)
    )
    along = jnp.sum(dunit * dirs, axis=1, keepdims=True)
    ddirs = norm * dunit - dirs * (norm * norm * norm * along)
    dbeta = -ddiag / jnp.maximum(beta, 1e-30) * (1.0 - 0.5 * beta)
    lane = iota((length, 128), 1)
    mask = place_ref[1]
    for at, part in enumerate((dquery, dkey, dvalue, ddirs)):
        scatter_rows(dproj_ref, slice(at * dim, (at + 1) * dim), part.astype(LOW), mask)
    scatter_rows(dbeta_ref, slice(None), jnp.where(lane == head, dbeta, 0.0).astype(LOW), mask)


def pack_heads(heads, *refs):
    *parts, out_ref = refs
    dim = parts[0].shape[1] // heads
    for head in range(heads):
        for at, part in enumerate(parts):
            start = (head * len(parts) + at) * dim
            out_ref[:, start : start + dim] = part[:, head * dim : (head + 1) * dim]


def prepare(heads, shard, masks, place_ref, tokens_ref, cot_ref, parts_ref, *rest):
    normed_ref, normed_t_ref, tokens_x_ref, cot_x_ref, small_ref, gains_ref, beta_ref, docs_ref, doc_col_ref = rest[:9]
    marks_ref, sems, mark_sems = rest[9:]
    span = marks_ref.shape[0]
    copies = []
    for slot in range(parts_ref.shape[0]):
        mask = sum(part for at, part in enumerate(masks) if slot >> at & 1)
        at = pl.multiple_of((place_ref[2] ^ mask) * shard, 16)
        copies.append(
            pltpu.make_async_copy(parts_ref.at[slot, pl.ds(0, shard), :], small_ref.at[pl.ds(at, shard), :], sems.at[slot])
        )
        if mask < span:
            copies.append(
                pltpu.make_async_copy(
                    parts_ref.at[slot, pl.ds(shard, 16), :], marks_ref.at[place_ref[0] ^ mask], mark_sems.at[mask]
                )
            )
    for copy in copies:
        copy.start()
    for copy in copies:
        copy.wait()
    small = small_ref[...]
    across = small.astype(WIDE).T
    gains_ref[...] = across[0:8]
    gain = across[heads : heads + 1]
    stream = tokens_ref[...].astype(WIDE)
    scale = lax.rsqrt(jnp.mean(stream * stream, axis=-1, keepdims=True) + EPSILON)
    normed_wide = stream * scale * gain
    normed = normed_wide.astype(LOW)
    normed_ref[...] = normed
    beta_ref[...] = mm(normed, small)
    mask = place_ref[1]
    scatter_rows(tokens_x_ref, slice(None), tokens_ref[...], mask)
    scatter_rows(cot_x_ref, slice(None), cot_ref[...], mask)
    for at in range(normed.shape[0] // 128):
        start = pl.multiple_of((mask ^ at) * 128, 128)
        normed_t_ref[:, pl.ds(start, 128)] = normed_wide[at * 128 : (at + 1) * 128].T.astype(LOW)
    all_marks = marks_ref[...].astype(WIDE)
    line = iota(all_marks.shape, 1)
    length = tokens_ref.shape[0]
    marks = jnp.concatenate(
        [jnp.sum(jnp.where(line == at, all_marks, 0.0), axis=1) for at in range(length // 128)], axis=1
    )
    upper = jnp.where(iota((length, length), 0) <= iota((length, length), 1), 1.0, 0.0)
    docs = mm(marks, upper)
    row = iota(docs.shape, 0)
    before = jnp.zeros_like(docs)
    for at in range(span - 1):
        before = before + jnp.where(row > at, docs[at : at + 1, length - 1 : length], 0.0)
    docs = docs + before
    docs_ref[...] = docs
    own = jnp.sum(jnp.where(row == place_ref[0], docs, 0.0), axis=0, keepdims=True)
    eye = iota((length, length), 0) == iota((length, length), 1)
    column = jnp.sum(jnp.where(eye, own, 0.0), axis=1, keepdims=True)
    doc_col_ref[...] = jnp.broadcast_to(column, doc_col_ref.shape)


def branch_forward(heads, dim, tokens_x_ref, gains_ref, w_out_ref, *rest):
    *pieces, middle_ref, normed_ref, att_ref = rest
    for at, part in enumerate(pieces):
        att_ref[:, at * dim : (at + 1) * dim] = part[...]
    middle = tokens_x_ref[...].astype(WIDE) + mm(att_ref[...], w_out_ref[...], tb=True)
    middle_ref[...] = middle
    scale = lax.rsqrt(jnp.mean(middle * middle, axis=-1, keepdims=True) + EPSILON)
    normed_ref[...] = (middle * scale * gains_ref[heads + 1 : heads + 2]).astype(LOW)


def mlp_forward(cot_ref, gate_ref, up_ref, down_ref, *rest):
    ways = (len(rest) - 3) // 2
    pieces, outs = rest[:ways], rest[ways + 1 : -2]
    all_ref, normed_ref, acc_ref = rest[ways], rest[-2], rest[-1]
    step = pl.program_id(0)
    chunk = pieces[0].shape[0]

    @pl.when(step == 0)
    def start():
        for at, part in enumerate(pieces):
            normed_ref[at * chunk : (at + 1) * chunk, :] = part[...]
        acc_ref[...] = jnp.zeros_like(acc_ref)

    normed = normed_ref[...]
    gate, up, d_hidden = mm(normed, gate_ref[...]), mm(normed, up_ref[...]), mm(cot_ref[...], down_ref[...])
    sig = jax.nn.sigmoid(gate)
    silu = gate * sig
    d_gate = (d_hidden * up * sig * (1.0 + gate * (1.0 - sig))).astype(LOW)
    d_up = (d_hidden * silu).astype(LOW)
    all_ref[0] = d_gate
    all_ref[1] = d_up
    all_ref[2] = (silu * up).astype(LOW)
    acc_ref[...] += mm(d_gate, gate_ref[...], tb=True) + mm(d_up, up_ref[...], tb=True)

    @pl.when(step == pl.num_programs(0) - 1)
    def finish():
        for at, part in enumerate(outs):
            part[...] = acc_ref[at * chunk : (at + 1) * chunk, :].astype(LOW)


def mlp_grads(cot_ref, near_ref, far_ref, down_ref, middle_ref, *rest):
    ways = (len(rest) - 3) // 2
    pieces, grad_ref, outs, left_ref, acc_ref = rest[:ways], rest[ways], rest[ways + 1 : -2], rest[-2], rest[-1]
    step, third = pl.program_id(0), pl.num_programs(0) // 3
    chunk = pieces[0].shape[0]

    @pl.when(step == 0)
    def start():
        for at, part in enumerate(pieces):
            left_ref[:, at * chunk : (at + 1) * chunk] = part[...].astype(WIDE).T.astype(LOW)
        acc_ref[...] = jnp.zeros_like(acc_ref)
        acc_ref[0:chunk, :] = middle_ref[...]

    @pl.when(step == 2 * third)
    def turn():
        for at in range(ways):
            part = cot_ref[at * chunk : (at + 1) * chunk, :]
            left_ref[:, at * chunk : (at + 1) * chunk] = part.astype(WIDE).T.astype(LOW)

    right = jnp.concatenate([near_ref[0], far_ref[0]], axis=0)
    grad_ref[...] = mm(left_ref[...], right).astype(LOW)

    @pl.when(step >= 2 * third)
    def down():
        acc_ref[...] += mm(right, down_ref[...], tb=True)

    @pl.when(step == 3 * third - 1)
    def finish():
        for at, part in enumerate(outs):
            part[...] = acc_ref[at * chunk : (at + 1) * chunk, :].astype(LOW)


def branch_backward(heads, inner, middle_ref, gains_ref, cot_ref, w_out_ref, *rest):
    ways = (len(rest) - 4) // 2
    backs, d_middle_ref, gain_ref, upper_ref, lower_ref, d_atts = rest[:ways], *rest[ways : ways + 4], rest[ways + 4 :]
    grad = total([part[...] for part in backs])
    middle = middle_ref[...]
    scale = lax.rsqrt(jnp.mean(middle * middle, axis=-1, keepdims=True) + EPSILON)
    gain_ref[...] = jnp.broadcast_to(jnp.sum(grad * middle * scale, axis=0, keepdims=True), gain_ref.shape)
    d_middle = cot_ref[...].astype(WIDE) + norm_back(grad, middle, scale, gains_ref[heads + 1 : heads + 2])
    d_middle_ref[...] = d_middle
    d_branch = d_middle.astype(LOW)
    half = upper_ref.shape[0]
    upper_ref[...] = d_branch[:half]
    lower_ref[...] = d_branch[half:]
    for at, part in enumerate(d_atts):
        part[...] = mm(d_branch, w_out_ref[:, at * inner : (at + 1) * inner]).astype(LOW)


def project_back(heads, tokens_x_ref, small_ref, w_ref, gain_two_ref, part_ref, d_proj_ref, *rest):
    d_betas, (gain_ref, d_beta_ref, *outs) = rest[:heads], rest[heads:]
    d_beta = total([part[...] for part in d_betas]).astype(LOW)
    d_beta_ref[...] = d_beta
    back = part_ref[...] + mm(d_beta, small_ref[...], tb=True) + mm(d_proj_ref[...], w_ref[...], tb=True)
    stream = tokens_x_ref[...].astype(WIDE)
    scale = lax.rsqrt(jnp.mean(stream * stream, axis=-1, keepdims=True) + EPSILON)
    gain = jnp.sum(back * stream * scale, axis=0, keepdims=True)
    gain_ref[...] = jnp.where(iota(gain_ref.shape, 0) == 0, gain, gain_two_ref[...])
    chunk = outs[0].shape[0]
    for at, part in enumerate(outs):
        part[...] = back[at * chunk : (at + 1) * chunk].astype(LOW)


def token_grad(heads, tokens_x_ref, gains_ref, d_middle_ref, *rest):
    *backs, out_ref = rest
    grad = total([part[...] for part in backs])
    stream = tokens_x_ref[...].astype(WIDE)
    scale = lax.rsqrt(jnp.mean(stream * stream, axis=-1, keepdims=True) + EPSILON)
    out_ref[...] = (d_middle_ref[...] + norm_back(grad, stream, scale, gains_ref[heads : heads + 1])).astype(LOW)


def token_join(place_ref, *rest):
    *pieces, out_ref = rest
    chunk = pieces[0].shape[0]
    for at, part in enumerate(pieces):
        start = pl.multiple_of((place_ref[1] ^ at) * chunk, chunk)
        out_ref[pl.ds(start, chunk), :] = part[...].astype(out_ref.dtype)


def weight_grads(left_ref, d_proj_ref, *rest):
    rest[-1][...] = mm(left_ref[...], d_proj_ref[...]).astype(LOW)


def out_grads(heads, ways, *rest):
    branches, atts, out_ref, turned_ref = rest[:ways], rest[ways : ways + heads], rest[-2], rest[-1]
    step = pl.program_id(0)
    chunk = 2 * branches[0].shape[0]

    @pl.when(step == 0)
    def turn():
        for at in range(ways // 2):
            part = jnp.concatenate([branches[2 * at][...], branches[2 * at + 1][...]], axis=0)
            turned_ref[:, at * chunk : (at + 1) * chunk] = part.astype(WIDE).T.astype(LOW)

    for head in range(heads):

        @pl.when(step == head)
        def one(head=head):
            out_ref[...] = mm(turned_ref[...], atts[head][...]).astype(LOW)


def small_grads(heads, ways, left_ref, d_beta_ref, *rest):
    gains, out_ref, rows_ref = rest[:ways], rest[-2], rest[-1]
    gain = total([part[...] for part in gains])
    rows_ref[...] = jnp.zeros_like(rows_ref)
    rows_ref[heads : heads + 1, :] = gain[0:1]
    rows_ref[heads + 1 : heads + 2, :] = gain[1:2]
    out_ref[...] = (mm(left_ref[...], d_beta_ref[...]) + rows_ref[...].T).astype(LOW)


def project_more(d_proj_ref, w_ref, *rest):
    part = mm(d_proj_ref[...], w_ref[...], tb=True)
    if len(rest) > 1:
        part = rest[0][...] + part
    rest[-1][...] = part


def grad_join(heads, dim, in_ref, *outs):
    width = 4 * dim
    for head in range(heads):
        for kind, out in enumerate(outs[:4]):
            at = head * width + kind * dim
            out[:, head * dim : (head + 1) * dim] = in_ref[:, at : at + dim].astype(WIDE)
    outs[4][...] = in_ref[:, heads * width : heads * width + 128].astype(WIDE)
    outs[5][...] = in_ref[:, heads * width + 128 :].astype(WIDE)


def fixed(shape):
    return pl.BlockSpec(shape, lambda *unused: (0,) * len(shape))


def column_at(shape, at):
    return pl.BlockSpec(shape, lambda *unused: (0, at))


ANYWHERE = pl.BlockSpec(memory_space=pl.ANY)
SCALARS = pl.BlockSpec(memory_space=pltpu.SMEM)


def run(kernel, name, ins, specs, outs, scratch=(), flops=10**9):
    return pl.pallas_call(
        kernel,
        grid=(1,),
        in_specs=specs,
        out_specs=[fixed(shape) for shape, unused in outs],
        out_shape=[jax.ShapeDtypeStruct(shape, dtype) for shape, dtype in outs],
        scratch_shapes=list(scratch),
        compiler_params=pltpu.CompilerParams(vmem_limit_bytes=VMEM_BYTES),
        cost_estimate=pl.CostEstimate(flops=flops, bytes_accessed=4 * 2**20, transcendentals=2**18),
        name=name,
    )(*ins)


def whole(*arrays):
    return [fixed(array.shape) for array in arrays]


def run_block_forward(places, normed, w_in, at, beta_raw, doc_col, doc_row, dim, head):
    length, width = normed.shape
    square, tall = (length, length), (length, dim)
    return run(
        functools.partial(block_forward, head),
        "block_forward",
        (places, normed, w_in, beta_raw, doc_col, doc_row),
        [SCALARS, *whole(normed), column_at((width, 4 * dim), at), *whole(beta_raw, doc_col, doc_row)],
        [
            ((length, 4 * dim), WIDE),
            ((2 * length + dim, dim), LOW),
            (tall, WIDE),
            (square, WIDE),
            (square, LOW),
            (square, LOW),
            (square, LOW),
            (tall, LOW),
            ((length, 128), WIDE),
            (tall, WIDE),
        ],
        flops=10**10,
    )


def run_cross_forward(places, q_moved, stats, acc, doc_col, docs, packs, swapped):
    length, dim = q_moved.shape
    ins = (q_moved, stats, acc, doc_col, docs)
    return run(
        functools.partial(cross_forward, swapped),
        "cross_forward",
        (places, *ins, *packs),
        [SCALARS, *whole(*ins), ANYWHERE, ANYWHERE],
        [((length, dim), WIDE), ((length, dim), LOW), ((length, dim), WIDE)],
        [
            pltpu.VMEM((SPAN,) + packs[0].shape[1:], LOW),
            pltpu.VMEM((length, dim), WIDE),
            pltpu.VMEM((SPAN - 1, length, length), WIDE),
            pltpu.VMEM((length, 128), WIDE),
            pltpu.SemaphoreType.DMA((2,)),
        ],
        flops=10**10,
    )


def run_cross_backward(places, q_moved, scores, attention, log_total, doc_col, docs, packs, d_atts, head, swapped):
    length, dim = q_moved.shape
    ins = (q_moved, scores, attention, log_total, doc_col, docs)
    both = (SPAN,) + packs[0].shape[1:]
    return run(
        functools.partial(cross_backward, swapped),
        "cross_backward",
        (places, *ins, *packs, *d_atts),
        [SCALARS, *whole(*ins), ANYWHERE, ANYWHERE] + [column_at((part.shape[0], dim), head) for part in d_atts],
        [(packs[0].shape, LOW)] * 2 + [((length, dim), WIDE), ((length, length), LOW), ((length, dim), WIDE)],
        [
            pltpu.VMEM(both, LOW),
            pltpu.VMEM(both, LOW),
            pltpu.VMEM((SPAN + 1, length, dim), WIDE),
            pltpu.VMEM((SPAN, length, dim), WIDE),
            pltpu.VMEM((length, dim), LOW),
            pltpu.VMEM((length, length), WIDE),
            pltpu.SemaphoreType.DMA((2,)),
        ],
        flops=10**10,
    )


def run_block_backward(places, proj, beta_raw, kept, d_packs, head, dim):
    length = proj.shape[0]
    ins = (proj, beta_raw, *kept, *d_packs)
    return run(
        functools.partial(block_backward, head),
        "block_backward",
        (places, *ins),
        [SCALARS, *whole(*ins)],
        [(proj.shape, LOW), ((length, 128), LOW)],
        flops=5 * 10**9,
    )


def norm_back(grad, value, scale, gain):
    weighted = grad * gain
    return scale * weighted - value * scale * scale * scale * jnp.mean(weighted * value, axis=-1, keepdims=True)


def total(parts):
    out = parts[0].astype(WIDE)
    for part in parts[1:]:
        out = out + part.astype(WIDE)
    return out


def per_device(
    tokens, cotangent, starts, gain_attn, w_query, w_key, w_value, w_dir, w_beta, w_out, gain_mlp, w_gate, w_up, w_down
):
    row_count, width = tokens.shape
    shard, inner = w_query.shape
    hidden_units = w_gate.shape[1]
    heads = w_beta.shape[1]
    dim = inner // heads
    count = lax.axis_size("seq")
    ways = lax.axis_size("head")
    chunk = row_count // ways
    seq_place, head_place = lax.axis_index("seq"), lax.axis_index("head")
    places = jnp.stack([seq_place % SPAN, head_place, seq_place]).astype(jnp.int32)

    def to_heads(parts):
        return [xor_move(part, "head", at) if at else part for at, part in enumerate(parts)]

    def over_heads(part):
        return to_heads([part] * ways)

    small = jnp.concatenate([w_beta, gain_attn[:, None], gain_mlp[:, None]], axis=1)
    small = jnp.pad(small, ((0, 0), (0, 128 - heads - 2)))
    marks = jnp.pad(starts.astype(LOW).reshape(row_count // 128, 128), ((0, 16 - row_count // 128), (0, 0)))
    masks = tuple(2 << at for at in range((count // 2).bit_length() - 1)) + (1,)
    small = doubled(jnp.concatenate([small, marks], axis=0), masks)
    four = (w_query, w_key, w_value, w_dir)
    (packed,) = run(functools.partial(pack_heads, heads), "pack_heads", four, whole(*four), [((shard, 4 * inner), LOW)])
    w_in = lax.all_gather(packed, "seq", axis=0, tiled=True)
    out_parts = jnp.concatenate(over_heads(w_out.T), axis=1)

    tall, wide_tall, part_low = (row_count, width), (width, row_count), ((chunk, width), LOW)
    normed, normed_x_t, tokens_x, cot_x, small_all, gains, beta_raw, docs, doc_col = run(
        functools.partial(prepare, heads, shard, masks),
        "prepare",
        (places, tokens, cotangent, small),
        [SCALARS, *whole(tokens, cotangent), ANYWHERE],
        [
            (tall, LOW),
            (wide_tall, LOW),
            (tall, LOW),
            (tall, LOW),
            ((width, 128), LOW),
            ((8, width), WIDE),
            ((row_count, 128), WIDE),
            ((SPAN, row_count), WIDE),
            ((row_count, 128), WIDE),
        ],
        [
            pltpu.VMEM((SPAN, 16, 128), LOW),
            pltpu.SemaphoreType.DMA((count,)),
            pltpu.SemaphoreType.DMA((SPAN,)),
        ],
    )
    normed, out_parts = lax.optimization_barrier((normed, out_parts))
    w_out_x = lax.all_gather(after(out_parts, w_in), "seq", axis=0, tiled=True)

    orders = [(2, 4)] * heads
    first, mixed, ready, full = [], [], {}, {}

    def step(kind, head):
        return (head, kind, xor_move(ready[head], "seq", orders[head][kind] if kind < 2 else 1))

    def meet(outs, moves):
        outs, arrived = lax.optimization_barrier((outs, [move[2] for move in moves]))
        for (head, kind, unused), part in zip(moves, arrived):
            ready[head] = (ready[head], part) if kind == 2 else jnp.concatenate([ready[head], part], axis=0)
        return outs

    flying = []
    for head in range(heads):
        held = normed if head == 0 else after(normed, first[-1][2])
        outs = run_block_forward(places, held, w_in, head, beta_raw, doc_col, docs, dim, head)
        first.append(meet(outs, flying))
        ready[head] = first[head][1][None]
        flying = [step(at, head - at) for at in range(max(0, head - 2), head + 1)]
    rest_in = jnp.concatenate([w_gate, w_up, w_down.T], axis=1)
    stage = {move[0]: move[1] for move in flying}
    for head in range(heads):
        kept = first[head]
        while stage.get(head, 2) < 2 or any(move[0] == head for move in flying):
            now = [move for move in flying if move[0] == head]
            flying = [move for move in flying if move[0] != head]
            meet((), now)
            if stage[head] < 2:
                stage[head] += 1
                flying.append(step(stage[head], head))
        if head == 0:
            held = kept[2]
        else:
            held = after(kept[2], mixed[-1][0])
        outs = run_cross_forward(places, held, kept[8], kept[9], doc_col, docs, ready[head], False)
        mixed.append(meet(outs, flying))
        flying = []
        for later in range(head + 1, heads):
            if stage[later] < 2:
                stage[later] += 1
                flying.append(step(stage[later], later))
        if head == 0:
            w_rest = lax.all_gather(after(rest_in, mixed[0][0], w_out_x), "seq", axis=0, tiled=True)
    packs = [ready[head] for head in range(heads)]

    att_x = jnp.concatenate([part[1] for part in mixed], axis=1)
    att_parts = to_heads([att_x[at * chunk : (at + 1) * chunk] for at in range(ways)])
    own_rows = fixed((chunk, width))
    middle, normed_two = run(
        functools.partial(branch_forward, heads, inner),
        "branch_forward",
        (tokens_x, gains, w_out_x, *att_parts),
        [own_rows, *whole(gains, w_out_x, *att_parts)],
        [((chunk, width), WIDE), part_low],
        [pltpu.VMEM((chunk, ways * inner), LOW)],
    )
    two_parts = over_heads(normed_two)

    blocks = 2
    cols = hidden_units // blocks

    def mlp_half(parts, at):
        rows = chunk * len(parts)
        return pl.pallas_call(
            mlp_forward,
            grid=(blocks,),
            in_specs=[
                pl.BlockSpec((rows, width), lambda step: (at, 0)),
                pl.BlockSpec((width, cols), lambda step: (0, step)),
                pl.BlockSpec((width, cols), lambda step: (0, blocks + step)),
                pl.BlockSpec((width, cols), lambda step: (0, 2 * blocks + step)),
                *whole(*parts),
            ],
            out_specs=[pl.BlockSpec((3, rows, cols), lambda step: (0, 0, step))] + [fixed((chunk, width))] * len(parts),
            out_shape=[jax.ShapeDtypeStruct((3, rows, hidden_units), LOW)]
            + [jax.ShapeDtypeStruct((chunk, width), LOW)] * len(parts),
            scratch_shapes=[pltpu.VMEM((rows, width), LOW), pltpu.VMEM((rows, width), WIDE)],
            compiler_params=pltpu.CompilerParams(vmem_limit_bytes=VMEM_BYTES),
            cost_estimate=pl.CostEstimate(flops=5 * 10**9, bytes_accessed=2**24, transcendentals=2**19),
            name="mlp_forward",
        )(cot_x, w_rest, w_rest, w_rest, *parts)

    near_all, *near_backs = mlp_half(two_parts[: ways // 2], 0)
    (near_all, near_backs), far_two = lax.optimization_barrier(((near_all, near_backs), two_parts[ways // 2 :]))
    near_moves = [xor_move(part, "head", at) if at else part for at, part in enumerate(near_backs)]
    far_all, *far_backs = mlp_half([after(part, near_all) for part in far_two], 1)
    (far_all, far_backs), near_moves = lax.optimization_barrier(((far_all, far_backs), near_moves))
    two_parts = two_parts[: ways // 2] + list(far_two)
    backs = near_moves + [xor_move(part, "head", ways // 2 + at) for at, part in enumerate(far_backs)]
    grad_mlp, *mlp_parts = pl.pallas_call(
        mlp_grads,
        grid=(3 * blocks,),
        in_specs=[
            fixed(tall),
            pl.BlockSpec((1, row_count // 2, cols), lambda step: (step // blocks, 0, step % blocks)),
            pl.BlockSpec((1, row_count // 2, cols), lambda step: (step // blocks, 0, step % blocks)),
            pl.BlockSpec((width, cols), lambda step: (0, jnp.maximum(step, 2 * blocks))),
            fixed((chunk, width)),
            *whole(*two_parts),
        ],
        out_specs=[pl.BlockSpec((width, cols), lambda step: (0, step))] + [fixed((chunk, width))] * ways,
        out_shape=[jax.ShapeDtypeStruct((width, 3 * hidden_units), LOW)]
        + [jax.ShapeDtypeStruct((chunk, width), LOW)] * ways,
        scratch_shapes=[pltpu.VMEM(wide_tall, LOW), pltpu.VMEM(tall, WIDE)],
        compiler_params=pltpu.CompilerParams(vmem_limit_bytes=VMEM_BYTES),
        cost_estimate=pl.CostEstimate(flops=10**10, bytes_accessed=2**24, transcendentals=0),
        name="mlp_grads",
    )(cot_x, near_all, far_all, w_rest, middle, *two_parts)
    grad_mlp, mlp_parts, backs = lax.optimization_barrier((grad_mlp, mlp_parts, backs))
    reduced_mlp = lax.psum_scatter(grad_mlp, "seq", scatter_dimension=0, tiled=True)

    d_middle, gain_two_sum, upper, lower, *d_atts = run(
        functools.partial(branch_backward, heads, inner),
        "branch_backward",
        (middle, gains, cot_x, w_out_x, *backs),
        [*whole(middle, gains), own_rows, *whole(w_out_x, *backs)],
        [((chunk, width), WIDE), ((8, width), WIDE)] + [((chunk // 2, width), LOW)] * 2 + [((chunk, inner), LOW)] * ways,
    )
    d_atts = to_heads(d_atts)

    def add(left, right):
        return (left.astype(WIDE) + right.astype(WIDE)).astype(LOW)

    second, low_sums, high_sums, last_sums, branch_parts = [], {}, {}, {}, [upper, lower]
    core, across = {}, {}
    halves_two = [after(part, *d_atts[1:]) for part in (upper, lower)]
    branch_moves = [(part, at) for at in range(1, ways) for part in halves_two]
    shares = [2] + [1] * (2 * heads - 3)

    def branch_next():
        some = shares.pop(0) if shares else len(branch_moves)
        out = [xor_move(part, "head", at) for part, at in branch_moves[:some]]
        del branch_moves[:some]
        return out

    for head in range(heads):
        kept = first[head]
        held = kept[2] if head == 0 else after(kept[2], second[-1][0])
        flying = (core.get(head - 1), across.get(head - 2), branch_next())
        outs = run_cross_backward(
            places, held, kept[3], mixed[head][0], mixed[head][2], doc_col, docs, packs[head], d_atts, head, False
        )
        outs, (core_in, across_in, branch_in) = lax.optimization_barrier((outs, flying))
        even, odd, *rest = outs
        second.append(rest)
        branch_parts += branch_in
        if head >= 2:
            last_sums[head - 2] = [add(low_sums[head - 2][at], across_in[at]) for at in range(2)]
        if head >= 1:
            high_sums[head - 1] = add(low_sums[head - 1][2:], core_in[2:])
            across[head - 1] = xor_move(high_sums[head - 1], "seq", orders[head - 1][1])
            low_sums[head - 1] = add(low_sums[head - 1][:2], core_in[:2])
        low_sums[head] = even
        core[head] = xor_move(odd, "seq", 1)
    mlp_rows = jnp.stack(mlp_parts)
    mlp_rows = jnp.concatenate([lax.dynamic_index_in_dim(mlp_rows, head_place ^ at, 0, False) for at in range(ways)])
    result = lax.psum(after(mlp_rows, reduced_mlp, second[-1][0]), "head")

    cols = 4 * dim
    grad_in = None

    def grads_into(kernel, ins, specs, at, grid, name, scratch=()):
        given = () if grad_in is None else (grad_in,)
        return pl.pallas_call(
            kernel,
            grid=(grid,),
            in_specs=specs + [ANYWHERE] * len(given),
            out_specs=at,
            out_shape=jax.ShapeDtypeStruct((width, (heads + 1) * cols), LOW),
            input_output_aliases={len(ins): 0} if given else {},
            scratch_shapes=list(scratch),
            compiler_params=pltpu.CompilerParams(vmem_limit_bytes=VMEM_BYTES),
            cost_estimate=pl.CostEstimate(flops=10**9, bytes_accessed=2**22, transcendentals=0),
            name=name,
        )(*ins, *given)

    d_projs, d_betas = [], []
    back_part = None
    for head in range(heads):
        if head not in last_sums:
            last_sums[head] = [add(low_sums[head][at], across[head][at]) for at in range(2)]
        near_sum, far_sum = last_sums[head]
        sent = [near_sum, xor_move(far_sum, "seq", orders[head][0])]
        if head >= 1:
            grad_in = grads_into(
                weight_grads,
                (normed_x_t, d_projs[-1]),
                whole(normed_x_t, d_projs[-1]),
                column_at((width, cols), head - 1),
                1,
                "weight_grads",
            )
            ins = (d_projs[-1], w_in) + (() if back_part is None else (back_part,))
            (back_part,) = run(
                project_more,
                "project_more",
                ins,
                [*whole(d_projs[-1]), column_at((width, cols), head - 1), *whole(*ins[2:])],
                [(tall, WIDE)],
            )
            if head == heads - 1:
                atts = [part[1] for part in mixed]
                grad_in = grads_into(
                    functools.partial(out_grads, heads, len(branch_parts)),
                    (*branch_parts, *atts),
                    whole(*branch_parts, *atts),
                    pl.BlockSpec((width, 128), lambda step: (0, heads * cols // 128 + 1 + step)),
                    heads,
                    "out_grads",
                    [pltpu.VMEM(wide_tall, LOW)],
                )
            grad_in, back_part, sent = lax.optimization_barrier((grad_in, back_part, sent))
        late = heads - 1 if head == 0 and heads - 1 not in across else None
        flying = (across.get(head + 1), core[late] if late else None, branch_next() if head + 1 < heads else [])
        proj, inverse, carried, qdir, solve = (first[head][at] for at in (0, 4, 5, 6, 7))
        if head == 0:
            proj, reduced_mlp = lax.optimization_barrier((proj, reduced_mlp))
        outs = run_block_backward(
            places, proj, beta_raw, (inverse, carried, qdir, solve, *second[head]), sent, head, dim
        )
        (d_proj, d_beta), (across_in, core_in, branch_in) = lax.optimization_barrier((outs, flying))
        branch_parts += branch_in
        if across_in is not None:
            across[head + 1] = across_in
        if late:
            across[late] = xor_move(add(low_sums[late][2:], core_in[2:]), "seq", orders[late][1])
            low_sums[late] = add(low_sums[late][:2], core_in[:2])
        d_projs.append(d_proj)
        d_betas.append(d_beta)
    back_ins = (tokens_x, small_all, w_in, gain_two_sum, back_part, d_projs[-1], *d_betas)
    gain_sums, d_beta, *backs = run(
        functools.partial(project_back, heads),
        "project_back",
        back_ins,
        [
            *whole(tokens_x, small_all),
            column_at((width, cols), heads - 1),
            *whole(*back_ins[3:]),
        ],
        [((8, width), WIDE), ((row_count, 128), LOW)] + [part_low] * ways,
    )
    backs = to_heads(backs)
    (d_tokens_own,) = run(
        functools.partial(token_grad, heads),
        "token_grad",
        (tokens_x, gains, d_middle, *backs),
        [own_rows, *whole(gains, d_middle, *backs)],
        [part_low],
    )
    token_parts = over_heads(d_tokens_own)
    grad_in = grads_into(
        weight_grads,
        (normed_x_t, d_projs[-1]),
        whole(normed_x_t, d_projs[-1]),
        column_at((width, cols), heads - 1),
        1,
        "weight_grads",
    )
    gain_parts = over_heads(gain_sums)
    ins = (normed_x_t, d_beta, *gain_parts)
    grad_in = grads_into(
        functools.partial(small_grads, heads, ways),
        ins,
        whole(*ins),
        column_at((width, 128), heads * cols // 128),
        1,
        "small_grads",
        [pltpu.VMEM((128, width), WIDE)],
    )
    grad_in, result = lax.optimization_barrier((grad_in, result))
    reduced_in = lax.psum_scatter(grad_in, "seq", scatter_dimension=0, tiled=True)
    *grads, small_sum, grad_out_t = run(
        functools.partial(grad_join, heads, dim),
        "grad_join",
        (reduced_in,),
        whole(reduced_in),
        [((shard, inner), WIDE)] * 4 + [((shard, 128), WIDE), ((shard, inner), WIDE)],
    )
    reduced_mlp = reduced_mlp.astype(WIDE)
    finished = (
        *grads,
        small_sum,
        grad_out_t.T,
        reduced_mlp[:, :hidden_units],
        reduced_mlp[:, hidden_units : 2 * hidden_units],
        reduced_mlp[:, 2 * hidden_units :].T,
    )
    finished, token_parts = lax.optimization_barrier((finished, token_parts))
    *grads, small_sum, grad_out, grad_gate, grad_up, grad_down = finished
    (d_tokens,) = run(
        token_join, "token_join", (places, *token_parts), [SCALARS, *whole(*token_parts)], [(tall, WIDE)]
    )
    return (
        result,
        d_tokens,
        small_sum[:, heads],
        *grads,
        small_sum[:, :heads],
        grad_out,
        small_sum[:, heads + 1],
        grad_gate,
        grad_up,
        grad_down,
    )


def solution(mesh):
    placed = (
        P("seq", None),
        P("seq", None),
        P("seq"),
        P("seq"),
        P("seq", "head"),
        P("seq", "head"),
        P("seq", "head"),
        P("seq", "head"),
        P("seq", "head"),
        P("head", "seq"),
        P("seq"),
        P("seq", "head"),
        P("seq", "head"),
        P("head", "seq"),
    )
    return jax.shard_map(
        per_device,
        mesh=mesh,
        in_specs=placed,
        out_specs=(
            P("seq", None),
            P("seq", None),
            P("seq"),
            P("seq", "head"),
            P("seq", "head"),
            P("seq", "head"),
            P("seq", "head"),
            P("seq", "head"),
            P("head", "seq"),
            P("seq"),
            P("seq", "head"),
            P("seq", "head"),
            P("head", "seq"),
        ),
        check_vma=False,
    )
```

```python
import functools

import jax
import jax.numpy as jnp
from jax import lax
from jax.experimental import pallas as pl
from jax.experimental.pallas import tpu as pltpu
from jax.sharding import PartitionSpec as P

SPAN = 8
EPSILON = 1e-06
NEGATIVE = -1e30
LOG2E = 1.4426950408889634
LOW = jnp.bfloat16
WIDE = jnp.float32
VMEM_BYTES = 40 * 2**20


def mm(left, right, ta=False, tb=False):
    dims = (((0 if ta else 1,), (1 if tb else 0,)), ((), ()))
    return lax.dot_general(
        left.astype(LOW), right.astype(LOW), dims, preferred_element_type=WIDE
    )


def halves(value):
    high = value.astype(LOW)
    return high, (value - high.astype(WIDE)).astype(LOW)


def mm3(left, right, ta=False, tb=False):
    left_hi, left_lo = left if isinstance(left, tuple) else halves(left)
    right_hi, right_lo = right if isinstance(right, tuple) else halves(right)
    return mm(left_hi, right_hi, ta, tb) + (mm(left_hi, right_lo, ta, tb) + mm(left_lo, right_hi, ta, tb))


def iota(shape, axis):
    return lax.broadcasted_iota(jnp.int32, shape, axis)


def lower_inverse(strict, beta):
    length = strict.shape[0]
    size = 128
    row, col = iota((size, size), 0), iota((size, size), 1)
    subs, blocks = [], []
    for at in range(0, length, size):
        sub = strict[at : at + size, at : at + size]
        scale = beta[at : at + size]
        diag = jnp.where(row == col, scale, 0.0)
        across = jnp.sum(diag, axis=0, keepdims=True)
        pair = ((row >> 1) == (col >> 1)) & (row > col)
        subs.append(sub)
        blocks.append(diag - jnp.where(pair, sub * scale * across, 0.0))
    bit = 1
    while (1 << bit) < size:
        mask = ((row >> (bit + 1)) == (col >> (bit + 1))) & ((row >> bit) != (col >> bit)) & (row > col)
        right = [mm3(jnp.where(mask, sub, 0.0), block) for sub, block in zip(subs, blocks)]
        blocks = [block - mm3(block, part) for block, part in zip(blocks, right)]
        bit += 1
    while len(blocks) > 1:
        size = blocks[0].shape[0]
        joined = []
        for pair_at in range(len(blocks) // 2):
            first, second = blocks[2 * pair_at], blocks[2 * pair_at + 1]
            at = 2 * pair_at * size
            corner = -mm3(second, mm3(strict[at + size : at + 2 * size, at : at + size], first))
            joined.append(
                jnp.concatenate(
                    [
                        jnp.concatenate([first, jnp.zeros_like(first)], axis=1),
                        jnp.concatenate([corner, second], axis=1),
                    ],
                    axis=0,
                )
            )
        blocks = joined
    return blocks[0]


def xor_move(value, axis, mask):
    return lax.ppermute(value, axis, [(at, at ^ mask) for at in range(lax.axis_size(axis))])


def after(value, *others):
    return lax.optimization_barrier((value, *others))[0]


def doubled_again(held, mask):
    return jnp.concatenate([held, xor_move(held, "seq", mask)], axis=0)


def doubled(block, masks):
    held = block[None]
    for mask in masks:
        held = doubled_again(held, mask)
    return held


def block_forward(
    place_ref, normed_ref, w_ref, beta_ref, doc_col_ref, doc_row_ref,
    proj_ref, pack_ref, qm_ref, score_ref, inv_ref, carried_ref, qdir_ref, solve_ref, stat_ref, acc_ref,
):
    proj_ref[...] = mm(normed_ref[...], w_ref[...])
    length, dim = qm_ref.shape
    query, key = proj_ref[:, 0:dim], proj_ref[:, dim : 2 * dim]
    value, dirs = proj_ref[:, 2 * dim : 3 * dim].astype(LOW), proj_ref[:, 3 * dim :]
    head = place_ref[3]
    beta = 2.0 * jax.nn.sigmoid(jnp.sum(jnp.where(iota((length, 128), 1) == head, beta_ref[...], 0.0), axis=1, keepdims=True))
    unit = dirs * lax.rsqrt(jnp.sum(dirs * dirs, axis=-1, keepdims=True) + EPSILON)
    row, col = iota((length, length), 0), iota((length, length), 1)
    unit_two = halves(unit)
    strict = jnp.where(row > col, mm3(unit_two, unit_two, tb=True), 0.0)
    inverse = lower_inverse(strict, beta)
    inverse_two = halves(inverse)
    solve = mm3(inverse_two, unit_two)
    solve_two = halves(solve)
    dir_key = jnp.where(row > col, mm3(unit_two, key, tb=True), 0.0)
    carried = mm3(inverse_two, dir_key)
    carried_two = halves(carried)
    qdir = jnp.where(row >= col, mm3(query, unit_two, tb=True), 0.0)
    qdir_two = halves(qdir)
    qm_ref[...] = query - mm3(qdir_two, solve_two)
    pack_ref[0:length, :] = (key - mm3(carried_two, unit_two, ta=True)).astype(LOW)
    pack_ref[length : 2 * length, :] = value
    eye = jnp.where(iota((dim, dim), 0) == iota((dim, dim), 1), 1.0, 0.0)
    pack_ref[2 * length :, :] = (eye - mm3(unit_two, solve_two, ta=True)).astype(LOW)
    inside = mm(query, key, tb=True) - mm(qdir_two[0], carried_two[0])
    inv_ref[...] = inverse.astype(LOW)
    carried_ref[...] = carried_two[0]
    qdir_ref[...] = qdir_two[0]
    solve_ref[...] = solve_two[0]
    allowed = (doc_col_ref[:, 0:1] == doc_row_ref[pl.ds(place_ref[0], 1), :]) & (row >= col)
    score = jnp.where(allowed, inside * (LOG2E * dim**-0.5), NEGATIVE)
    score_ref[...] = score
    peak = jnp.max(score, axis=1, keepdims=True)
    weight = jnp.exp2(score - peak)
    lane = iota((length, 128), 1)
    stat_ref[...] = jnp.where(lane == 0, peak, jnp.sum(weight, axis=1, keepdims=True))
    acc_ref[...] = mm(weight, value)


def bring(halves_in, pack_ref, sems):
    size = halves_in[0].shape[0]
    copies = [
        pltpu.make_async_copy(part, pack_ref.at[pl.ds(at * size, size)], sems.at[at]) for at, part in enumerate(halves_in)
    ]
    for copy in copies:
        copy.start()
    for copy in copies:
        copy.wait()


def slot_of(mask, swapped):
    core, first, second = mask & 1, (mask >> 1) & 1, mask >> 2
    return 4 * core + (2 * first + second if swapped else first + 2 * second)


def cross_forward(
    swapped, place_ref, qm_ref, stat_in_ref, acc_ref, doc_col_ref, doc_row_ref, far_ref, core_ref,
    att_ref, att_x_ref, log_ref, pack_ref, moved_ref, score_ref, peak_ref, sems,
):
    bring((far_ref, core_ref), pack_ref, sems)
    length, dim = qm_ref.shape
    place = place_ref[0]
    moved_ref[...] = qm_ref[...]
    att_ref[...] = acc_ref[...]
    own_peak = stat_in_ref[:, 0:1]
    peak_ref[...] = jnp.broadcast_to(own_peak, (length, 128))

    def look(step, carry):
        at = place - step
        slot = slot_of(place ^ at, swapped)
        moved = moved_ref[...]
        score = mm(moved * (LOG2E * dim**-0.5), pack_ref[slot, 0:length, :], tb=True)
        moved_ref[...] = mm(moved, pack_ref[slot, 2 * length :, :])
        allowed = doc_col_ref[:, 0:1] == doc_row_ref[pl.ds(at, 1), :]
        score = jnp.where(allowed, score, NEGATIVE)
        score_ref[at] = score
        high = peak_ref[...]
        for lane in range(0, length, 128):
            high = jnp.maximum(high, score[:, lane : lane + 128])
        peak_ref[...] = high
        return carry

    def two_looks(pair, carry):
        look(2 * pair + 1, carry)
        return look(2 * pair + 2, carry)

    lax.fori_loop(0, place // 2, two_looks, 0)
    lax.fori_loop(place // 2 * 2 + 1, place + 1, look, 0)
    peak = jnp.max(peak_ref[...], axis=1, keepdims=True)
    rescale = jnp.exp2(own_peak - peak)
    att_ref[...] = att_ref[...] * rescale
    lanes = iota((length, 128), 1)
    moved_ref[...] = jnp.where(lanes == 0, stat_in_ref[:, 1:2] * rescale, 0.0)

    def use(at, carry):
        slot = slot_of(place ^ at, swapped)
        weight = jnp.exp2(score_ref[at] - peak)
        sums = moved_ref[...]
        for lane in range(0, length, 128):
            sums = sums + weight[:, lane : lane + 128]
        moved_ref[...] = sums
        att_ref[...] += mm(weight, pack_ref[slot, length : 2 * length, :])
        return carry

    def two_uses(pair, carry):
        use(2 * pair, carry)
        return use(2 * pair + 1, carry)

    lax.fori_loop(0, place // 2, two_uses, 0)
    lax.fori_loop(place // 2 * 2, place, use, 0)
    total = jnp.sum(moved_ref[...], axis=1, keepdims=True)
    attention = att_ref[...] / total
    att_ref[...] = attention
    scatter_rows(att_x_ref, slice(None), attention.astype(LOW), place_ref[1])
    log_ref[...] = jnp.broadcast_to(peak + jnp.log2(total), (length, 128))


def same_document(doc_row_ref, at, place):
    first = doc_row_ref[pl.ds(at, 1), :][:, 0:1]
    last = doc_row_ref[pl.ds(place, 1), :][:, doc_row_ref.shape[1] - 1 :]
    return jnp.sum(last - first) == 0.0


def scatter_rows(ref, columns, value, mask, chunk=128):
    for at in range(value.shape[0] // chunk):
        start = pl.multiple_of((mask ^ at) * chunk, chunk)
        ref[pl.ds(start, chunk), columns] = value[at * chunk : (at + 1) * chunk]


def cross_backward(swapped, place_ref, qm_ref, score_ref, att_ref, log_ref, doc_col_ref, doc_row_ref, far_ref, core_ref, *rest):
    *datts, even_ref, odd_ref, dqm_ref, dinside_ref, dval_ref = rest[:-7]
    pack_ref, sums_ref, chain_ref, dchain_ref, datt_ref, turned_ref, sems = rest[-7:]
    bring((far_ref, core_ref), pack_ref, sems)
    length, dim = qm_ref.shape
    place = place_ref[0]
    chunk = datts[0].shape[0]
    for at, part in enumerate(datts):
        start = pl.multiple_of((place_ref[1] ^ at) * chunk, chunk)
        datt_ref[pl.ds(start, chunk), :] = part[...]
    scale = dim**-0.5
    datt = datt_ref[...]
    log_total = log_ref[:, 0:1]
    delta = jnp.sum(datt.astype(WIDE) * att_ref[...], axis=1, keepdims=True)
    value = pack_ref[0, length : 2 * length, :]
    probs = jnp.exp2(score_ref[...] - log_total)
    dprob = mm(datt, value, tb=True)
    dinside_ref[...] = (probs * (dprob - delta) * scale).astype(LOW)
    dval_ref[...] = mm(probs, datt, ta=True)
    chain_ref[1] = qm_ref[...]

    def put(slot, rows, part):
        sums_ref[slot, rows, :] = part.astype(LOW)

    def blank(at, carry):
        put(slot_of(place ^ at, swapped), slice(None), jnp.zeros(sums_ref.shape[1:], LOW))
        return carry

    lax.fori_loop(place, SPAN, blank, 0)

    def hop(step, carry):
        at = place - step
        slot = slot_of(place ^ at, swapped)
        moved = chain_ref[step]
        key = pack_ref[slot, 0:length, :]
        value = pack_ref[slot, length : 2 * length, :]
        through = pack_ref[slot, 2 * length :, :]
        chain_ref[step + 1] = mm(moved, through)
        allowed = doc_col_ref[:, 0:1] == doc_row_ref[pl.ds(at, 1), :]
        probs = jnp.exp2(jnp.where(allowed, mm(moved * (LOG2E * scale), key, tb=True), NEGATIVE) - log_total)
        dscore = (probs * (mm(datt, value, tb=True) - delta)).astype(LOW)
        dchain_ref[step] = mm(dscore, key) * scale
        put(slot, slice(0, length), mm(dscore, moved * scale, ta=True))
        put(slot, slice(length, 2 * length), mm(probs, datt, ta=True))
        return carry

    def two_hops(pair, carry):
        hop(2 * pair + 1, carry)
        return hop(2 * pair + 2, carry)

    lax.fori_loop(0, place // 2, two_hops, 0)
    lax.fori_loop(place // 2 * 2 + 1, place + 1, hop, 0)

    def back(count, carry):
        step = place - count
        slot = slot_of(place ^ (place - step), swapped)
        through = pack_ref[slot, 2 * length :, :]
        grad = dqm_ref[...]
        put(slot, slice(2 * length, 2 * length + dim), mm(chain_ref[step], grad, ta=True))
        dqm_ref[...] = dchain_ref[step] + mm(grad, through, tb=True)
        return carry

    dqm_ref[...] = jnp.zeros((length, dim), WIDE)
    lax.fori_loop(0, place, back, 0)
    even_ref[...] = sums_ref[: SPAN // 2]
    odd_ref[...] = sums_ref[SPAN // 2 :]


def block_backward(
    place_ref, proj_ref, beta_ref, inv_ref, carried_ref, qdir_ref, solve_ref, dqm_ref, dinside_ref, dval_ref, *rest
):
    *dpacks, dproj_ref, dbeta_ref = rest
    length, dim = dqm_ref.shape
    query, key, dirs = proj_ref[:, 0:dim], proj_ref[:, dim : 2 * dim], proj_ref[:, 3 * dim :]
    head = place_ref[3]
    beta = 2.0 * jax.nn.sigmoid(jnp.sum(jnp.where(iota((length, 128), 1) == head, beta_ref[...], 0.0), axis=1, keepdims=True))
    norm = lax.rsqrt(jnp.sum(dirs * dirs, axis=-1, keepdims=True) + EPSILON)
    unit = dirs * norm
    low_unit, low_key, low_query = unit.astype(LOW), key.astype(LOW), query.astype(LOW)
    row, col = iota((length, length), 0), iota((length, length), 1)
    inverse, carried, qdir, solve = inv_ref[...], carried_ref[...], qdir_ref[...], solve_ref[...]
    dqm, dinside = dqm_ref[...].astype(LOW), dinside_ref[...]

    def summed(rows):
        return sum(part[rows, :].astype(WIDE) for part in dpacks)

    dkm = summed(slice(0, length))
    dthrough = summed(slice(2 * length, 2 * length + dim)).astype(LOW)
    dvalue = dval_ref[...] + summed(slice(length, 2 * length))
    dkm_low = dkm.astype(LOW)
    dqdir = -jnp.where(row >= col, mm(dqm, solve, tb=True) + mm(dinside, carried, tb=True), 0.0).astype(LOW)
    dquery = dqm_ref[...] + mm(dinside, low_key) + mm(dqdir, low_unit)
    dsolve = -(mm(qdir, dqm, ta=True) + mm(low_unit, dthrough))
    dcarried = -(mm(low_unit, dkm_low, tb=True) + mm(qdir, dinside, ta=True))
    ysolve = mm(inverse, dsolve, ta=True)
    ycarried = mm(inverse, dcarried, ta=True)
    ddir_key = jnp.where(row > col, ycarried, 0.0).astype(LOW)
    dlower = -(mm(ysolve, solve, tb=True) + mm(ycarried, carried, tb=True))
    ddiag = jnp.sum(jnp.where(row == col, dlower, 0.0), axis=1, keepdims=True)
    dgram = jnp.where(row > col, dlower, 0.0).astype(LOW)
    dkey = dkm + mm(dinside, low_query, ta=True) + mm(ddir_key, low_unit, ta=True)
    dunit = (
        ysolve
        - mm(solve, dthrough, tb=True)
        - mm(carried, dkm_low)
        + mm(dqdir, low_query, ta=True)
        + mm(ddir_key, low_key)
        + mm(dgram, low_unit)
        + mm(dgram, low_unit, ta=True)
    )
    along = jnp.sum(dunit * dirs, axis=1, keepdims=True)
    ddirs = norm * dunit - dirs * (norm * norm * norm * along)
    dbeta = -ddiag / jnp.maximum(beta, 1e-30) * (1.0 - 0.5 * beta)
    lane = iota((length, 128), 1)
    mask = place_ref[1]
    for at, part in enumerate((dquery, dkey, dvalue, ddirs)):
        scatter_rows(dproj_ref, slice(at * dim, (at + 1) * dim), part.astype(LOW), mask)
    scatter_rows(dbeta_ref, slice(None), jnp.where(lane == head, dbeta, 0.0).astype(LOW), mask)


def pack_heads(heads, *refs):
    *parts, out_ref = refs
    dim = parts[0].shape[1] // heads
    for head in range(heads):
        for at, part in enumerate(parts):
            start = (head * len(parts) + at) * dim
            out_ref[:, start : start + dim] = part[:, head * dim : (head + 1) * dim]


def prepare(heads, shard, masks, place_ref, tokens_ref, cot_ref, parts_ref, *rest):
    normed_ref, normed_t_ref, tokens_x_ref, cot_x_ref, small_ref, gains_ref, beta_ref, docs_ref, doc_col_ref = rest[:9]
    marks_ref, sems, mark_sems = rest[9:]
    span = marks_ref.shape[0]
    copies = []
    for slot in range(parts_ref.shape[0]):
        mask = sum(part for at, part in enumerate(masks) if slot >> at & 1)
        at = pl.multiple_of((place_ref[2] ^ mask) * shard, 16)
        copies.append(
            pltpu.make_async_copy(parts_ref.at[slot, pl.ds(0, shard), :], small_ref.at[pl.ds(at, shard), :], sems.at[slot])
        )
        if mask < span:
            copies.append(
                pltpu.make_async_copy(
                    parts_ref.at[slot, pl.ds(shard, 16), :], marks_ref.at[place_ref[0] ^ mask], mark_sems.at[mask]
                )
            )
    for copy in copies:
        copy.start()
    for copy in copies:
        copy.wait()
    small = small_ref[...]
    across = small.astype(WIDE).T
    gains_ref[...] = across[0:8]
    gain = across[heads : heads + 1]
    stream = tokens_ref[...].astype(WIDE)
    scale = lax.rsqrt(jnp.mean(stream * stream, axis=-1, keepdims=True) + EPSILON)
    normed_wide = stream * scale * gain
    normed = normed_wide.astype(LOW)
    normed_ref[...] = normed
    beta_ref[...] = mm(normed, small)
    mask = place_ref[1]
    scatter_rows(tokens_x_ref, slice(None), tokens_ref[...], mask)
    scatter_rows(cot_x_ref, slice(None), cot_ref[...], mask)
    for at in range(normed.shape[0] // 128):
        start = pl.multiple_of((mask ^ at) * 128, 128)
        normed_t_ref[:, pl.ds(start, 128)] = normed_wide[at * 128 : (at + 1) * 128].T.astype(LOW)
    all_marks = marks_ref[...].astype(WIDE)
    line = iota(all_marks.shape, 1)
    length = tokens_ref.shape[0]
    marks = jnp.concatenate(
        [jnp.sum(jnp.where(line == at, all_marks, 0.0), axis=1) for at in range(length // 128)], axis=1
    )
    upper = jnp.where(iota((length, length), 0) <= iota((length, length), 1), 1.0, 0.0)
    docs = mm(marks, upper)
    row = iota(docs.shape, 0)
    before = jnp.zeros_like(docs)
    for at in range(span - 1):
        before = before + jnp.where(row > at, docs[at : at + 1, length - 1 : length], 0.0)
    docs = docs + before
    docs_ref[...] = docs
    own = jnp.sum(jnp.where(row == place_ref[0], docs, 0.0), axis=0, keepdims=True)
    eye = iota((length, length), 0) == iota((length, length), 1)
    column = jnp.sum(jnp.where(eye, own, 0.0), axis=1, keepdims=True)
    doc_col_ref[...] = jnp.broadcast_to(column, doc_col_ref.shape)


def branch_forward(heads, dim, tokens_x_ref, gains_ref, w_out_ref, *rest):
    *pieces, middle_ref, normed_ref, att_ref = rest
    for at, part in enumerate(pieces):
        att_ref[:, at * dim : (at + 1) * dim] = part[...]
    middle = tokens_x_ref[...].astype(WIDE) + mm(att_ref[...], w_out_ref[...], tb=True)
    middle_ref[...] = middle
    scale = lax.rsqrt(jnp.mean(middle * middle, axis=-1, keepdims=True) + EPSILON)
    normed_ref[...] = (middle * scale * gains_ref[heads + 1 : heads + 2]).astype(LOW)


def mlp_forward(cot_ref, gate_ref, up_ref, down_ref, *rest):
    ways = (len(rest) - 3) // 2
    pieces, outs = rest[:ways], rest[ways + 1 : -2]
    all_ref, normed_ref, acc_ref = rest[ways], rest[-2], rest[-1]
    step = pl.program_id(0)
    chunk = pieces[0].shape[0]

    @pl.when(step == 0)
    def start():
        for at, part in enumerate(pieces):
            normed_ref[at * chunk : (at + 1) * chunk, :] = part[...]
        acc_ref[...] = jnp.zeros_like(acc_ref)

    normed = normed_ref[...]
    gate, up, d_hidden = mm(normed, gate_ref[...]), mm(normed, up_ref[...]), mm(cot_ref[...], down_ref[...])
    sig = jax.nn.sigmoid(gate)
    silu = gate * sig
    d_gate = (d_hidden * up * sig * (1.0 + gate * (1.0 - sig))).astype(LOW)
    d_up = (d_hidden * silu).astype(LOW)
    all_ref[0] = d_gate
    all_ref[1] = d_up
    all_ref[2] = (silu * up).astype(LOW)
    acc_ref[...] += mm(d_gate, gate_ref[...], tb=True) + mm(d_up, up_ref[...], tb=True)

    @pl.when(step == pl.num_programs(0) - 1)
    def finish():
        for at, part in enumerate(outs):
            part[...] = acc_ref[at * chunk : (at + 1) * chunk, :].astype(LOW)


def mlp_grads(cot_ref, near_ref, far_ref, down_ref, middle_ref, *rest):
    ways = (len(rest) - 3) // 2
    pieces, grad_ref, outs, left_ref, acc_ref = rest[:ways], rest[ways], rest[ways + 1 : -2], rest[-2], rest[-1]
    step, third = pl.program_id(0), pl.num_programs(0) // 3
    chunk = pieces[0].shape[0]

    @pl.when(step == 0)
    def start():
        for at, part in enumerate(pieces):
            left_ref[:, at * chunk : (at + 1) * chunk] = part[...].astype(WIDE).T.astype(LOW)
        acc_ref[...] = jnp.zeros_like(acc_ref)
        acc_ref[0:chunk, :] = middle_ref[...]

    @pl.when(step == 2 * third)
    def turn():
        for at in range(ways):
            part = cot_ref[at * chunk : (at + 1) * chunk, :]
            left_ref[:, at * chunk : (at + 1) * chunk] = part.astype(WIDE).T.astype(LOW)

    right = jnp.concatenate([near_ref[0], far_ref[0]], axis=0)
    grad_ref[...] = mm(left_ref[...], right).astype(LOW)

    @pl.when(step >= 2 * third)
    def down():
        acc_ref[...] += mm(right, down_ref[...], tb=True)

    @pl.when(step == 3 * third - 1)
    def finish():
        for at, part in enumerate(outs):
            part[...] = acc_ref[at * chunk : (at + 1) * chunk, :].astype(LOW)


def branch_backward(heads, inner, middle_ref, gains_ref, cot_ref, w_out_ref, *rest):
    ways = (len(rest) - 4) // 2
    backs, d_middle_ref, gain_ref, upper_ref, lower_ref, d_atts = rest[:ways], *rest[ways : ways + 4], rest[ways + 4 :]
    grad = total([part[...] for part in backs])
    middle = middle_ref[...]
    scale = lax.rsqrt(jnp.mean(middle * middle, axis=-1, keepdims=True) + EPSILON)
    gain_ref[...] = jnp.broadcast_to(jnp.sum(grad * middle * scale, axis=0, keepdims=True), gain_ref.shape)
    d_middle = cot_ref[...].astype(WIDE) + norm_back(grad, middle, scale, gains_ref[heads + 1 : heads + 2])
    d_middle_ref[...] = d_middle
    d_branch = d_middle.astype(LOW)
    half = upper_ref.shape[0]
    upper_ref[...] = d_branch[:half]
    lower_ref[...] = d_branch[half:]
    for at, part in enumerate(d_atts):
        part[...] = mm(d_branch, w_out_ref[:, at * inner : (at + 1) * inner]).astype(LOW)


def project_back(heads, tokens_x_ref, small_ref, w_ref, gain_two_ref, part_ref, d_proj_ref, *rest):
    d_betas, (gain_ref, d_beta_ref, *outs) = rest[:heads], rest[heads:]
    d_beta = total([part[...] for part in d_betas]).astype(LOW)
    d_beta_ref[...] = d_beta
    back = part_ref[...] + mm(d_beta, small_ref[...], tb=True) + mm(d_proj_ref[...], w_ref[...], tb=True)
    stream = tokens_x_ref[...].astype(WIDE)
    scale = lax.rsqrt(jnp.mean(stream * stream, axis=-1, keepdims=True) + EPSILON)
    gain = jnp.sum(back * stream * scale, axis=0, keepdims=True)
    gain_ref[...] = jnp.where(iota(gain_ref.shape, 0) == 0, gain, gain_two_ref[...])
    chunk = outs[0].shape[0]
    for at, part in enumerate(outs):
        part[...] = back[at * chunk : (at + 1) * chunk].astype(LOW)


def token_grad(heads, tokens_x_ref, gains_ref, d_middle_ref, *rest):
    *backs, out_ref = rest
    grad = total([part[...] for part in backs])
    stream = tokens_x_ref[...].astype(WIDE)
    scale = lax.rsqrt(jnp.mean(stream * stream, axis=-1, keepdims=True) + EPSILON)
    out_ref[...] = (d_middle_ref[...] + norm_back(grad, stream, scale, gains_ref[heads : heads + 1])).astype(LOW)


def token_join(place_ref, *rest):
    *pieces, out_ref = rest
    chunk = pieces[0].shape[0]
    for at, part in enumerate(pieces):
        start = pl.multiple_of((place_ref[1] ^ at) * chunk, chunk)
        out_ref[pl.ds(start, chunk), :] = part[...].astype(out_ref.dtype)


def weight_grads(left_ref, d_proj_ref, *rest):
    rest[-1][...] = mm(left_ref[...], d_proj_ref[...]).astype(LOW)


def out_grads(heads, ways, *rest):
    branches, atts, out_ref, turned_ref = rest[:ways], rest[ways : ways + heads], rest[-2], rest[-1]
    step = pl.program_id(0)
    chunk = 2 * branches[0].shape[0]

    @pl.when(step == 0)
    def turn():
        for at in range(ways // 2):
            part = jnp.concatenate([branches[2 * at][...], branches[2 * at + 1][...]], axis=0)
            turned_ref[:, at * chunk : (at + 1) * chunk] = part.astype(WIDE).T.astype(LOW)

    for head in range(heads):

        @pl.when(step == head)
        def one(head=head):
            out_ref[...] = mm(turned_ref[...], atts[head][...]).astype(LOW)


def small_grads(heads, ways, left_ref, d_beta_ref, *rest):
    gains, out_ref, rows_ref = rest[:ways], rest[-2], rest[-1]
    gain = total([part[...] for part in gains])
    rows_ref[...] = jnp.zeros_like(rows_ref)
    rows_ref[heads : heads + 1, :] = gain[0:1]
    rows_ref[heads + 1 : heads + 2, :] = gain[1:2]
    out_ref[...] = (mm(left_ref[...], d_beta_ref[...]) + rows_ref[...].T).astype(LOW)


def project_more(d_proj_ref, w_ref, *rest):
    part = mm(d_proj_ref[...], w_ref[...], tb=True)
    if len(rest) > 1:
        part = rest[0][...] + part
    rest[-1][...] = part


def grad_join(heads, dim, in_ref, *outs):
    width = 4 * dim
    for head in range(heads):
        for kind, out in enumerate(outs[:4]):
            at = head * width + kind * dim
            out[:, head * dim : (head + 1) * dim] = in_ref[:, at : at + dim].astype(WIDE)
    outs[4][...] = in_ref[:, heads * width : heads * width + 128].astype(WIDE)
    outs[5][...] = in_ref[:, heads * width + 128 :].astype(WIDE)


def fixed(shape):
    return pl.BlockSpec(shape, lambda *unused: (0,) * len(shape))


def column_at(shape, at):
    return pl.BlockSpec(shape, lambda *unused: (0, at))


ANYWHERE = pl.BlockSpec(memory_space=pl.ANY)
SCALARS = pl.BlockSpec(memory_space=pltpu.SMEM)


def run(kernel, name, ins, specs, outs, scratch=(), flops=10**9):
    return pl.pallas_call(
        kernel,
        grid=(1,),
        in_specs=specs,
        out_specs=[fixed(shape) for shape, unused in outs],
        out_shape=[jax.ShapeDtypeStruct(shape, dtype) for shape, dtype in outs],
        scratch_shapes=list(scratch),
        compiler_params=pltpu.CompilerParams(vmem_limit_bytes=VMEM_BYTES),
        cost_estimate=pl.CostEstimate(flops=flops, bytes_accessed=4 * 2**20, transcendentals=2**18),
        name=name,
    )(*ins)


def whole(*arrays):
    return [fixed(array.shape) for array in arrays]


def run_block_forward(places, normed, w_in, at, beta_raw, doc_col, doc_row, dim, head):
    length, width = normed.shape
    square, tall = (length, length), (length, dim)
    return run(
        block_forward,
        "block_forward",
        (places, normed, w_in, beta_raw, doc_col, doc_row),
        [SCALARS, *whole(normed), column_at((width, 4 * dim), at), *whole(beta_raw, doc_col, doc_row)],
        [
            ((length, 4 * dim), WIDE),
            ((2 * length + dim, dim), LOW),
            (tall, WIDE),
            (square, WIDE),
            (square, LOW),
            (square, LOW),
            (square, LOW),
            (tall, LOW),
            ((length, 128), WIDE),
            (tall, WIDE),
        ],
        flops=10**10,
    )


def run_cross_forward(places, q_moved, stats, acc, doc_col, docs, packs, swapped):
    length, dim = q_moved.shape
    ins = (q_moved, stats, acc, doc_col, docs)
    return run(
        functools.partial(cross_forward, swapped),
        "cross_forward",
        (places, *ins, *packs),
        [SCALARS, *whole(*ins), ANYWHERE, ANYWHERE],
        [((length, dim), WIDE), ((length, dim), LOW), ((length, dim), WIDE)],
        [
            pltpu.VMEM((SPAN,) + packs[0].shape[1:], LOW),
            pltpu.VMEM((length, dim), WIDE),
            pltpu.VMEM((SPAN - 1, length, length), WIDE),
            pltpu.VMEM((length, 128), WIDE),
            pltpu.SemaphoreType.DMA((2,)),
        ],
        flops=10**10,
    )


def run_cross_backward(places, q_moved, scores, attention, log_total, doc_col, docs, packs, d_atts, head, swapped):
    length, dim = q_moved.shape
    ins = (q_moved, scores, attention, log_total, doc_col, docs)
    both = (SPAN,) + packs[0].shape[1:]
    return run(
        functools.partial(cross_backward, swapped),
        "cross_backward",
        (places, *ins, *packs, *d_atts),
        [SCALARS, *whole(*ins), ANYWHERE, ANYWHERE] + [column_at((part.shape[0], dim), head) for part in d_atts],
        [(packs[0].shape, LOW)] * 2 + [((length, dim), WIDE), ((length, length), LOW), ((length, dim), WIDE)],
        [
            pltpu.VMEM(both, LOW),
            pltpu.VMEM(both, LOW),
            pltpu.VMEM((SPAN + 1, length, dim), WIDE),
            pltpu.VMEM((SPAN, length, dim), WIDE),
            pltpu.VMEM((length, dim), LOW),
            pltpu.VMEM((length, length), WIDE),
            pltpu.SemaphoreType.DMA((2,)),
        ],
        flops=10**10,
    )


def run_block_backward(places, proj, beta_raw, kept, d_packs, head, dim):
    length = proj.shape[0]
    ins = (proj, beta_raw, *kept, *d_packs)
    return run(
        block_backward,
        "block_backward",
        (places, *ins),
        [SCALARS, *whole(*ins)],
        [(proj.shape, LOW), ((length, 128), LOW)],
        flops=5 * 10**9,
    )


def norm_back(grad, value, scale, gain):
    weighted = grad * gain
    return scale * weighted - value * scale * scale * scale * jnp.mean(weighted * value, axis=-1, keepdims=True)


def total(parts):
    out = parts[0].astype(WIDE)
    for part in parts[1:]:
        out = out + part.astype(WIDE)
    return out


def per_device(
    tokens, cotangent, starts, gain_attn, w_query, w_key, w_value, w_dir, w_beta, w_out, gain_mlp, w_gate, w_up, w_down
):
    row_count, width = tokens.shape
    shard, inner = w_query.shape
    hidden_units = w_gate.shape[1]
    heads = w_beta.shape[1]
    dim = inner // heads
    count = lax.axis_size("seq")
    ways = lax.axis_size("head")
    chunk = row_count // ways
    seq_place, head_place = lax.axis_index("seq"), lax.axis_index("head")
    places = jnp.stack([seq_place % SPAN, head_place, seq_place]).astype(jnp.int32)
    places_of = [jnp.concatenate([places, jnp.full((1,), head, jnp.int32)]) for head in range(heads)]

    def to_heads(parts):
        return [xor_move(part, "head", at) if at else part for at, part in enumerate(parts)]

    def over_heads(part):
        return to_heads([part] * ways)

    small = jnp.concatenate([w_beta, gain_attn[:, None], gain_mlp[:, None]], axis=1)
    small = jnp.pad(small, ((0, 0), (0, 128 - heads - 2)))
    marks = jnp.pad(starts.astype(LOW).reshape(row_count // 128, 128), ((0, 16 - row_count // 128), (0, 0)))
    masks = tuple(2 << at for at in range((count // 2).bit_length() - 1)) + (1,)
    small = doubled(jnp.concatenate([small, marks], axis=0), masks)
    four = (w_query, w_key, w_value, w_dir)
    (packed,) = run(functools.partial(pack_heads, heads), "pack_heads", four, whole(*four), [((shard, 4 * inner), LOW)])
    w_in = lax.all_gather(packed, "seq", axis=0, tiled=True)
    out_parts = jnp.concatenate(over_heads(w_out.T), axis=1)

    tall, wide_tall, part_low = (row_count, width), (width, row_count), ((chunk, width), LOW)
    normed, normed_x_t, tokens_x, cot_x, small_all, gains, beta_raw, docs, doc_col = run(
        functools.partial(prepare, heads, shard, masks),
        "prepare",
        (places, tokens, cotangent, small),
        [SCALARS, *whole(tokens, cotangent), ANYWHERE],
        [
            (tall, LOW),
            (wide_tall, LOW),
            (tall, LOW),
            (tall, LOW),
            ((width, 128), LOW),
            ((8, width), WIDE),
            ((row_count, 128), WIDE),
            ((SPAN, row_count), WIDE),
            ((row_count, 128), WIDE),
        ],
        [
            pltpu.VMEM((SPAN, 16, 128), LOW),
            pltpu.SemaphoreType.DMA((count,)),
            pltpu.SemaphoreType.DMA((SPAN,)),
        ],
    )
    normed, out_parts = lax.optimization_barrier((normed, out_parts))
    w_out_x = lax.all_gather(after(out_parts, w_in), "seq", axis=0, tiled=True)

    orders = [(2, 4)] * heads
    first, mixed, ready, full = [], [], {}, {}

    def step(kind, head):
        return (head, kind, xor_move(ready[head], "seq", orders[head][kind] if kind < 2 else 1))

    def meet(outs, moves):
        outs, arrived = lax.optimization_barrier((outs, [move[2] for move in moves]))
        for (head, kind, unused), part in zip(moves, arrived):
            ready[head] = (ready[head], part) if kind == 2 else jnp.concatenate([ready[head], part], axis=0)
        return outs

    flying = []
    for head in range(heads):
        held = normed if head == 0 else after(normed, first[-1][2])
        outs = run_block_forward(places_of[head], held, w_in, head, beta_raw, doc_col, docs, dim, head)
        first.append(meet(outs, flying))
        ready[head] = first[head][1][None]
        flying = [step(at, head - at) for at in range(max(0, head - 2), head + 1)]
    rest_in = jnp.concatenate([w_gate, w_up, w_down.T], axis=1)
    stage = {move[0]: move[1] for move in flying}
    for head in range(heads):
        kept = first[head]
        while stage.get(head, 2) < 2 or any(move[0] == head for move in flying):
            now = [move for move in flying if move[0] == head]
            flying = [move for move in flying if move[0] != head]
            meet((), now)
            if stage[head] < 2:
                stage[head] += 1
                flying.append(step(stage[head], head))
        if head == 0:
            held = kept[2]
        else:
            held = after(kept[2], mixed[-1][0])
        outs = run_cross_forward(places, held, kept[8], kept[9], doc_col, docs, ready[head], False)
        mixed.append(meet(outs, flying))
        flying = []
        for later in range(head + 1, heads):
            if stage[later] < 2:
                stage[later] += 1
                flying.append(step(stage[later], later))
        if head == 0:
            w_rest = lax.all_gather(after(rest_in, mixed[0][0], w_out_x), "seq", axis=0, tiled=True)
    packs = [ready[head] for head in range(heads)]

    att_x = jnp.concatenate([part[1] for part in mixed], axis=1)
    att_parts = to_heads([att_x[at * chunk : (at + 1) * chunk] for at in range(ways)])
    own_rows = fixed((chunk, width))
    middle, normed_two = run(
        functools.partial(branch_forward, heads, inner),
        "branch_forward",
        (tokens_x, gains, w_out_x, *att_parts),
        [own_rows, *whole(gains, w_out_x, *att_parts)],
        [((chunk, width), WIDE), part_low],
        [pltpu.VMEM((chunk, ways * inner), LOW)],
    )
    two_parts = over_heads(normed_two)

    blocks = 2
    cols = hidden_units // blocks

    def mlp_half(parts, at):
        rows = chunk * len(parts)
        return pl.pallas_call(
            mlp_forward,
            grid=(blocks,),
            in_specs=[
                pl.BlockSpec((rows, width), lambda step: (at, 0)),
                pl.BlockSpec((width, cols), lambda step: (0, step)),
                pl.BlockSpec((width, cols), lambda step: (0, blocks + step)),
                pl.BlockSpec((width, cols), lambda step: (0, 2 * blocks + step)),
                *whole(*parts),
            ],
            out_specs=[pl.BlockSpec((3, rows, cols), lambda step: (0, 0, step))] + [fixed((chunk, width))] * len(parts),
            out_shape=[jax.ShapeDtypeStruct((3, rows, hidden_units), LOW)]
            + [jax.ShapeDtypeStruct((chunk, width), LOW)] * len(parts),
            scratch_shapes=[pltpu.VMEM((rows, width), LOW), pltpu.VMEM((rows, width), WIDE)],
            compiler_params=pltpu.CompilerParams(vmem_limit_bytes=VMEM_BYTES),
            cost_estimate=pl.CostEstimate(flops=5 * 10**9, bytes_accessed=2**24, transcendentals=2**19),
            name="mlp_forward",
        )(cot_x, w_rest, w_rest, w_rest, *parts)

    near_all, *near_backs = mlp_half(two_parts[: ways // 2], 0)
    (near_all, near_backs), far_two = lax.optimization_barrier(((near_all, near_backs), two_parts[ways // 2 :]))
    near_moves = [xor_move(part, "head", at) if at else part for at, part in enumerate(near_backs)]
    far_all, *far_backs = mlp_half([after(part, near_all) for part in far_two], 1)
    (far_all, far_backs), near_moves = lax.optimization_barrier(((far_all, far_backs), near_moves))
    two_parts = two_parts[: ways // 2] + list(far_two)
    backs = near_moves + [xor_move(part, "head", ways // 2 + at) for at, part in enumerate(far_backs)]
    grad_mlp, *mlp_parts = pl.pallas_call(
        mlp_grads,
        grid=(3 * blocks,),
        in_specs=[
            fixed(tall),
            pl.BlockSpec((1, row_count // 2, cols), lambda step: (step // blocks, 0, step % blocks)),
            pl.BlockSpec((1, row_count // 2, cols), lambda step: (step // blocks, 0, step % blocks)),
            pl.BlockSpec((width, cols), lambda step: (0, jnp.maximum(step, 2 * blocks))),
            fixed((chunk, width)),
            *whole(*two_parts),
        ],
        out_specs=[pl.BlockSpec((width, cols), lambda step: (0, step))] + [fixed((chunk, width))] * ways,
        out_shape=[jax.ShapeDtypeStruct((width, 3 * hidden_units), LOW)]
        + [jax.ShapeDtypeStruct((chunk, width), LOW)] * ways,
        scratch_shapes=[pltpu.VMEM(wide_tall, LOW), pltpu.VMEM(tall, WIDE)],
        compiler_params=pltpu.CompilerParams(vmem_limit_bytes=VMEM_BYTES),
        cost_estimate=pl.CostEstimate(flops=10**10, bytes_accessed=2**24, transcendentals=0),
        name="mlp_grads",
    )(cot_x, near_all, far_all, w_rest, middle, *two_parts)
    grad_mlp, mlp_parts, backs = lax.optimization_barrier((grad_mlp, mlp_parts, backs))
    reduced_mlp = lax.psum_scatter(grad_mlp, "seq", scatter_dimension=0, tiled=True)

    d_middle, gain_two_sum, upper, lower, *d_atts = run(
        functools.partial(branch_backward, heads, inner),
        "branch_backward",
        (middle, gains, cot_x, w_out_x, *backs),
        [*whole(middle, gains), own_rows, *whole(w_out_x, *backs)],
        [((chunk, width), WIDE), ((8, width), WIDE)] + [((chunk // 2, width), LOW)] * 2 + [((chunk, inner), LOW)] * ways,
    )
    d_atts = to_heads(d_atts)

    def add(left, right):
        return (left.astype(WIDE) + right.astype(WIDE)).astype(LOW)

    second, low_sums, high_sums, last_sums, branch_parts = [], {}, {}, {}, [upper, lower]
    core, across = {}, {}
    halves_two = [after(part, *d_atts[1:]) for part in (upper, lower)]
    branch_moves = [(part, at) for at in range(1, ways) for part in halves_two]
    shares = [2] + [1] * (2 * heads - 3)

    def branch_next():
        some = shares.pop(0) if shares else len(branch_moves)
        out = [xor_move(part, "head", at) for part, at in branch_moves[:some]]
        del branch_moves[:some]
        return out

    for head in range(heads):
        kept = first[head]
        held = kept[2] if head == 0 else after(kept[2], second[-1][0])
        flying = (core.get(head - 1), across.get(head - 2), branch_next())
        outs = run_cross_backward(
            places, held, kept[3], mixed[head][0], mixed[head][2], doc_col, docs, packs[head], d_atts, head, False
        )
        outs, (core_in, across_in, branch_in) = lax.optimization_barrier((outs, flying))
        even, odd, *rest = outs
        second.append(rest)
        branch_parts += branch_in
        if head >= 2:
            last_sums[head - 2] = [add(low_sums[head - 2][at], across_in[at]) for at in range(2)]
        if head >= 1:
            high_sums[head - 1] = add(low_sums[head - 1][2:], core_in[2:])
            across[head - 1] = xor_move(high_sums[head - 1], "seq", orders[head - 1][1])
            low_sums[head - 1] = add(low_sums[head - 1][:2], core_in[:2])
        low_sums[head] = even
        core[head] = xor_move(odd, "seq", 1)
    mlp_rows = jnp.stack(mlp_parts)
    mlp_rows = jnp.concatenate([lax.dynamic_index_in_dim(mlp_rows, head_place ^ at, 0, False) for at in range(ways)])
    result = lax.psum(after(mlp_rows, reduced_mlp, second[-1][0]), "head")

    cols = 4 * dim
    grad_in = None

    def grads_into(kernel, ins, specs, at, grid, name, scratch=()):
        given = () if grad_in is None else (grad_in,)
        return pl.pallas_call(
            kernel,
            grid=(grid,),
            in_specs=specs + [ANYWHERE] * len(given),
            out_specs=at,
            out_shape=jax.ShapeDtypeStruct((width, (heads + 1) * cols), LOW),
            input_output_aliases={len(ins): 0} if given else {},
            scratch_shapes=list(scratch),
            compiler_params=pltpu.CompilerParams(vmem_limit_bytes=VMEM_BYTES),
            cost_estimate=pl.CostEstimate(flops=10**9, bytes_accessed=2**22, transcendentals=0),
            name=name,
        )(*ins, *given)

    d_projs, d_betas = [], []
    back_part = None
    for head in range(heads):
        if head not in last_sums:
            last_sums[head] = [add(low_sums[head][at], across[head][at]) for at in range(2)]
        near_sum, far_sum = last_sums[head]
        sent = [near_sum, xor_move(far_sum, "seq", orders[head][0])]
        if head >= 1:
            grad_in = grads_into(
                weight_grads,
                (normed_x_t, d_projs[-1]),
                whole(normed_x_t, d_projs[-1]),
                column_at((width, cols), head - 1),
                1,
                "weight_grads",
            )
            ins = (d_projs[-1], w_in) + (() if back_part is None else (back_part,))
            (back_part,) = run(
                project_more,
                "project_more",
                ins,
                [*whole(d_projs[-1]), column_at((width, cols), head - 1), *whole(*ins[2:])],
                [(tall, WIDE)],
            )
            if head == heads - 1:
                atts = [part[1] for part in mixed]
                grad_in = grads_into(
                    functools.partial(out_grads, heads, len(branch_parts)),
                    (*branch_parts, *atts),
                    whole(*branch_parts, *atts),
                    pl.BlockSpec((width, 128), lambda step: (0, heads * cols // 128 + 1 + step)),
                    heads,
                    "out_grads",
                    [pltpu.VMEM(wide_tall, LOW)],
                )
            grad_in, back_part, sent = lax.optimization_barrier((grad_in, back_part, sent))
        late = heads - 1 if head == 0 and heads - 1 not in across else None
        flying = (across.get(head + 1), core[late] if late else None, branch_next() if head + 1 < heads else [])
        proj, inverse, carried, qdir, solve = (first[head][at] for at in (0, 4, 5, 6, 7))
        if head == 0:
            proj, reduced_mlp = lax.optimization_barrier((proj, reduced_mlp))
        outs = run_block_backward(
            places_of[head], proj, beta_raw, (inverse, carried, qdir, solve, *second[head]), sent, head, dim
        )
        (d_proj, d_beta), (across_in, core_in, branch_in) = lax.optimization_barrier((outs, flying))
        branch_parts += branch_in
        if across_in is not None:
            across[head + 1] = across_in
        if late:
            across[late] = xor_move(add(low_sums[late][2:], core_in[2:]), "seq", orders[late][1])
            low_sums[late] = add(low_sums[late][:2], core_in[:2])
        d_projs.append(d_proj)
        d_betas.append(d_beta)
    back_ins = (tokens_x, small_all, w_in, gain_two_sum, back_part, d_projs[-1], *d_betas)
    gain_sums, d_beta, *backs = run(
        functools.partial(project_back, heads),
        "project_back",
        back_ins,
        [
            *whole(tokens_x, small_all),
            column_at((width, cols), heads - 1),
            *whole(*back_ins[3:]),
        ],
        [((8, width), WIDE), ((row_count, 128), LOW)] + [part_low] * ways,
    )
    backs = to_heads(backs)
    (d_tokens_own,) = run(
        functools.partial(token_grad, heads),
        "token_grad",
        (tokens_x, gains, d_middle, *backs),
        [own_rows, *whole(gains, d_middle, *backs)],
        [part_low],
    )
    token_parts = over_heads(d_tokens_own)
    grad_in = grads_into(
        weight_grads,
        (normed_x_t, d_projs[-1]),
        whole(normed_x_t, d_projs[-1]),
        column_at((width, cols), heads - 1),
        1,
        "weight_grads",
    )
    gain_parts = over_heads(gain_sums)
    ins = (normed_x_t, d_beta, *gain_parts)
    grad_in = grads_into(
        functools.partial(small_grads, heads, ways),
        ins,
        whole(*ins),
        column_at((width, 128), heads * cols // 128),
        1,
        "small_grads",
        [pltpu.VMEM((128, width), WIDE)],
    )
    grad_in, result = lax.optimization_barrier((grad_in, result))
    reduced_in = lax.psum_scatter(grad_in, "seq", scatter_dimension=0, tiled=True)
    *grads, small_sum, grad_out_t = run(
        functools.partial(grad_join, heads, dim),
        "grad_join",
        (reduced_in,),
        whole(reduced_in),
        [((shard, inner), WIDE)] * 4 + [((shard, 128), WIDE), ((shard, inner), WIDE)],
    )
    reduced_mlp = reduced_mlp.astype(WIDE)
    finished = (
        *grads,
        small_sum,
        grad_out_t.T,
        reduced_mlp[:, :hidden_units],
        reduced_mlp[:, hidden_units : 2 * hidden_units],
        reduced_mlp[:, 2 * hidden_units :].T,
    )
    finished, token_parts = lax.optimization_barrier((finished, token_parts))
    *grads, small_sum, grad_out, grad_gate, grad_up, grad_down = finished
    (d_tokens,) = run(
        token_join, "token_join", (places, *token_parts), [SCALARS, *whole(*token_parts)], [(tall, WIDE)]
    )
    return (
        result,
        d_tokens,
        small_sum[:, heads],
        *grads,
        small_sum[:, :heads],
        grad_out,
        small_sum[:, heads + 1],
        grad_gate,
        grad_up,
        grad_down,
    )


def solution(mesh):
    placed = (
        P("seq", None),
        P("seq", None),
        P("seq"),
        P("seq"),
        P("seq", "head"),
        P("seq", "head"),
        P("seq", "head"),
        P("seq", "head"),
        P("seq", "head"),
        P("head", "seq"),
        P("seq"),
        P("seq", "head"),
        P("seq", "head"),
        P("head", "seq"),
    )
    return jax.shard_map(
        per_device,
        mesh=mesh,
        in_specs=placed,
        out_specs=(
            P("seq", None),
            P("seq", None),
            P("seq"),
            P("seq", "head"),
            P("seq", "head"),
            P("seq", "head"),
            P("seq", "head"),
            P("seq", "head"),
            P("head", "seq"),
            P("seq"),
            P("seq", "head"),
            P("seq", "head"),
            P("head", "seq"),
        ),
        check_vma=False,
    )
```

```python
import functools

import jax
import jax.numpy as jnp
from jax import lax
from jax.experimental import pallas as pl
from jax.experimental.pallas import tpu as pltpu
from jax.sharding import PartitionSpec as P

SPAN = 8
EPSILON = 1e-06
NEGATIVE = -1e30
LOG2E = 1.4426950408889634
LOW = jnp.bfloat16
WIDE = jnp.float32
VMEM_BYTES = 36 * 2**20


def mm(left, right, ta=False, tb=False):
    dims = (((0 if ta else 1,), (1 if tb else 0,)), ((), ()))
    return lax.dot_general(
        left.astype(LOW), right.astype(LOW), dims, preferred_element_type=WIDE
    )


def halves(value):
    high = value.astype(LOW)
    return high, (value - high.astype(WIDE)).astype(LOW)


def mm3(left, right, ta=False, tb=False):
    left_hi, left_lo = left if isinstance(left, tuple) else halves(left)
    right_hi, right_lo = right if isinstance(right, tuple) else halves(right)
    return mm(left_hi, right_hi, ta, tb) + (mm(left_hi, right_lo, ta, tb) + mm(left_lo, right_hi, ta, tb))


def iota(shape, axis):
    return lax.broadcasted_iota(jnp.int32, shape, axis)


def lower_inverse(strict, beta):
    length = strict.shape[0]
    size = 128
    row, col = iota((size, size), 0), iota((size, size), 1)
    subs, blocks = [], []
    for at in range(0, length, size):
        sub = strict[at : at + size, at : at + size]
        scale = beta[at : at + size]
        diag = jnp.where(row == col, scale, 0.0)
        across = jnp.sum(diag, axis=0, keepdims=True)
        pair = ((row >> 1) == (col >> 1)) & (row > col)
        subs.append(sub)
        blocks.append(diag - jnp.where(pair, sub * scale * across, 0.0))
    bit = 1
    while (1 << bit) < size:
        mask = ((row >> (bit + 1)) == (col >> (bit + 1))) & ((row >> bit) != (col >> bit)) & (row > col)
        right = [mm3(jnp.where(mask, sub, 0.0), block) for sub, block in zip(subs, blocks)]
        blocks = [block - mm3(block, part) for block, part in zip(blocks, right)]
        bit += 1
    while len(blocks) > 1:
        size = blocks[0].shape[0]
        joined = []
        for pair_at in range(len(blocks) // 2):
            first, second = blocks[2 * pair_at], blocks[2 * pair_at + 1]
            at = 2 * pair_at * size
            corner = -mm3(second, mm3(strict[at + size : at + 2 * size, at : at + size], first))
            joined.append(
                jnp.concatenate(
                    [
                        jnp.concatenate([first, jnp.zeros_like(first)], axis=1),
                        jnp.concatenate([corner, second], axis=1),
                    ],
                    axis=0,
                )
            )
        blocks = joined
    return blocks[0]


def xor_move(value, axis, mask):
    return lax.ppermute(value, axis, [(at, at ^ mask) for at in range(lax.axis_size(axis))])


def after(value, *others):
    return lax.optimization_barrier((value, *others))[0]


def doubled_again(held, mask):
    return jnp.concatenate([held, xor_move(held, "seq", mask)], axis=0)


def doubled(block, masks):
    held = block[None]
    for mask in masks:
        held = doubled_again(held, mask)
    return held


def block_forward(
    place_ref, normed_ref, w_ref, beta_ref, doc_col_ref, doc_row_ref,
    proj_ref, pack_ref, qm_ref, score_ref, inv_ref, carried_ref, qdir_ref, solve_ref, stat_ref, acc_ref,
):
    proj_ref[...] = mm(normed_ref[...], w_ref[...])
    length, dim = qm_ref.shape
    query, key = proj_ref[:, 0:dim], proj_ref[:, dim : 2 * dim]
    value, dirs = proj_ref[:, 2 * dim : 3 * dim].astype(LOW), proj_ref[:, 3 * dim :]
    head = place_ref[3]
    beta = 2.0 * jax.nn.sigmoid(jnp.sum(jnp.where(iota((length, 128), 1) == head, beta_ref[...], 0.0), axis=1, keepdims=True))
    unit = dirs * lax.rsqrt(jnp.sum(dirs * dirs, axis=-1, keepdims=True) + EPSILON)
    row, col = iota((length, length), 0), iota((length, length), 1)
    unit_two = halves(unit)
    strict = jnp.where(row > col, mm3(unit_two, unit_two, tb=True), 0.0)
    inverse = lower_inverse(strict, beta)
    inverse_two = halves(inverse)
    solve = mm3(inverse_two, unit_two)
    solve_two = halves(solve)
    dir_key = jnp.where(row > col, mm3(unit_two, key, tb=True), 0.0)
    carried = mm3(inverse_two, dir_key)
    carried_two = halves(carried)
    qdir = jnp.where(row >= col, mm3(query, unit_two, tb=True), 0.0)
    qdir_two = halves(qdir)
    qm_ref[...] = query - mm3(qdir_two, solve_two)
    pack_ref[0:length, :] = (key - mm3(carried_two, unit_two, ta=True)).astype(LOW)
    pack_ref[length : 2 * length, :] = value
    eye = jnp.where(iota((dim, dim), 0) == iota((dim, dim), 1), 1.0, 0.0)
    pack_ref[2 * length :, :] = (eye - mm3(unit_two, solve_two, ta=True)).astype(LOW)
    inside = mm(query, key, tb=True) - mm(qdir_two[0], carried_two[0])
    inv_ref[...] = inverse.astype(LOW)
    carried_ref[...] = carried_two[0]
    qdir_ref[...] = qdir_two[0]
    solve_ref[...] = solve_two[0]
    allowed = (doc_col_ref[:, 0:1] == doc_row_ref[pl.ds(place_ref[0], 1), :]) & (row >= col)
    score = jnp.where(allowed, inside * (LOG2E * dim**-0.5), NEGATIVE)
    score_ref[...] = score
    peak = jnp.max(score, axis=1, keepdims=True)
    weight = jnp.exp2(score - peak)
    lane = iota((length, 128), 1)
    stat_ref[...] = jnp.where(lane == 0, peak, jnp.sum(weight, axis=1, keepdims=True))
    acc_ref[...] = mm(weight, value)


def bring(halves_in, pack_ref, sems):
    size = halves_in[0].shape[0]
    copies = [
        pltpu.make_async_copy(part, pack_ref.at[pl.ds(at * size, size)], sems.at[at]) for at, part in enumerate(halves_in)
    ]
    for copy in copies:
        copy.start()
    for copy in copies:
        copy.wait()


def slot_of(mask, swapped):
    core, first, second = mask & 1, (mask >> 1) & 1, mask >> 2
    return 4 * core + (2 * first + second if swapped else first + 2 * second)


def cross_forward(
    swapped, place_ref, qm_ref, stat_in_ref, acc_ref, doc_col_ref, doc_row_ref, far_ref, core_ref,
    att_ref, att_x_ref, log_ref, pack_ref, moved_ref, score_ref, peak_ref, sems,
):
    bring((far_ref, core_ref), pack_ref, sems)
    length, dim = qm_ref.shape
    place = place_ref[0]
    moved_ref[...] = qm_ref[...]
    att_ref[...] = acc_ref[...]
    own_peak = stat_in_ref[:, 0:1]
    peak_ref[...] = jnp.broadcast_to(own_peak, (length, 128))

    def look(step, carry):
        at = place - step
        slot = slot_of(place ^ at, swapped)
        moved = moved_ref[...]
        score = mm(moved * (LOG2E * dim**-0.5), pack_ref[slot, 0:length, :], tb=True)
        moved_ref[...] = mm(moved, pack_ref[slot, 2 * length :, :])
        allowed = doc_col_ref[:, 0:1] == doc_row_ref[pl.ds(at, 1), :]
        score = jnp.where(allowed, score, NEGATIVE)
        score_ref[at] = score
        high = peak_ref[...]
        for lane in range(0, length, 128):
            high = jnp.maximum(high, score[:, lane : lane + 128])
        peak_ref[...] = high
        return carry

    def two_looks(pair, carry):
        look(2 * pair + 1, carry)
        return look(2 * pair + 2, carry)

    lax.fori_loop(0, place // 2, two_looks, 0)
    lax.fori_loop(place // 2 * 2 + 1, place + 1, look, 0)
    peak = jnp.max(peak_ref[...], axis=1, keepdims=True)
    rescale = jnp.exp2(own_peak - peak)
    att_ref[...] = att_ref[...] * rescale
    lanes = iota((length, 128), 1)
    moved_ref[...] = jnp.where(lanes == 0, stat_in_ref[:, 1:2] * rescale, 0.0)

    def use(at, carry):
        slot = slot_of(place ^ at, swapped)
        weight = jnp.exp2(score_ref[at] - peak)
        sums = moved_ref[...]
        for lane in range(0, length, 128):
            sums = sums + weight[:, lane : lane + 128]
        moved_ref[...] = sums
        att_ref[...] += mm(weight, pack_ref[slot, length : 2 * length, :])
        return carry

    def two_uses(pair, carry):
        use(2 * pair, carry)
        return use(2 * pair + 1, carry)

    lax.fori_loop(0, place // 2, two_uses, 0)
    lax.fori_loop(place // 2 * 2, place, use, 0)
    total = jnp.sum(moved_ref[...], axis=1, keepdims=True)
    attention = att_ref[...] / total
    att_ref[...] = attention
    scatter_rows(att_x_ref, slice(None), attention.astype(LOW), place_ref[1])
    log_ref[...] = jnp.broadcast_to(peak + jnp.log2(total), (length, 128))


def same_document(doc_row_ref, at, place):
    first = doc_row_ref[pl.ds(at, 1), :][:, 0:1]
    last = doc_row_ref[pl.ds(place, 1), :][:, doc_row_ref.shape[1] - 1 :]
    return jnp.sum(last - first) == 0.0


def scatter_rows(ref, columns, value, mask, chunk=128):
    for at in range(value.shape[0] // chunk):
        start = pl.multiple_of((mask ^ at) * chunk, chunk)
        ref[pl.ds(start, chunk), columns] = value[at * chunk : (at + 1) * chunk]


def cross_backward(swapped, place_ref, qm_ref, score_ref, att_ref, log_ref, doc_col_ref, doc_row_ref, far_ref, core_ref, *rest):
    *datts, even_ref, odd_ref, dqm_ref, dinside_ref, dval_ref = rest[:-7]
    pack_ref, sums_ref, chain_ref, dchain_ref, datt_ref, turned_ref, sems = rest[-7:]
    bring((far_ref, core_ref), pack_ref, sems)
    length, dim = qm_ref.shape
    place = place_ref[0]
    chunk = datts[0].shape[0]
    for at, part in enumerate(datts):
        start = pl.multiple_of((place_ref[1] ^ at) * chunk, chunk)
        datt_ref[pl.ds(start, chunk), :] = part[...]
    scale = dim**-0.5
    datt = datt_ref[...]
    log_total = log_ref[:, 0:1]
    delta = jnp.sum(datt.astype(WIDE) * att_ref[...], axis=1, keepdims=True)
    value = pack_ref[0, length : 2 * length, :]
    probs = jnp.exp2(score_ref[...] - log_total)
    dprob = mm(datt, value, tb=True)
    dinside_ref[...] = (probs * (dprob - delta) * scale).astype(LOW)
    dval_ref[...] = mm(probs, datt, ta=True)
    chain_ref[1] = qm_ref[...]

    def put(slot, rows, part):
        sums_ref[slot, rows, :] = part.astype(LOW)

    def blank(at, carry):
        put(slot_of(place ^ at, swapped), slice(None), jnp.zeros(sums_ref.shape[1:], LOW))
        return carry

    lax.fori_loop(place, SPAN, blank, 0)

    def hop(step, carry):
        at = place - step
        slot = slot_of(place ^ at, swapped)
        moved = chain_ref[step]
        key = pack_ref[slot, 0:length, :]
        value = pack_ref[slot, length : 2 * length, :]
        through = pack_ref[slot, 2 * length :, :]
        chain_ref[step + 1] = mm(moved, through)
        allowed = doc_col_ref[:, 0:1] == doc_row_ref[pl.ds(at, 1), :]
        probs = jnp.exp2(jnp.where(allowed, mm(moved * (LOG2E * scale), key, tb=True), NEGATIVE) - log_total)
        dscore = (probs * (mm(datt, value, tb=True) - delta)).astype(LOW)
        dchain_ref[step] = mm(dscore, key) * scale
        put(slot, slice(0, length), mm(dscore, moved * scale, ta=True))
        put(slot, slice(length, 2 * length), mm(probs, datt, ta=True))
        return carry

    def two_hops(pair, carry):
        hop(2 * pair + 1, carry)
        return hop(2 * pair + 2, carry)

    lax.fori_loop(0, place // 2, two_hops, 0)
    lax.fori_loop(place // 2 * 2 + 1, place + 1, hop, 0)

    def back(count, carry):
        step = place - count
        slot = slot_of(place ^ (place - step), swapped)
        through = pack_ref[slot, 2 * length :, :]
        grad = dqm_ref[...]
        put(slot, slice(2 * length, 2 * length + dim), mm(chain_ref[step], grad, ta=True))
        dqm_ref[...] = dchain_ref[step] + mm(grad, through, tb=True)
        return carry

    dqm_ref[...] = jnp.zeros((length, dim), WIDE)
    lax.fori_loop(0, place, back, 0)
    even_ref[...] = sums_ref[: SPAN // 2]
    odd_ref[...] = sums_ref[SPAN // 2 :]


def block_backward(
    place_ref, proj_ref, beta_ref, inv_ref, carried_ref, qdir_ref, solve_ref, dqm_ref, dinside_ref, dval_ref, *rest
):
    *dpacks, dproj_ref, dbeta_ref = rest
    length, dim = dqm_ref.shape
    query, key, dirs = proj_ref[:, 0:dim], proj_ref[:, dim : 2 * dim], proj_ref[:, 3 * dim :]
    head = place_ref[3]
    beta = 2.0 * jax.nn.sigmoid(jnp.sum(jnp.where(iota((length, 128), 1) == head, beta_ref[...], 0.0), axis=1, keepdims=True))
    norm = lax.rsqrt(jnp.sum(dirs * dirs, axis=-1, keepdims=True) + EPSILON)
    unit = dirs * norm
    low_unit, low_key, low_query = unit.astype(LOW), key.astype(LOW), query.astype(LOW)
    row, col = iota((length, length), 0), iota((length, length), 1)
    inverse, carried, qdir, solve = inv_ref[...], carried_ref[...], qdir_ref[...], solve_ref[...]
    dqm, dinside = dqm_ref[...].astype(LOW), dinside_ref[...]

    def summed(rows):
        return sum(part[rows, :].astype(WIDE) for part in dpacks)

    dkm = summed(slice(0, length))
    dthrough = summed(slice(2 * length, 2 * length + dim)).astype(LOW)
    dvalue = dval_ref[...] + summed(slice(length, 2 * length))
    dkm_low = dkm.astype(LOW)
    dqdir = -jnp.where(row >= col, mm(dqm, solve, tb=True) + mm(dinside, carried, tb=True), 0.0).astype(LOW)
    dquery = dqm_ref[...] + mm(dinside, low_key) + mm(dqdir, low_unit)
    dsolve = -(mm(qdir, dqm, ta=True) + mm(low_unit, dthrough))
    dcarried = -(mm(low_unit, dkm_low, tb=True) + mm(qdir, dinside, ta=True))
    ysolve = mm(inverse, dsolve, ta=True)
    ycarried = mm(inverse, dcarried, ta=True)
    ddir_key = jnp.where(row > col, ycarried, 0.0).astype(LOW)
    dlower = -(mm(ysolve, solve, tb=True) + mm(ycarried, carried, tb=True))
    ddiag = jnp.sum(jnp.where(row == col, dlower, 0.0), axis=1, keepdims=True)
    dgram = jnp.where(row > col, dlower, 0.0).astype(LOW)
    dkey = dkm + mm(dinside, low_query, ta=True) + mm(ddir_key, low_unit, ta=True)
    dunit = (
        ysolve
        - mm(solve, dthrough, tb=True)
        - mm(carried, dkm_low)
        + mm(dqdir, low_query, ta=True)
        + mm(ddir_key, low_key)
        + mm(dgram, low_unit)
        + mm(dgram, low_unit, ta=True)
    )
    along = jnp.sum(dunit * dirs, axis=1, keepdims=True)
    ddirs = norm * dunit - dirs * (norm * norm * norm * along)
    dbeta = -ddiag / jnp.maximum(beta, 1e-30) * (1.0 - 0.5 * beta)
    lane = iota((length, 128), 1)
    mask = place_ref[1]
    for at, part in enumerate((dquery, dkey, dvalue, ddirs)):
        scatter_rows(dproj_ref, slice(at * dim, (at + 1) * dim), part.astype(LOW), mask)
    scatter_rows(dbeta_ref, slice(None), jnp.where(lane == head, dbeta, 0.0).astype(LOW), mask)


def pack_heads(heads, *refs):
    *parts, out_ref = refs
    dim = parts[0].shape[1] // heads
    for head in range(heads):
        for at, part in enumerate(parts):
            start = (head * len(parts) + at) * dim
            out_ref[:, start : start + dim] = part[:, head * dim : (head + 1) * dim]


def prepare(heads, shard, masks, place_ref, tokens_ref, cot_ref, parts_ref, *rest):
    normed_ref, normed_t_ref, tokens_x_ref, cot_x_ref, small_ref, gains_ref, beta_ref, docs_ref, doc_col_ref = rest[:9]
    marks_ref, sems, mark_sems = rest[9:]
    span = marks_ref.shape[0]
    copies = []
    for slot in range(parts_ref.shape[0]):
        mask = sum(part for at, part in enumerate(masks) if slot >> at & 1)
        at = pl.multiple_of((place_ref[2] ^ mask) * shard, 16)
        copies.append(
            pltpu.make_async_copy(parts_ref.at[slot, pl.ds(0, shard), :], small_ref.at[pl.ds(at, shard), :], sems.at[slot])
        )
        if mask < span:
            copies.append(
                pltpu.make_async_copy(
                    parts_ref.at[slot, pl.ds(shard, 16), :], marks_ref.at[place_ref[0] ^ mask], mark_sems.at[mask]
                )
            )
    for copy in copies:
        copy.start()
    for copy in copies:
        copy.wait()
    small = small_ref[...]
    across = small.astype(WIDE).T
    gains_ref[...] = across[0:8]
    gain = across[heads : heads + 1]
    stream = tokens_ref[...].astype(WIDE)
    scale = lax.rsqrt(jnp.mean(stream * stream, axis=-1, keepdims=True) + EPSILON)
    normed_wide = stream * scale * gain
    normed = normed_wide.astype(LOW)
    normed_ref[...] = normed
    beta_ref[...] = mm(normed, small)
    mask = place_ref[1]
    scatter_rows(tokens_x_ref, slice(None), tokens_ref[...], mask)
    scatter_rows(cot_x_ref, slice(None), cot_ref[...], mask)
    for at in range(normed.shape[0] // 128):
        start = pl.multiple_of((mask ^ at) * 128, 128)
        normed_t_ref[:, pl.ds(start, 128)] = normed_wide[at * 128 : (at + 1) * 128].T.astype(LOW)
    all_marks = marks_ref[...].astype(WIDE)
    line = iota(all_marks.shape, 1)
    length = tokens_ref.shape[0]
    marks = jnp.concatenate(
        [jnp.sum(jnp.where(line == at, all_marks, 0.0), axis=1) for at in range(length // 128)], axis=1
    )
    upper = jnp.where(iota((length, length), 0) <= iota((length, length), 1), 1.0, 0.0)
    docs = mm(marks, upper)
    row = iota(docs.shape, 0)
    before = jnp.zeros_like(docs)
    for at in range(span - 1):
        before = before + jnp.where(row > at, docs[at : at + 1, length - 1 : length], 0.0)
    docs = docs + before
    docs_ref[...] = docs
    own = jnp.sum(jnp.where(row == place_ref[0], docs, 0.0), axis=0, keepdims=True)
    eye = iota((length, length), 0) == iota((length, length), 1)
    column = jnp.sum(jnp.where(eye, own, 0.0), axis=1, keepdims=True)
    doc_col_ref[...] = jnp.broadcast_to(column, doc_col_ref.shape)


def branch_forward(heads, dim, tokens_x_ref, gains_ref, w_out_ref, *rest):
    *pieces, middle_ref, normed_ref, att_ref = rest
    for at, part in enumerate(pieces):
        att_ref[:, at * dim : (at + 1) * dim] = part[...]
    middle = tokens_x_ref[...].astype(WIDE) + mm(att_ref[...], w_out_ref[...], tb=True)
    middle_ref[...] = middle
    scale = lax.rsqrt(jnp.mean(middle * middle, axis=-1, keepdims=True) + EPSILON)
    normed_ref[...] = (middle * scale * gains_ref[heads + 1 : heads + 2]).astype(LOW)


def mlp_forward(cot_ref, gate_ref, up_ref, down_ref, *rest):
    ways = (len(rest) - 3) // 2
    pieces, outs = rest[:ways], rest[ways + 1 : -2]
    all_ref, normed_ref, acc_ref = rest[ways], rest[-2], rest[-1]
    step = pl.program_id(0)
    chunk = pieces[0].shape[0]

    @pl.when(step == 0)
    def start():
        for at, part in enumerate(pieces):
            normed_ref[at * chunk : (at + 1) * chunk, :] = part[...]
        acc_ref[...] = jnp.zeros_like(acc_ref)

    normed = normed_ref[...]
    gate, up, d_hidden = mm(normed, gate_ref[...]), mm(normed, up_ref[...]), mm(cot_ref[...], down_ref[...])
    sig = jax.nn.sigmoid(gate)
    silu = gate * sig
    d_gate = (d_hidden * up * sig * (1.0 + gate * (1.0 - sig))).astype(LOW)
    d_up = (d_hidden * silu).astype(LOW)
    all_ref[0] = d_gate
    all_ref[1] = d_up
    all_ref[2] = (silu * up).astype(LOW)
    acc_ref[...] += mm(d_gate, gate_ref[...], tb=True) + mm(d_up, up_ref[...], tb=True)

    @pl.when(step == pl.num_programs(0) - 1)
    def finish():
        for at, part in enumerate(outs):
            part[...] = acc_ref[at * chunk : (at + 1) * chunk, :].astype(LOW)


def mlp_grads(cot_ref, near_ref, far_ref, down_ref, middle_ref, *rest):
    ways = (len(rest) - 3) // 2
    pieces, grad_ref, outs, left_ref, acc_ref = rest[:ways], rest[ways], rest[ways + 1 : -2], rest[-2], rest[-1]
    step, third = pl.program_id(0), pl.num_programs(0) // 3
    chunk = pieces[0].shape[0]

    @pl.when(step == 0)
    def start():
        for at, part in enumerate(pieces):
            left_ref[:, at * chunk : (at + 1) * chunk] = part[...].astype(WIDE).T.astype(LOW)
        acc_ref[...] = jnp.zeros_like(acc_ref)
        acc_ref[0:chunk, :] = middle_ref[...]

    @pl.when(step == 2 * third)
    def turn():
        for at in range(ways):
            part = cot_ref[at * chunk : (at + 1) * chunk, :]
            left_ref[:, at * chunk : (at + 1) * chunk] = part.astype(WIDE).T.astype(LOW)

    right = jnp.concatenate([near_ref[0], far_ref[0]], axis=0)
    grad_ref[...] = mm(left_ref[...], right).astype(LOW)

    @pl.when(step >= 2 * third)
    def down():
        acc_ref[...] += mm(right, down_ref[...], tb=True)

    @pl.when(step == 3 * third - 1)
    def finish():
        for at, part in enumerate(outs):
            part[...] = acc_ref[at * chunk : (at + 1) * chunk, :].astype(LOW)


def branch_backward(heads, inner, middle_ref, gains_ref, cot_ref, w_out_ref, *rest):
    ways = (len(rest) - 4) // 2
    backs, d_middle_ref, gain_ref, upper_ref, lower_ref, d_atts = rest[:ways], *rest[ways : ways + 4], rest[ways + 4 :]
    grad = total([part[...] for part in backs])
    middle = middle_ref[...]
    scale = lax.rsqrt(jnp.mean(middle * middle, axis=-1, keepdims=True) + EPSILON)
    gain_ref[...] = jnp.broadcast_to(jnp.sum(grad * middle * scale, axis=0, keepdims=True), gain_ref.shape)
    d_middle = cot_ref[...].astype(WIDE) + norm_back(grad, middle, scale, gains_ref[heads + 1 : heads + 2])
    d_middle_ref[...] = d_middle
    d_branch = d_middle.astype(LOW)
    half = upper_ref.shape[0]
    upper_ref[...] = d_branch[:half]
    lower_ref[...] = d_branch[half:]
    for at, part in enumerate(d_atts):
        part[...] = mm(d_branch, w_out_ref[:, at * inner : (at + 1) * inner]).astype(LOW)


def project_back(heads, tokens_x_ref, small_ref, w_ref, gain_two_ref, part_ref, d_proj_ref, *rest):
    d_betas, (gain_ref, d_beta_ref, *outs) = rest[:heads], rest[heads:]
    d_beta = total([part[...] for part in d_betas]).astype(LOW)
    d_beta_ref[...] = d_beta
    back = part_ref[...] + mm(d_beta, small_ref[...], tb=True) + mm(d_proj_ref[...], w_ref[...], tb=True)
    stream = tokens_x_ref[...].astype(WIDE)
    scale = lax.rsqrt(jnp.mean(stream * stream, axis=-1, keepdims=True) + EPSILON)
    gain = jnp.sum(back * stream * scale, axis=0, keepdims=True)
    gain_ref[...] = jnp.where(iota(gain_ref.shape, 0) == 0, gain, gain_two_ref[...])
    chunk = outs[0].shape[0]
    for at, part in enumerate(outs):
        part[...] = back[at * chunk : (at + 1) * chunk].astype(LOW)


def token_grad(heads, tokens_x_ref, gains_ref, d_middle_ref, *rest):
    *backs, out_ref = rest
    grad = total([part[...] for part in backs])
    stream = tokens_x_ref[...].astype(WIDE)
    scale = lax.rsqrt(jnp.mean(stream * stream, axis=-1, keepdims=True) + EPSILON)
    out_ref[...] = (d_middle_ref[...] + norm_back(grad, stream, scale, gains_ref[heads : heads + 1])).astype(LOW)


def token_join(place_ref, *rest):
    *pieces, out_ref = rest
    chunk = pieces[0].shape[0]
    for at, part in enumerate(pieces):
        start = pl.multiple_of((place_ref[1] ^ at) * chunk, chunk)
        out_ref[pl.ds(start, chunk), :] = part[...].astype(out_ref.dtype)


def weight_grads(left_ref, d_proj_ref, *rest):
    rest[-1][...] = mm(left_ref[...], d_proj_ref[...]).astype(LOW)


def out_grads(heads, ways, *rest):
    branches, atts, out_ref, turned_ref = rest[:ways], rest[ways : ways + heads], rest[-2], rest[-1]
    step = pl.program_id(0)
    chunk = 2 * branches[0].shape[0]

    @pl.when(step == 0)
    def turn():
        for at in range(ways // 2):
            part = jnp.concatenate([branches[2 * at][...], branches[2 * at + 1][...]], axis=0)
            turned_ref[:, at * chunk : (at + 1) * chunk] = part.astype(WIDE).T.astype(LOW)

    for head in range(heads):

        @pl.when(step == head)
        def one(head=head):
            out_ref[...] = mm(turned_ref[...], atts[head][...]).astype(LOW)


def small_grads(heads, ways, left_ref, d_beta_ref, *rest):
    gains, out_ref, rows_ref = rest[:ways], rest[-2], rest[-1]
    gain = total([part[...] for part in gains])
    rows_ref[...] = jnp.zeros_like(rows_ref)
    rows_ref[heads : heads + 1, :] = gain[0:1]
    rows_ref[heads + 1 : heads + 2, :] = gain[1:2]
    out_ref[...] = (mm(left_ref[...], d_beta_ref[...]) + rows_ref[...].T).astype(LOW)


def project_more(d_proj_ref, w_ref, *rest):
    part = mm(d_proj_ref[...], w_ref[...], tb=True)
    if len(rest) > 1:
        part = rest[0][...] + part
    rest[-1][...] = part


def grad_join(heads, dim, in_ref, *outs):
    width = 4 * dim
    for head in range(heads):
        for kind, out in enumerate(outs[:4]):
            at = head * width + kind * dim
            out[:, head * dim : (head + 1) * dim] = in_ref[:, at : at + dim].astype(WIDE)
    outs[4][...] = in_ref[:, heads * width : heads * width + 128].astype(WIDE)
    outs[5][...] = in_ref[:, heads * width + 128 :].astype(WIDE)


def fixed(shape):
    return pl.BlockSpec(shape, lambda *unused: (0,) * len(shape))


def column_at(shape, at):
    return pl.BlockSpec(shape, lambda *unused: (0, at))


ANYWHERE = pl.BlockSpec(memory_space=pl.ANY)
SCALARS = pl.BlockSpec(memory_space=pltpu.SMEM)


def run(kernel, name, ins, specs, outs, scratch=(), flops=10**9):
    return pl.pallas_call(
        kernel,
        grid=(1,),
        in_specs=specs,
        out_specs=[fixed(shape) for shape, unused in outs],
        out_shape=[jax.ShapeDtypeStruct(shape, dtype) for shape, dtype in outs],
        scratch_shapes=list(scratch),
        compiler_params=pltpu.CompilerParams(vmem_limit_bytes=VMEM_BYTES),
        cost_estimate=pl.CostEstimate(flops=flops, bytes_accessed=4 * 2**20, transcendentals=2**18),
        name=name,
    )(*ins)


def whole(*arrays):
    return [fixed(array.shape) for array in arrays]


def run_block_forward(places, normed, w_in, at, beta_raw, doc_col, doc_row, dim, head):
    length, width = normed.shape
    square, tall = (length, length), (length, dim)
    return run(
        block_forward,
        "block_forward",
        (places, normed, w_in, beta_raw, doc_col, doc_row),
        [SCALARS, *whole(normed), column_at((width, 4 * dim), at), *whole(beta_raw, doc_col, doc_row)],
        [
            ((length, 4 * dim), WIDE),
            ((2 * length + dim, dim), LOW),
            (tall, WIDE),
            (square, WIDE),
            (square, LOW),
            (square, LOW),
            (square, LOW),
            (tall, LOW),
            ((length, 128), WIDE),
            (tall, WIDE),
        ],
        flops=10**10,
    )


def run_cross_forward(places, q_moved, stats, acc, doc_col, docs, packs, swapped):
    length, dim = q_moved.shape
    ins = (q_moved, stats, acc, doc_col, docs)
    return run(
        functools.partial(cross_forward, swapped),
        "cross_forward",
        (places, *ins, *packs),
        [SCALARS, *whole(*ins), ANYWHERE, ANYWHERE],
        [((length, dim), WIDE), ((length, dim), LOW), ((length, dim), WIDE)],
        [
            pltpu.VMEM((SPAN,) + packs[0].shape[1:], LOW),
            pltpu.VMEM((length, dim), WIDE),
            pltpu.VMEM((SPAN - 1, length, length), WIDE),
            pltpu.VMEM((length, 128), WIDE),
            pltpu.SemaphoreType.DMA((2,)),
        ],
        flops=10**10,
    )


def run_cross_backward(places, q_moved, scores, attention, log_total, doc_col, docs, packs, d_atts, head, swapped):
    length, dim = q_moved.shape
    ins = (q_moved, scores, attention, log_total, doc_col, docs)
    both = (SPAN,) + packs[0].shape[1:]
    return run(
        functools.partial(cross_backward, swapped),
        "cross_backward",
        (places, *ins, *packs, *d_atts),
        [SCALARS, *whole(*ins), ANYWHERE, ANYWHERE] + [column_at((part.shape[0], dim), head) for part in d_atts],
        [(packs[0].shape, LOW)] * 2 + [((length, dim), WIDE), ((length, length), LOW), ((length, dim), WIDE)],
        [
            pltpu.VMEM(both, LOW),
            pltpu.VMEM(both, LOW),
            pltpu.VMEM((SPAN + 1, length, dim), WIDE),
            pltpu.VMEM((SPAN, length, dim), WIDE),
            pltpu.VMEM((length, dim), LOW),
            pltpu.VMEM((length, length), WIDE),
            pltpu.SemaphoreType.DMA((2,)),
        ],
        flops=10**10,
    )


def run_block_backward(places, proj, beta_raw, kept, d_packs, head, dim):
    length = proj.shape[0]
    ins = (proj, beta_raw, *kept, *d_packs)
    return run(
        block_backward,
        "block_backward",
        (places, *ins),
        [SCALARS, *whole(*ins)],
        [(proj.shape, LOW), ((length, 128), LOW)],
        flops=5 * 10**9,
    )


def norm_back(grad, value, scale, gain):
    weighted = grad * gain
    return scale * weighted - value * scale * scale * scale * jnp.mean(weighted * value, axis=-1, keepdims=True)


def total(parts):
    out = parts[0].astype(WIDE)
    for part in parts[1:]:
        out = out + part.astype(WIDE)
    return out


def per_device(
    tokens, cotangent, starts, gain_attn, w_query, w_key, w_value, w_dir, w_beta, w_out, gain_mlp, w_gate, w_up, w_down
):
    row_count, width = tokens.shape
    shard, inner = w_query.shape
    hidden_units = w_gate.shape[1]
    heads = w_beta.shape[1]
    dim = inner // heads
    count = lax.axis_size("seq")
    ways = lax.axis_size("head")
    chunk = row_count // ways
    seq_place, head_place = lax.axis_index("seq"), lax.axis_index("head")
    places = jnp.stack([seq_place % SPAN, head_place, seq_place]).astype(jnp.int32)
    places_of = [jnp.concatenate([places, jnp.full((1,), head, jnp.int32)]) for head in range(heads)]

    def to_heads(parts):
        return [xor_move(part, "head", at) if at else part for at, part in enumerate(parts)]

    def over_heads(part):
        return to_heads([part] * ways)

    small = jnp.concatenate([w_beta, gain_attn[:, None], gain_mlp[:, None]], axis=1)
    small = jnp.pad(small, ((0, 0), (0, 128 - heads - 2)))
    marks = jnp.pad(starts.astype(LOW).reshape(row_count // 128, 128), ((0, 16 - row_count // 128), (0, 0)))
    masks = tuple(2 << at for at in range((count // 2).bit_length() - 1)) + (1,)
    small = doubled(jnp.concatenate([small, marks], axis=0), masks)
    four = (w_query, w_key, w_value, w_dir)
    (packed,) = run(functools.partial(pack_heads, heads), "pack_heads", four, whole(*four), [((shard, 4 * inner), LOW)])
    w_in = lax.all_gather(packed, "seq", axis=0, tiled=True)
    out_parts = jnp.concatenate(over_heads(w_out.T), axis=1)

    tall, wide_tall, part_low = (row_count, width), (width, row_count), ((chunk, width), LOW)
    normed, normed_x_t, tokens_x, cot_x, small_all, gains, beta_raw, docs, doc_col = run(
        functools.partial(prepare, heads, shard, masks),
        "prepare",
        (places, tokens, cotangent, small),
        [SCALARS, *whole(tokens, cotangent), ANYWHERE],
        [
            (tall, LOW),
            (wide_tall, LOW),
            (tall, LOW),
            (tall, LOW),
            ((width, 128), LOW),
            ((8, width), WIDE),
            ((row_count, 128), WIDE),
            ((SPAN, row_count), WIDE),
            ((row_count, 128), WIDE),
        ],
        [
            pltpu.VMEM((SPAN, 16, 128), LOW),
            pltpu.SemaphoreType.DMA((count,)),
            pltpu.SemaphoreType.DMA((SPAN,)),
        ],
    )
    normed, out_parts = lax.optimization_barrier((normed, out_parts))
    w_out_x = lax.all_gather(after(out_parts, w_in), "seq", axis=0, tiled=True)

    orders = [(2, 4)] * heads
    first, mixed, ready, full = [], [], {}, {}

    def step(kind, head):
        return (head, kind, xor_move(ready[head], "seq", orders[head][kind] if kind < 2 else 1))

    def meet(outs, moves):
        outs, arrived = lax.optimization_barrier((outs, [move[2] for move in moves]))
        for (head, kind, unused), part in zip(moves, arrived):
            ready[head] = (ready[head], part) if kind == 2 else jnp.concatenate([ready[head], part], axis=0)
        return outs

    flying = []
    for head in range(heads):
        held = normed if head == 0 else after(normed, first[-1][2])
        outs = run_block_forward(places_of[head], held, w_in, head, beta_raw, doc_col, docs, dim, head)
        first.append(meet(outs, flying))
        ready[head] = first[head][1][None]
        flying = [step(at, head - at) for at in range(max(0, head - 2), head + 1)]
    rest_in = jnp.concatenate([w_gate, w_up, w_down.T], axis=1)
    stage = {move[0]: move[1] for move in flying}
    for head in range(heads):
        kept = first[head]
        while stage.get(head, 2) < 2 or any(move[0] == head for move in flying):
            now = [move for move in flying if move[0] == head]
            flying = [move for move in flying if move[0] != head]
            meet((), now)
            if stage[head] < 2:
                stage[head] += 1
                flying.append(step(stage[head], head))
        if head == 0:
            held = kept[2]
        else:
            held = after(kept[2], mixed[-1][0])
        outs = run_cross_forward(places, held, kept[8], kept[9], doc_col, docs, ready[head], False)
        mixed.append(meet(outs, flying))
        flying = []
        for later in range(head + 1, heads):
            if stage[later] < 2:
                stage[later] += 1
                flying.append(step(stage[later], later))
        if head == 0:
            w_rest = lax.all_gather(after(rest_in, mixed[0][0], w_out_x), "seq", axis=0, tiled=True)
    packs = [ready[head] for head in range(heads)]

    att_x = jnp.concatenate([part[1] for part in mixed], axis=1)
    att_parts = to_heads([att_x[at * chunk : (at + 1) * chunk] for at in range(ways)])
    own_rows = fixed((chunk, width))
    middle, normed_two = run(
        functools.partial(branch_forward, heads, inner),
        "branch_forward",
        (tokens_x, gains, w_out_x, *att_parts),
        [own_rows, *whole(gains, w_out_x, *att_parts)],
        [((chunk, width), WIDE), part_low],
        [pltpu.VMEM((chunk, ways * inner), LOW)],
    )
    two_parts = over_heads(normed_two)

    blocks = 2
    cols = hidden_units // blocks

    def mlp_half(parts, at):
        rows = chunk * len(parts)
        return pl.pallas_call(
            mlp_forward,
            grid=(blocks,),
            in_specs=[
                pl.BlockSpec((rows, width), lambda step: (at, 0)),
                pl.BlockSpec((width, cols), lambda step: (0, step)),
                pl.BlockSpec((width, cols), lambda step: (0, blocks + step)),
                pl.BlockSpec((width, cols), lambda step: (0, 2 * blocks + step)),
                *whole(*parts),
            ],
            out_specs=[pl.BlockSpec((3, rows, cols), lambda step: (0, 0, step))] + [fixed((chunk, width))] * len(parts),
            out_shape=[jax.ShapeDtypeStruct((3, rows, hidden_units), LOW)]
            + [jax.ShapeDtypeStruct((chunk, width), LOW)] * len(parts),
            scratch_shapes=[pltpu.VMEM((rows, width), LOW), pltpu.VMEM((rows, width), WIDE)],
            compiler_params=pltpu.CompilerParams(vmem_limit_bytes=VMEM_BYTES),
            cost_estimate=pl.CostEstimate(flops=5 * 10**9, bytes_accessed=2**24, transcendentals=2**19),
            name="mlp_forward",
        )(cot_x, w_rest, w_rest, w_rest, *parts)

    near_all, *near_backs = mlp_half(two_parts[: ways // 2], 0)
    (near_all, near_backs), far_two = lax.optimization_barrier(((near_all, near_backs), two_parts[ways // 2 :]))
    near_moves = [xor_move(part, "head", at) if at else part for at, part in enumerate(near_backs)]
    far_all, *far_backs = mlp_half([after(part, near_all) for part in far_two], 1)
    (far_all, far_backs), near_moves = lax.optimization_barrier(((far_all, far_backs), near_moves))
    two_parts = two_parts[: ways // 2] + list(far_two)
    backs = near_moves + [xor_move(part, "head", ways // 2 + at) for at, part in enumerate(far_backs)]
    grad_mlp, *mlp_parts = pl.pallas_call(
        mlp_grads,
        grid=(3 * blocks,),
        in_specs=[
            fixed(tall),
            pl.BlockSpec((1, row_count // 2, cols), lambda step: (step // blocks, 0, step % blocks)),
            pl.BlockSpec((1, row_count // 2, cols), lambda step: (step // blocks, 0, step % blocks)),
            pl.BlockSpec((width, cols), lambda step: (0, jnp.maximum(step, 2 * blocks))),
            fixed((chunk, width)),
            *whole(*two_parts),
        ],
        out_specs=[pl.BlockSpec((width, cols), lambda step: (0, step))] + [fixed((chunk, width))] * ways,
        out_shape=[jax.ShapeDtypeStruct((width, 3 * hidden_units), LOW)]
        + [jax.ShapeDtypeStruct((chunk, width), LOW)] * ways,
        scratch_shapes=[pltpu.VMEM(wide_tall, LOW), pltpu.VMEM(tall, WIDE)],
        compiler_params=pltpu.CompilerParams(vmem_limit_bytes=VMEM_BYTES),
        cost_estimate=pl.CostEstimate(flops=10**10, bytes_accessed=2**24, transcendentals=0),
        name="mlp_grads",
    )(cot_x, near_all, far_all, w_rest, middle, *two_parts)
    grad_mlp, mlp_parts, backs = lax.optimization_barrier((grad_mlp, mlp_parts, backs))
    reduced_mlp = lax.psum_scatter(grad_mlp, "seq", scatter_dimension=0, tiled=True)

    d_middle, gain_two_sum, upper, lower, *d_atts = run(
        functools.partial(branch_backward, heads, inner),
        "branch_backward",
        (middle, gains, cot_x, w_out_x, *backs),
        [*whole(middle, gains), own_rows, *whole(w_out_x, *backs)],
        [((chunk, width), WIDE), ((8, width), WIDE)] + [((chunk // 2, width), LOW)] * 2 + [((chunk, inner), LOW)] * ways,
    )
    d_atts = to_heads(d_atts)

    def add(left, right):
        return (left.astype(WIDE) + right.astype(WIDE)).astype(LOW)

    second, low_sums, high_sums, last_sums, branch_parts = [], {}, {}, {}, [upper, lower]
    core, across = {}, {}
    halves_two = [after(part, *d_atts[1:]) for part in (upper, lower)]
    branch_moves = [(part, at) for at in range(1, ways) for part in halves_two]
    shares = [2] + [1] * (2 * heads - 3)

    def branch_next():
        some = shares.pop(0) if shares else len(branch_moves)
        out = [xor_move(part, "head", at) for part, at in branch_moves[:some]]
        del branch_moves[:some]
        return out

    for head in range(heads):
        kept = first[head]
        held = kept[2] if head == 0 else after(kept[2], second[-1][0])
        flying = (core.get(head - 1), across.get(head - 2), branch_next())
        outs = run_cross_backward(
            places, held, kept[3], mixed[head][0], mixed[head][2], doc_col, docs, packs[head], d_atts, head, False
        )
        outs, (core_in, across_in, branch_in) = lax.optimization_barrier((outs, flying))
        even, odd, *rest = outs
        second.append(rest)
        branch_parts += branch_in
        if head >= 2:
            last_sums[head - 2] = [add(low_sums[head - 2][at], across_in[at]) for at in range(2)]
        if head >= 1:
            high_sums[head - 1] = add(low_sums[head - 1][2:], core_in[2:])
            across[head - 1] = xor_move(high_sums[head - 1], "seq", orders[head - 1][1])
            low_sums[head - 1] = add(low_sums[head - 1][:2], core_in[:2])
        low_sums[head] = even
        core[head] = xor_move(odd, "seq", 1)
    mlp_rows = jnp.stack(mlp_parts)
    mlp_rows = jnp.concatenate([lax.dynamic_index_in_dim(mlp_rows, head_place ^ at, 0, False) for at in range(ways)])
    result = lax.psum(after(mlp_rows, reduced_mlp, second[-1][0]), "head")

    cols = 4 * dim
    grad_in = None

    def grads_into(kernel, ins, specs, at, grid, name, scratch=()):
        given = () if grad_in is None else (grad_in,)
        return pl.pallas_call(
            kernel,
            grid=(grid,),
            in_specs=specs + [ANYWHERE] * len(given),
            out_specs=at,
            out_shape=jax.ShapeDtypeStruct((width, (heads + 1) * cols), LOW),
            input_output_aliases={len(ins): 0} if given else {},
            scratch_shapes=list(scratch),
            compiler_params=pltpu.CompilerParams(vmem_limit_bytes=VMEM_BYTES),
            cost_estimate=pl.CostEstimate(flops=10**9, bytes_accessed=2**22, transcendentals=0),
            name=name,
        )(*ins, *given)

    d_projs, d_betas = [], []
    back_part = None
    for head in range(heads):
        if head not in last_sums:
            last_sums[head] = [add(low_sums[head][at], across[head][at]) for at in range(2)]
        near_sum, far_sum = last_sums[head]
        sent = [near_sum, xor_move(far_sum, "seq", orders[head][0])]
        if head >= 1:
            grad_in = grads_into(
                weight_grads,
                (normed_x_t, d_projs[-1]),
                whole(normed_x_t, d_projs[-1]),
                column_at((width, cols), head - 1),
                1,
                "weight_grads",
            )
            ins = (d_projs[-1], w_in) + (() if back_part is None else (back_part,))
            (back_part,) = run(
                project_more,
                "project_more",
                ins,
                [*whole(d_projs[-1]), column_at((width, cols), head - 1), *whole(*ins[2:])],
                [(tall, WIDE)],
            )
            if head == heads - 1:
                atts = [part[1] for part in mixed]
                grad_in = grads_into(
                    functools.partial(out_grads, heads, len(branch_parts)),
                    (*branch_parts, *atts),
                    whole(*branch_parts, *atts),
                    pl.BlockSpec((width, 128), lambda step: (0, heads * cols // 128 + 1 + step)),
                    heads,
                    "out_grads",
                    [pltpu.VMEM(wide_tall, LOW)],
                )
            grad_in, back_part, sent = lax.optimization_barrier((grad_in, back_part, sent))
        late = heads - 1 if head == 0 and heads - 1 not in across else None
        flying = (across.get(head + 1), core[late] if late else None, branch_next() if head + 1 < heads else [])
        proj, inverse, carried, qdir, solve = (first[head][at] for at in (0, 4, 5, 6, 7))
        if head == 0:
            proj, reduced_mlp = lax.optimization_barrier((proj, reduced_mlp))
        outs = run_block_backward(
            places_of[head], proj, beta_raw, (inverse, carried, qdir, solve, *second[head]), sent, head, dim
        )
        (d_proj, d_beta), (across_in, core_in, branch_in) = lax.optimization_barrier((outs, flying))
        branch_parts += branch_in
        if across_in is not None:
            across[head + 1] = across_in
        if late:
            across[late] = xor_move(add(low_sums[late][2:], core_in[2:]), "seq", orders[late][1])
            low_sums[late] = add(low_sums[late][:2], core_in[:2])
        d_projs.append(d_proj)
        d_betas.append(d_beta)
    back_ins = (tokens_x, small_all, w_in, gain_two_sum, back_part, d_projs[-1], *d_betas)
    gain_sums, d_beta, *backs = run(
        functools.partial(project_back, heads),
        "project_back",
        back_ins,
        [
            *whole(tokens_x, small_all),
            column_at((width, cols), heads - 1),
            *whole(*back_ins[3:]),
        ],
        [((8, width), WIDE), ((row_count, 128), LOW)] + [part_low] * ways,
    )
    backs = to_heads(backs)
    (d_tokens_own,) = run(
        functools.partial(token_grad, heads),
        "token_grad",
        (tokens_x, gains, d_middle, *backs),
        [own_rows, *whole(gains, d_middle, *backs)],
        [part_low],
    )
    token_parts = over_heads(d_tokens_own)
    grad_in = grads_into(
        weight_grads,
        (normed_x_t, d_projs[-1]),
        whole(normed_x_t, d_projs[-1]),
        column_at((width, cols), heads - 1),
        1,
        "weight_grads",
    )
    gain_parts = over_heads(gain_sums)
    ins = (normed_x_t, d_beta, *gain_parts)
    grad_in = grads_into(
        functools.partial(small_grads, heads, ways),
        ins,
        whole(*ins),
        column_at((width, 128), heads * cols // 128),
        1,
        "small_grads",
        [pltpu.VMEM((128, width), WIDE)],
    )
    grad_in, result = lax.optimization_barrier((grad_in, result))
    reduced_in = lax.psum_scatter(grad_in, "seq", scatter_dimension=0, tiled=True)
    *grads, small_sum, grad_out_t = run(
        functools.partial(grad_join, heads, dim),
        "grad_join",
        (reduced_in,),
        whole(reduced_in),
        [((shard, inner), WIDE)] * 4 + [((shard, 128), WIDE), ((shard, inner), WIDE)],
    )
    reduced_mlp = reduced_mlp.astype(WIDE)
    finished = (
        *grads,
        small_sum,
        grad_out_t.T,
        reduced_mlp[:, :hidden_units],
        reduced_mlp[:, hidden_units : 2 * hidden_units],
        reduced_mlp[:, 2 * hidden_units :].T,
    )
    finished, token_parts = lax.optimization_barrier((finished, token_parts))
    *grads, small_sum, grad_out, grad_gate, grad_up, grad_down = finished
    (d_tokens,) = run(
        token_join, "token_join", (places, *token_parts), [SCALARS, *whole(*token_parts)], [(tall, WIDE)]
    )
    return (
        result,
        d_tokens,
        small_sum[:, heads],
        *grads,
        small_sum[:, :heads],
        grad_out,
        small_sum[:, heads + 1],
        grad_gate,
        grad_up,
        grad_down,
    )


def solution(mesh):
    placed = (
        P("seq", None),
        P("seq", None),
        P("seq"),
        P("seq"),
        P("seq", "head"),
        P("seq", "head"),
        P("seq", "head"),
        P("seq", "head"),
        P("seq", "head"),
        P("head", "seq"),
        P("seq"),
        P("seq", "head"),
        P("seq", "head"),
        P("head", "seq"),
    )
    return jax.shard_map(
        per_device,
        mesh=mesh,
        in_specs=placed,
        out_specs=(
            P("seq", None),
            P("seq", None),
            P("seq"),
            P("seq", "head"),
            P("seq", "head"),
            P("seq", "head"),
            P("seq", "head"),
            P("seq", "head"),
            P("head", "seq"),
            P("seq"),
            P("seq", "head"),
            P("seq", "head"),
            P("head", "seq"),
        ),
        check_vma=False,
    )
```
